32 devices in a mesh: wide: 8 (over y, x, core), narrow: 4 (over z).
Axes of the slice: x: 2, y: 2, z: 4, core: 2. Of those that a mesh axis runs over, the one named last changes fastest.
Arguments:
- tokens: bfloat16 [8192, 768], P(('wide', 'narrow')), may hold values from -6 to 6
- memory: bfloat16 [8192, 768], P(('wide', 'narrow')), may hold values from -6 to 6
- doc_lengths: int32 [32, 8], P(('wide', 'narrow')), may hold values from 0 to 256, as said below
- mem_lengths: int32 [32, 8], P(('wide', 'narrow')), may hold values from 0 to 256, as said below
- pad_mask: int32 [8192], P(('wide', 'narrow')), may hold values 0 or 1
- self_query: bfloat16 [768, 768], P(('wide', 'narrow')), may hold values from -0.078125 to 0.078125
- self_key: bfloat16 [768, 768], P(('wide', 'narrow')), may hold values from -0.078125 to 0.078125
- self_value: bfloat16 [768, 768], P(('wide', 'narrow')), may hold values from -0.21875 to 0.21875
- self_output: bfloat16 [768, 768], P(('wide', 'narrow')), may hold values from -0.875 to 0.875
- self_gain: bfloat16 [768], P(('wide', 'narrow')), may hold values from 0.5 to 1.5
- bias_table: bfloat16 [32, 12], P('narrow'), may hold values from -4 to 4
- cross_query: bfloat16 [768, 768], P(('wide', 'narrow')), may hold values from -0.078125 to 0.078125
- cross_key: bfloat16 [768, 768], P(('wide', 'narrow')), may hold values from -0.078125 to 0.078125
- cross_value: bfloat16 [768, 768], P(('wide', 'narrow')), may hold values from -0.21875 to 0.21875
- cross_output: bfloat16 [768, 768], P(('wide', 'narrow')), may hold values from -0.875 to 0.875
- cross_gain: bfloat16 [768], P(('wide', 'narrow')), may hold values from 0.5 to 1.5
- hidden_in: bfloat16 [768, 3072], P(('wide', 'narrow')), may hold values from -0.21875 to 0.21875
- hidden_out: bfloat16 [3072, 768], P(('wide', 'narrow')), may hold values from -0.109375 to 0.109375
- hidden_gain: bfloat16 [768], P(('wide', 'narrow')), may hold values from 0.5 to 1.5
- out_grad: bfloat16 [8192, 768], P(('wide', 'narrow')), may hold values from -6 to 6
Outputs:
- layer_out: bfloat16 [8192, 768], P(('wide', 'narrow'))
- tokens_grad: float32 [8192, 768], P(('wide', 'narrow'))
- memory_grad: float32 [8192, 768], P(('wide', 'narrow'))
- self_query_grad: float32 [768, 768], P(('wide', 'narrow'))
- self_key_grad: float32 [768, 768], P(('wide', 'narrow'))
- self_value_grad: float32 [768, 768], P(('wide', 'narrow'))
- self_output_grad: float32 [768, 768], P(('wide', 'narrow'))
- self_gain_grad: float32 [768], P(('wide', 'narrow'))
- bias_table_grad: float32 [32, 12], P('narrow')
- cross_query_grad: float32 [768, 768], P(('wide', 'narrow'))
- cross_key_grad: float32 [768, 768], P(('wide', 'narrow'))
- cross_value_grad: float32 [768, 768], P(('wide', 'narrow'))
- cross_output_grad: float32 [768, 768], P(('wide', 'narrow'))
- cross_gain_grad: float32 [768], P(('wide', 'narrow'))
- hidden_in_grad: float32 [768, 3072], P(('wide', 'narrow'))
- hidden_out_grad: float32 [3072, 768], P(('wide', 'narrow'))
- hidden_gain_grad: float32 [768], P(('wide', 'narrow'))
The draws below stay inside these ranges and needn't reach their ends.
Inputs may be any that keep to these rules, and one draw needn't show every extreme that they name: `doc_lengths`: each row holds, in order, the lengths of the 8 sequences packed into one device's 256 token slots and sums to 256; lengths may be 0; in every draw one device holds a single sequence of 256 tokens. `mem_lengths`: each row holds, in order, the lengths of the encoder memories of the 8 sequences of that device, packed into its 256 memory slots, and sums to 256; every sequence with tokens has one memory token or more; the device that holds a single sequence gives it all 256 memory slots.
All inputs are finite; a program needn't handle non-finite values. No bound on the sum of `pad_mask` on one device may be relied on, other than what follows from the above.
Results may differ from the reference program's by a relative error of at most 0.023.
Values may be sent and summed in bfloat16 or wider, within the bound.
No kernel may reach another device: no remote copies, remote signals or barrier semaphores. Data moves between devices by JAX's collectives and lax.ppermute only.
A program may use at most 192 MiB of HBM per device.

```python
import math
import jax
import jax.numpy as jnp
import numpy as np
from jax import lax

D = 768
FF = 3072
HEADS = 12
DH = 64
BUCKETS = 32
REACH = 128
TOK_DEV = 256
DOCS = 8
MEM_DEV = 256
PACKS = 32
TOKENS = 8192
MEM_TOKENS = 8192


def forced_device(key):
    return jax.random.randint(jax.random.fold_in(key, 77), (), 0, PACKS)


def draw_doc_lengths(key, part):
    forced = forced_device(key)
    key = jax.random.fold_in(key, 1)
    power_key, extra_key = jax.random.split(key)
    length_unit = max(TOK_DEV // 26, 1)
    powers = jax.random.randint(power_key, (PACKS, DOCS), 0, 5)
    extra = jax.random.randint(extra_key, (PACKS, DOCS), 0, length_unit + 1)
    raw_lengths = length_unit * jnp.left_shift(jnp.ones_like(powers), powers) + extra
    running = jnp.cumsum(raw_lengths, axis=1)
    kept_lengths = jnp.where(running <= TOK_DEV, raw_lengths, 0)
    leading = kept_lengths[:, :DOCS - 1]
    remainder = TOK_DEV - jnp.sum(leading, axis=1, keepdims=True)
    lengths = jnp.concatenate([leading, remainder], axis=1)
    device_rows = jnp.arange(PACKS)[:, None]
    single = jnp.where(jnp.arange(DOCS)[None, :] == 0, TOK_DEV, 0)
    return jnp.where(device_rows == forced, single, lengths).astype(jnp.int32)


def draw_mem_lengths(key, part):
    forced = forced_device(key)
    key = jax.random.fold_in(key, 2)
    share = max(MEM_DEV // DOCS, 1)
    leading = jax.random.randint(key, (PACKS, DOCS - 1), 1, share + 1)
    remainder = MEM_DEV - jnp.sum(leading, axis=1, keepdims=True)
    lengths = jnp.concatenate([leading, remainder], axis=1)
    device_rows = jnp.arange(PACKS)[:, None]
    single = jnp.where(jnp.arange(DOCS)[None, :] == 0, MEM_DEV, 0)
    return jnp.where(device_rows == forced, single, lengths).astype(jnp.int32)


def set_ends(entries, own_key, low, high):
    longest = entries.shape.index(max(entries.shape))
    spots = []
    for shift in (0, 1):
        where = [jax.random.randint(jax.random.fold_in(own_key, axis), (), 0, length) for axis, length in enumerate(entries.shape)]
        where[longest] = (where[longest] + shift) % entries.shape[longest]
        spots.append(tuple(where))
    return entries.at[spots[0]].set(low).at[spots[1]].set(high)


def shard_levels(key, shape, shards, smallest, high):
    def one(position, shards_of):
        steps = jax.random.uniform(jax.random.fold_in(jax.random.fold_in(key, 6), position), (shards_of,), jnp.float32, smallest / len(shards), high / len(shards))
        return jnp.repeat(jnp.exp(steps), shape[position] // shards_of).reshape((-1,) + (1,) * (len(shape) - position - 1))

    factor_of = one(*shards[0])
    for cut in shards[1:]:
        factor_of = factor_of * one(*cut)
    return factor_of


def gaussian(key, shape, deviation, reach, cuts=(), kind=jnp.bfloat16):
    drawn = jax.random.normal(key, shape, jnp.float32) * deviation
    if len(cuts) > 0:
        drawn = shard_levels(key, shape, cuts, -0.22, 0.18) * drawn
    return jnp.clip(drawn, min=-reach, max=reach).astype(kind)


def setup_inputs(seed: int = 0) -> dict:
    keys = jax.random.split(jax.random.key(seed), 21)
    return {
        "tokens": gaussian(keys[0], (TOKENS, D), 1.0, 6.0, ((0, 32),)),
        "memory": gaussian(keys[1], (MEM_TOKENS, D), 1.0, 6.0, ((0, 32),)),
        "doc_lengths": draw_doc_lengths(jax.random.fold_in(keys[20], 71), 0),
        "mem_lengths": draw_mem_lengths(jax.random.fold_in(keys[20], 71), 0),
        "pad_mask": set_ends((jax.random.randint(keys[4], (TOKENS,), 0, 8) < 7).astype(jnp.int32), jax.random.fold_in(keys[4], 1), 0, 1),
        "self_query": gaussian(keys[5], (D, D), (8 * D) ** -0.5, 0.078125, ((0, 32),)),
        "self_key": gaussian(keys[6], (D, D), (8 * D) ** -0.5, 0.078125, ((0, 32),)),
        "self_value": gaussian(keys[7], (D, D), D ** -0.5, 0.21875, ((0, 32),)),
        "self_output": gaussian(keys[8], (D, D), (D // 16) ** -0.5, 0.875, ((0, 32),)),
        "self_gain": jnp.clip(1.0 + 0.1 * jax.random.normal(keys[9], (D,), jnp.float32), 0.5, 1.5).astype(jnp.bfloat16),
        "bias_table": gaussian(keys[10], (BUCKETS, HEADS), 1.0, 4.0, ((0, 4),)),
        "cross_query": gaussian(keys[11], (D, D), (8 * D) ** -0.5, 0.078125, ((0, 32),)),
        "cross_key": gaussian(keys[12], (D, D), (8 * D) ** -0.5, 0.078125, ((0, 32),)),
        "cross_value": gaussian(keys[13], (D, D), D ** -0.5, 0.21875, ((0, 32),)),
        "cross_output": gaussian(keys[14], (D, D), (D // 16) ** -0.5, 0.875, ((0, 32),)),
        "cross_gain": jnp.clip(1.0 + 0.1 * jax.random.normal(keys[15], (D,), jnp.float32), 0.5, 1.5).astype(jnp.bfloat16),
        "hidden_in": gaussian(keys[16], (D, FF), D ** -0.5, 0.21875, ((0, 32),)),
        "hidden_out": gaussian(keys[17], (FF, D), FF ** -0.5, 0.109375, ((0, 32),)),
        "hidden_gain": jnp.clip(1.0 + 0.1 * jax.random.normal(keys[18], (D,), jnp.float32), 0.5, 1.5).astype(jnp.bfloat16),
        "out_grad": gaussian(keys[19], (TOKENS, D), 1.0, 6.0, ((0, 32),)),
    }


@jax.custom_vjp
def low(v):
    return lax.optimization_barrier(v.astype(jnp.bfloat16)).astype(jnp.float32)

@jax.custom_vjp
def low_back(v):
    return v

def low_keep(v):
    return (low(v), None)

def low_pass(kept, grad):
    return (grad,)

def back_keep(v):
    return (v, None)

def back_low(kept, grad):
    return (low(grad),)
low.defvjp(low_keep, low_pass)
low_back.defvjp(back_keep, back_low)

def bucket_edges(bucket_count, far_reach):
    exact_span = bucket_count // 2
    edge_list = list(range(1, exact_span + 1))
    for target in range(exact_span + 1, bucket_count):
        distance = exact_span
        while exact_span + int(math.log(distance / exact_span) / math.log(far_reach / exact_span) * (bucket_count - exact_span)) < target:
            distance += 1
        edge_list.append(distance)
    return edge_list

def bucket_of(distances):
    edge_array = jnp.asarray(np.array(bucket_edges(BUCKETS, REACH), dtype=np.int32))
    return lax.optimization_barrier(jnp.sum((distances[..., None] >= edge_array).astype(jnp.int32), axis=-1)).astype(jnp.int32)

def segment_ids(length_row, slot_count):
    ends = jnp.cumsum(length_row).astype(jnp.int32)
    places = jnp.arange(slot_count, dtype=jnp.int32)
    return lax.optimization_barrier(jnp.sum((places[:, None] >= ends[None, :]).astype(jnp.int32), axis=1)).astype(jnp.int32)

def normalize(values, scale_gain):
    return values * lax.rsqrt(lax.optimization_barrier(jnp.mean(values * values, axis=-1, keepdims=True)) + 1e-06) * scale_gain

def matmul(left_side, right_side):
    return jnp.dot(left_side, right_side, preferred_element_type=jnp.float32, precision=lax.Precision.HIGHEST)

def attend(queries, keys_all, values_all, score_bias, allowed):
    scores = jnp.einsum('qhd,khd->hqk', queries, keys_all, precision=lax.Precision.HIGHEST)
    if score_bias is not None:
        scores = scores + score_bias
    scores = low_back(jnp.where(allowed[None], scores, -1000000000.0))
    row_top = lax.optimization_barrier(jnp.max(scores, axis=-1, keepdims=True))
    weights = jnp.exp(scores - row_top)
    probabilities = low(weights / lax.optimization_barrier(jnp.sum(weights, axis=-1, keepdims=True)))
    return jnp.einsum('hqk,khd->qhd', probabilities, values_all, precision=lax.Precision.HIGHEST)

def pack_layer(params, token_pack, memory_pack, doc_row, mem_row, pad_row):
    self_query, self_key, self_value, self_output, self_gain, bias_table, cross_query, cross_key, cross_value, cross_output, cross_gain, hidden_in, hidden_out, hidden_gain = params
    tok_rows = token_pack.shape[0]
    mem_rows = memory_pack.shape[0]
    model_width = token_pack.shape[1]
    seg_ids = segment_ids(doc_row, tok_rows)
    mem_ids = segment_ids(mem_row, mem_rows)
    places = jnp.arange(tok_rows, dtype=jnp.int32)
    self_allowed = (seg_ids[:, None] == seg_ids[None, :]) & (places[None, :] <= places[:, None]) & ((pad_row[None, :] == 1) | (places[None, :] == places[:, None]))
    cross_allowed = seg_ids[:, None] == mem_ids[None, :]
    buckets = bucket_of(jnp.maximum(places[:, None] - places[None, :], 0))
    rel_bias = jnp.transpose(bias_table[buckets], (2, 0, 1))

    def heads_of(matrix):
        return matrix.reshape(matrix.shape[0], HEADS, DH)
    normed_self = low(normalize(token_pack, self_gain))
    queries = low(low_back(matmul(normed_self, self_query)))
    keys_self = low(low_back(matmul(normed_self, self_key)))
    values_self = low(low_back(matmul(normed_self, self_value)))
    attended = attend(heads_of(queries), heads_of(keys_self), heads_of(values_self), rel_bias, self_allowed)
    attended = low(low_back(attended.reshape(tok_rows, model_width)))
    after_self = token_pack + low_back(matmul(attended, self_output))
    normed_cross = low(normalize(after_self, cross_gain))
    cross_queries = low(low_back(matmul(normed_cross, cross_query)))
    cross_keys = low(low_back(matmul(memory_pack, cross_key)))
    cross_values = low(low_back(matmul(memory_pack, cross_value)))
    cross_attended = attend(heads_of(cross_queries), heads_of(cross_keys), heads_of(cross_values), None, cross_allowed)
    cross_attended = low(low_back(cross_attended.reshape(tok_rows, model_width)))
    after_cross = after_self + low_back(matmul(cross_attended, cross_output))
    normed_hidden = low(normalize(after_cross, hidden_gain))
    upper = low_back(matmul(normed_hidden, hidden_in))
    activated = low(low_back(jax.nn.gelu(upper, approximate=True)))
    return after_cross + low_back(matmul(activated, hidden_out))

def reference(tokens, memory, doc_lengths, mem_lengths, pad_mask, self_query, self_key, self_value, self_output, self_gain, bias_table, cross_query, cross_key, cross_value, cross_output, cross_gain, hidden_in, hidden_out, hidden_gain, out_grad):
    weight_list = (self_query, self_key, self_value, self_output, self_gain, bias_table, cross_query, cross_key, cross_value, cross_output, cross_gain, hidden_in, hidden_out, hidden_gain)
    params = tuple((weight.astype(jnp.float32) for weight in weight_list))
    pack_count = tokens.shape[0] // TOK_DEV
    model_width = tokens.shape[1]
    token_packs = tokens.astype(jnp.float32).reshape(pack_count, TOK_DEV, model_width)
    memory_packs = memory.astype(jnp.float32).reshape(pack_count, MEM_DEV, model_width)
    pad_packs = pad_mask.reshape(pack_count, TOK_DEV)
    layer_fn = jax.checkpoint(pack_layer)

    def forward(param_tuple, token_arrays, memory_arrays):

        def pack_step(pack_items):
            token_pack, memory_pack, doc_row, mem_row, pad_row = pack_items
            return layer_fn(param_tuple, token_pack, memory_pack, doc_row, mem_row, pad_row)
        return lax.map(pack_step, (token_arrays, memory_arrays, doc_lengths, mem_lengths, pad_packs))
    layer_packs, pullback = jax.vjp(forward, params, token_packs, memory_packs)
    param_grads, token_grads, memory_grads = pullback(out_grad.astype(jnp.float32).reshape(pack_count, TOK_DEV, model_width))
    return (layer_packs.reshape(pack_count * TOK_DEV, model_width).astype(jnp.bfloat16), token_grads.reshape(pack_count * TOK_DEV, model_width), memory_grads.reshape(pack_count * MEM_DEV, model_width), param_grads[0], param_grads[1], param_grads[2], param_grads[3], param_grads[4], param_grads[5], param_grads[6], param_grads[7], param_grads[8], param_grads[9], param_grads[10], param_grads[11], param_grads[12], param_grads[13])
```

```python
import functools
import math

import jax
import jax.numpy as jnp
import numpy as np
from jax import lax
from jax.experimental import pallas as pl
from jax.experimental.pallas import tpu as pltpu
from jax.sharding import PartitionSpec as P

BUCKETS = 32
REACH = 128
LOW = jnp.bfloat16
F32 = jnp.float32
EXTRA = 8
NN = (((1,), (0,)), ((), ()))
NT = (((1,), (1,)), ((), ()))
TN = (((0,), (0,)), ((), ()))


def bucket_edges(bucket_count, far_reach):
    exact_span = bucket_count // 2
    edge_list = list(range(1, exact_span + 1))
    for target in range(exact_span + 1, bucket_count):
        distance = exact_span
        while (
            exact_span
            + int(
                math.log(distance / exact_span)
                / math.log(far_reach / exact_span)
                * (bucket_count - exact_span)
            )
            < target
        ):
            distance += 1
        edge_list.append(distance)
    return edge_list


def rolled_one_hot(rows):
    edges = np.array(bucket_edges(BUCKETS, REACH))
    distances = (rows - np.arange(rows)) % rows
    buckets = (distances[:, None] >= edges[None, :]).sum(axis=1)
    return (np.arange(BUCKETS)[:, None] == buckets[None, :]).astype(np.float32)


def grid_sizes():
    wide = lax.axis_size("wide")
    inner = wide // 2
    across = 1
    while across * across < inner:
        across *= 2
    return {"y": inner // across, "x": across, "c": 2, "z": lax.axis_size("narrow")}


def grid_place():
    sizes = grid_sizes()
    wide = lax.axis_index("wide")
    return {
        "y": wide // (2 * sizes["x"]),
        "x": (wide // 2) % sizes["x"],
        "c": wide % 2,
        "z": lax.axis_index("narrow"),
    }


def shifted(array, dim, step):
    sizes = grid_sizes()
    count = sizes[dim]
    if dim == "z":
        return lax.ppermute(array, "narrow", [(i, (i + step) % count) for i in range(count)])
    stride = {"y": 2 * sizes["x"], "x": 2, "c": 1}[dim]
    pairs = []
    for source in range(lax.axis_size("wide")):
        place = (source // stride) % count
        pairs.append((source, source + ((place + step) % count - place) * stride))
    return lax.ppermute(array, "wide", pairs)


def gather_stage(block, dim, axis):
    count = grid_sizes()[dim]
    here = grid_place()[dim]
    cyclic = [block] + [shifted(block, dim, count - step) for step in range(1, count)]
    ordered = []
    for place in range(count):
        picked = cyclic[0]
        for step in range(1, count):
            picked = jnp.where((here + step) % count == place, cyclic[step], picked)
        ordered.append(picked)
    return jnp.stack(ordered, axis)


def gather_all(block, order):
    block = gather_stage(block, "z", 0)
    if order == "xy":
        block = gather_stage(gather_stage(block, "x", 0), "y", 0)
    else:
        block = gather_stage(gather_stage(block, "y", 0), "x", 1)
    return gather_stage(block, "c", 2)


def take(array, place, axis):
    return lax.dynamic_index_in_dim(array, place, axis, keepdims=False)


def total_of(parts):
    total = parts[0].astype(F32)
    for part in parts[1:]:
        total = total + part.astype(F32)
    return total


def scatter_stage(parts, dim, axis):
    count = grid_sizes()[dim]
    here = grid_place()[dim]
    kept = [take(part, here, axis) for part in parts]
    for step in range(1, count):
        other = (here + step) % count
        sent = total_of([take(part, other, axis) for part in parts]).astype(LOW)
        kept.append(shifted(sent, dim, step))
    return kept


def scatter_all(partial, order):
    parts = scatter_stage([partial], "c", 2)
    if order == "yx":
        parts = scatter_stage(scatter_stage(parts, "y", 0), "x", 0)
    else:
        parts = scatter_stage(scatter_stage(parts, "x", 1), "y", 0)
    return total_of(scatter_stage(parts, "z", 0))


def head_mask(rows, head):
    lanes = lax.broadcasted_iota(jnp.int32, (rows, 128), 1)
    return (lanes >= 64) if head else (lanes < 64)


def attend_kernel(causal, *refs):
    if causal:
        q_ref, k_ref, v_ref, row_ref, col_ref, pad_ref, bias_ref, out_ref, prob_ref = refs
    else:
        q_ref, k_ref, v_ref, row_ref, col_ref, out_ref, prob_ref = refs
    rows = q_ref.shape[0]
    cols = k_ref.shape[0]
    allowed = row_ref[...] == col_ref[...]
    if causal:
        i = lax.broadcasted_iota(jnp.int32, (rows, cols), 0)
        j = lax.broadcasted_iota(jnp.int32, (rows, cols), 1)
        allowed = allowed & (j <= i) & ((pad_ref[...] == 1) | (i == j))
    q = q_ref[...]
    k = k_ref[...]
    v = v_ref[...]
    result = None
    for head in range(2):
        mine = head_mask(rows, head)
        scores = lax.dot_general(
            jnp.where(mine, q, jnp.zeros_like(q)), k, NT, preferred_element_type=F32
        )
        if causal:
            row = jnp.broadcast_to(bias_ref[0, head : head + 1, :], (rows, cols))
            scores = scores + pltpu.roll(row, 0, 1, stride=1, stride_axis=0)
        scores = jnp.where(allowed, scores, -1e9)
        weights = jnp.exp(scores - jnp.max(scores, axis=1, keepdims=True))
        probs = (weights / jnp.sum(weights, axis=1, keepdims=True)).astype(LOW)
        prob_ref[head] = probs
        part = lax.dot_general(probs, v, NN, preferred_element_type=F32)
        result = part if head == 0 else jnp.where(mine, part, result)
    out_ref[...] = result.astype(LOW)


def attend(queries, keys, values, places, row_ids, col_ids, pad=None, bias=None):
    rows = queries.shape[0]
    cols = keys.shape[0]
    pairs = 6
    q_at, k_at, v_at = places

    def block(count, start):
        return pl.BlockSpec((count, 128), lambda h: (0, start + h))

    def whole(shape):
        return pl.BlockSpec(shape, lambda h: (0,) * len(shape))

    in_specs = [block(rows, q_at), block(cols, k_at), block(cols, v_at), whole((rows, 1)), whole((1, cols))]
    args = [queries, keys, values, row_ids, col_ids]
    if bias is not None:
        in_specs += [whole((1, cols)), pl.BlockSpec((1, 2, cols), lambda h: (h, 0, 0))]
        args += [pad, bias]
    return pl.pallas_call(
        functools.partial(attend_kernel, bias is not None),
        grid=(pairs,),
        in_specs=in_specs,
        out_specs=[block(rows, 0), pl.BlockSpec((2, rows, cols), lambda h: (h, 0, 0))],
        out_shape=[
            jax.ShapeDtypeStruct((rows, pairs * 128), LOW),
            jax.ShapeDtypeStruct((pairs * 2, rows, cols), LOW),
        ],
        compiler_params=pltpu.CompilerParams(vmem_limit_bytes=32 * 1024 * 1024),
        cost_estimate=pl.CostEstimate(flops=12 * rows * cols * 64 * 4, bytes_accessed=4 * 1024 * 1024, transcendentals=12 * rows * cols),
    )(*args)


def attend_back_kernel(causal, *refs):
    if causal:
        q_ref, k_ref, v_ref, g_ref, prob_ref, dq_ref, dk_ref, dv_ref, dist_ref = refs
    else:
        q_ref, k_ref, v_ref, g_ref, prob_ref, dq_ref, dk_ref, dv_ref = refs
    rows = q_ref.shape[0]
    cols = k_ref.shape[0]
    q = q_ref[...]
    k = k_ref[...]
    v = v_ref[...]
    g = g_ref[...]
    if causal:
        i = lax.broadcasted_iota(jnp.int32, (rows, rows), 0)
        j = lax.broadcasted_iota(jnp.int32, (rows, rows), 1)
        flip = (i + j == rows - 1).astype(LOW)
    grads = None
    for head in range(2):
        mine = head_mask(rows, head)
        probs = prob_ref[head]
        wide_probs = probs.astype(F32)
        grad_probs = lax.dot_general(
            jnp.where(mine, g, jnp.zeros_like(g)), v, NT, preferred_element_type=F32
        )
        moved = wide_probs * grad_probs
        centre = jnp.sum(moved, axis=1, keepdims=True)
        grad_scores = moved - wide_probs * centre
        low_scores = grad_scores.astype(LOW)
        if causal:
            turned = lax.dot_general(flip, low_scores, NN, preferred_element_type=F32)
            lined = pltpu.roll(turned, 1, 1, stride=1, stride_axis=0)
            dist_ref[0, head : head + 1, :] = jnp.sum(lined, axis=0, keepdims=True)
        new = (
            lax.dot_general(low_scores, k, NN, preferred_element_type=F32),
            lax.dot_general(low_scores, q, TN, preferred_element_type=F32),
            lax.dot_general(probs, g, TN, preferred_element_type=F32),
        )
        grads = new if head == 0 else tuple(jnp.where(mine, b, a) for a, b in zip(grads, new))
    dq_ref[...] = grads[0].astype(LOW)
    dk_ref[...] = grads[1].astype(LOW)
    dv_ref[...] = grads[2].astype(LOW)


def attend_back(queries, keys, values, places, grad, probs, causal):
    rows = queries.shape[0]
    cols = keys.shape[0]
    pairs = 6
    q_at, k_at, v_at = places

    def block(count, start):
        return pl.BlockSpec((count, 128), lambda h: (0, start + h))

    out_specs = [block(rows, 0), block(cols, 0), block(cols, 0)]
    out_shape = [jax.ShapeDtypeStruct((n, pairs * 128), LOW) for n in (rows, cols, cols)]
    if causal:
        out_specs.append(pl.BlockSpec((1, 2, cols), lambda h: (h, 0, 0)))
        out_shape.append(jax.ShapeDtypeStruct((pairs, 2, cols), F32))
    return pl.pallas_call(
        functools.partial(attend_back_kernel, causal),
        grid=(pairs,),
        in_specs=[
            block(rows, q_at),
            block(cols, k_at),
            block(cols, v_at),
            block(rows, 0),
            pl.BlockSpec((2, rows, cols), lambda h: (h, 0, 0)),
        ],
        out_specs=out_specs,
        out_shape=out_shape,
        compiler_params=pltpu.CompilerParams(vmem_limit_bytes=32 * 1024 * 1024),
        cost_estimate=pl.CostEstimate(flops=12 * rows * cols * 64 * 8, bytes_accessed=4 * 1024 * 1024, transcendentals=0),
    )(queries, keys, values, grad, probs)


def segment_ids(length_row, slot_count):
    ends = jnp.cumsum(length_row).astype(jnp.int32)
    places = jnp.arange(slot_count, dtype=jnp.int32)
    return jnp.sum((places[:, None] >= ends[None, :]).astype(jnp.int32), axis=1).astype(jnp.int32)


def scale_of(values):
    return lax.rsqrt(jnp.mean(values * values, axis=-1, keepdims=True) + 1e-06)


def norm_back(values, scale, gain, grad):
    weighted = grad * gain
    middle = jnp.mean(values * weighted, axis=-1, keepdims=True)
    return (
        scale * weighted - values * (scale * scale * scale * middle),
        jnp.sum(grad * values * scale, axis=0),
    )


def dot(left, right, dims=NN):
    return lax.dot_general(left, right, dims, preferred_element_type=F32)


def gelu_tanh(values):
    return jax.nn.gelu(values, approximate=True)


def local(
    tokens, memory, doc_lengths, mem_lengths, pad_mask,
    self_query, self_key, self_value, self_output, self_gain, bias_table,
    cross_query, cross_key, cross_value, cross_output, cross_gain,
    hidden_in, hidden_out, hidden_gain, out_grad,
):
    sizes = grid_sizes()
    grid = (sizes["y"], sizes["x"], sizes["c"], sizes["z"])
    device_count = math.prod(grid)
    rows, width = tokens.shape
    mem_rows = memory.shape[0]
    ff = hidden_in.shape[1]
    share = self_query.shape[0]
    ff_share = hidden_out.shape[0]
    table_rows, heads = bias_table.shape

    gains = jnp.pad(
        jnp.concatenate([self_gain, cross_gain, hidden_gain])[None], ((0, 0), (0, 2 * width - 3 * share))
    )
    table_own = jnp.pad(bias_table.reshape(1, -1), ((0, 0), (0, 2 * width - table_rows * heads)))
    self_a = jnp.concatenate(
        [
            jnp.concatenate([self_query, self_key], axis=1),
            gains,
            table_own,
            jnp.zeros((EXTRA - 2, 2 * width), LOW),
        ],
        axis=0,
    )
    self_a = gather_all(self_a, "xy")
    self_b = gather_all(jnp.concatenate([self_value, self_output], axis=1), "yx")
    cross_a = gather_all(jnp.concatenate([cross_query, cross_output], axis=1), "xy")
    cross_b = gather_all(jnp.concatenate([cross_key, cross_value], axis=1), "yx")
    ff_in = gather_all(hidden_in, "xy").reshape(width, ff)
    ff_out = gather_all(hidden_out, "yx").reshape(ff, width)

    gain_rows = self_a[..., share, : 3 * share].reshape(device_count, 3, share)
    self_gain, cross_gain, hidden_gain = (
        gain_rows[:, n].reshape(width).astype(F32) for n in range(3)
    )
    table = self_a[0, 0, 0, :, share + 1, : table_rows * heads].reshape(sizes["z"] * table_rows, heads)
    self_qk = self_a[..., :share, :].reshape(width, 2 * width)
    self_vo = self_b.reshape(width, 2 * width)
    cross_qo = cross_a.reshape(width, 2 * width)
    cross_kv = cross_b.reshape(width, 2 * width)

    seg_ids = segment_ids(doc_lengths[0], rows)
    mem_ids = segment_ids(mem_lengths[0], mem_rows)
    one_hot = jnp.asarray(rolled_one_hot(rows))
    bias = dot(table.T, one_hot.astype(LOW)).reshape(heads // 2, 2, rows)

    residual = tokens.astype(F32)
    scale_self = scale_of(residual)
    normed_self = (residual * scale_self * self_gain).astype(LOW)
    qk_self = dot(normed_self, self_qk).astype(LOW)
    v_self = dot(normed_self, self_vo[:, :width]).astype(LOW)
    self_places = (0, width // 128, 0)
    attended, self_probs = attend(
        qk_self, qk_self, v_self, self_places, seg_ids[:, None], seg_ids[None], pad_mask[None], bias
    )
    after_self = residual + dot(attended, self_vo[:, width:])
    scale_cross = scale_of(after_self)
    normed_cross = (after_self * scale_cross * cross_gain).astype(LOW)
    cross_q = dot(normed_cross, cross_qo[:, :width]).astype(LOW)
    kv_cross = dot(memory, cross_kv).astype(LOW)
    cross_places = (0, 0, width // 128)
    cross_attended, cross_probs = attend(
        cross_q, kv_cross, kv_cross, cross_places, seg_ids[:, None], mem_ids[None]
    )
    after_cross = after_self + dot(cross_attended, cross_qo[:, width:])
    scale_hidden = scale_of(after_cross)
    normed_hidden = (after_cross * scale_hidden * hidden_gain).astype(LOW)
    upper = dot(normed_hidden, ff_in)
    activated, gelu_pull = jax.vjp(gelu_tanh, upper)
    activated = activated.astype(LOW)
    layer_out = (after_cross + dot(activated, ff_out)).astype(LOW)

    ff_out_grad = scatter_all(
        dot(activated, out_grad, TN).astype(LOW).reshape(grid + (ff_share, width)), "yx"
    )
    grad_act = dot(out_grad, ff_out, NT).astype(LOW)
    grad_upper = gelu_pull(grad_act.astype(F32))[0].astype(LOW)
    ff_in_grad = scatter_all(
        dot(normed_hidden, grad_upper, TN).astype(LOW).reshape(grid + (share, ff)), "xy"
    )
    grad_normed = dot(grad_upper, ff_in, NT)
    back, hidden_gain_part = norm_back(after_cross, scale_hidden, hidden_gain, grad_normed)
    grad_after_cross = out_grad.astype(F32) + back

    grad_branch = grad_after_cross.astype(LOW)
    grad_att = dot(grad_branch, cross_qo[:, width:], NT).astype(LOW)
    cross_dq, cross_dk, cross_dv = attend_back(
        cross_q, kv_cross, kv_cross, cross_places, grad_att, cross_probs, False
    )
    cross_qo_grad = jnp.concatenate(
        [dot(normed_cross, cross_dq, TN), dot(cross_attended, grad_branch, TN)], axis=1
    ).astype(LOW)
    cross_kv_grad = jnp.concatenate(
        [dot(memory, cross_dk, TN), dot(memory, cross_dv, TN)], axis=1
    ).astype(LOW)
    cross_qo_grad = scatter_all(cross_qo_grad.reshape(grid + (share, 2 * width)), "yx")
    cross_kv_grad = scatter_all(cross_kv_grad.reshape(grid + (share, 2 * width)), "xy")
    memory_grad = dot(cross_dk, cross_kv[:, :width], NT) + dot(cross_dv, cross_kv[:, width:], NT)
    grad_normed = dot(cross_dq, cross_qo[:, :width], NT)
    back, cross_gain_part = norm_back(after_self, scale_cross, cross_gain, grad_normed)
    grad_after_self = grad_after_cross + back

    grad_branch = grad_after_self.astype(LOW)
    grad_att = dot(grad_branch, self_vo[:, width:], NT).astype(LOW)
    self_dq, self_dk, self_dv, dist_grad = attend_back(
        qk_self, qk_self, v_self, self_places, grad_att, self_probs, True
    )
    self_qk_grad = jnp.concatenate(
        [dot(normed_self, self_dq, TN), dot(normed_self, self_dk, TN)], axis=1
    ).astype(LOW)
    self_vo_grad = jnp.concatenate(
        [dot(normed_self, self_dv, TN), dot(attended, grad_branch, TN)], axis=1
    ).astype(LOW)
    grad_normed = (
        dot(self_dq, self_qk[:, :width], NT)
        + dot(self_dk, self_qk[:, width:], NT)
        + dot(self_dv, self_vo[:, :width], NT)
    )
    back, self_gain_part = norm_back(residual, scale_self, self_gain, grad_normed)
    tokens_grad = grad_after_self + back
    table_part = lax.dot_general(
        one_hot, dist_grad.reshape(heads, rows), NT, precision=lax.Precision.HIGHEST, preferred_element_type=F32
    )

    gain_part = jnp.stack([self_gain_part, cross_gain_part, hidden_gain_part])
    gain_part = jnp.transpose(gain_part.reshape(3, device_count, share), (1, 0, 2)).reshape(
        grid + (1, 3 * share)
    )
    table_part = jnp.broadcast_to(
        table_part.reshape(1, 1, 1, sizes["z"], 1, table_rows * heads),
        grid + (1, table_rows * heads),
    )
    extra = jnp.concatenate(
        [
            gain_part,
            table_part,
            jnp.zeros(grid + (1, 2 * width - 3 * share - table_rows * heads), F32),
        ],
        axis=-1,
    ).astype(LOW)
    extra = jnp.concatenate([extra, jnp.zeros(grid + (EXTRA - 1, 2 * width), LOW)], axis=-2)
    self_qk_grad = jnp.concatenate([self_qk_grad.reshape(grid + (share, 2 * width)), extra], axis=-2)
    self_qk_grad = scatter_all(self_qk_grad, "yx")
    self_vo_grad = scatter_all(self_vo_grad.reshape(grid + (share, 2 * width)), "xy")
    last = self_qk_grad[share]
    return (
        layer_out,
        tokens_grad,
        memory_grad,
        self_qk_grad[:share, :width],
        self_qk_grad[:share, width:],
        self_vo_grad[:, :width],
        self_vo_grad[:, width:],
        last[:share],
        last[3 * share : 3 * share + table_rows * heads].reshape(table_rows, heads),
        cross_qo_grad[:, :width],
        cross_kv_grad[:, :width],
        cross_kv_grad[:, width:],
        cross_qo_grad[:, width:],
        last[share : 2 * share],
        ff_in_grad,
        ff_out_grad,
        last[2 * share : 3 * share],
    )


def solution(mesh):
    rows = P(("wide", "narrow"), None)
    line = P(("wide", "narrow"))
    table = P("narrow", None)
    return jax.shard_map(
        local,
        mesh=mesh,
        in_specs=(
            (rows,) * 4 + (line,) + (rows,) * 4 + (line, table) + (rows,) * 4 + (line,) + (rows,) * 2 + (line, rows)
        ),
        out_specs=(rows,) * 7 + (line, table) + (rows,) * 4 + (line,) + (rows,) * 2 + (line,),
        check_vma=False,
    )
```

```python
import math

import jax
import jax.numpy as jnp
import numpy as np
from jax import lax
from jax.experimental import pallas as pl
from jax.experimental.pallas import tpu as pltpu
from jax.sharding import PartitionSpec as P

BUCKETS = 32
REACH = 128
LOW = jnp.bfloat16
F32 = jnp.float32
NN = (((1,), (0,)), ((), ()))
NT = (((1,), (1,)), ((), ()))
TN = (((0,), (0,)), ((), ()))
PAIRS = 6
LANES = 128
TABLE_LANE = 16
CHUNK = 384
MiB = 1024 * 1024
FIRST_AT = 4


def bucket_edges(bucket_count, far_reach):
    exact_span = bucket_count // 2
    edge_list = list(range(1, exact_span + 1))
    for target in range(exact_span + 1, bucket_count):
        distance = exact_span
        while (
            exact_span
            + int(
                math.log(distance / exact_span)
                / math.log(far_reach / exact_span)
                * (bucket_count - exact_span)
            )
            < target
        ):
            distance += 1
        edge_list.append(distance)
    return edge_list


def rolled_one_hot(rows):
    edges = np.array(bucket_edges(BUCKETS, REACH))
    distances = (rows - np.arange(rows)) % rows
    buckets = (distances[:, None] >= edges[None, :]).sum(axis=1)
    return (np.arange(BUCKETS)[:, None] == buckets[None, :]).astype(np.float32)


def table_hot(rows, blocks, share, table_rows):
    one_hot = rolled_one_hot(rows)
    groups = -(-table_rows // share)
    hot = np.zeros((groups, blocks * share, rows), np.float32)
    for block in range(blocks):
        for row in range(table_rows):
            hot[row // share, block * share + row % share] = one_hot[block * table_rows + row]
    return hot


def grid_sizes():
    wide = lax.axis_size("wide")
    inner = wide // 2
    across = 1
    while across * across < inner:
        across *= 2
    return {"y": inner // across, "x": across, "c": 2, "z": lax.axis_size("narrow")}


def grid_place():
    sizes = grid_sizes()
    wide = lax.axis_index("wide")
    return {
        "y": wide // (2 * sizes["x"]),
        "x": (wide // 2) % sizes["x"],
        "c": wide % 2,
        "z": lax.axis_index("narrow"),
    }


def shifted(array, dim, step):
    sizes = grid_sizes()
    count = sizes[dim]
    if dim == "z":
        return lax.ppermute(array, "narrow", [(i, (i + step) % count) for i in range(count)])
    stride = {"y": 2 * sizes["x"], "x": 2, "c": 1}[dim]
    pairs = []
    for source in range(lax.axis_size("wide")):
        place = (source // stride) % count
        pairs.append((source, source + ((place + step) % count - place) * stride))
    return lax.ppermute(array, "wide", pairs)


def after(value, *earlier):
    return lax.optimization_barrier((value, *earlier))[0]


def received(block, dim):
    count = grid_sizes()[dim]
    return [shifted(block, dim, count - step) for step in range(1, count)]


def swapped(array):
    return shifted(array, "c", 1)


def in_order(block, others, dim, axis):
    here = grid_place()[dim]
    cyclic = [block] + others
    count = len(cyclic)
    ordered = []
    for place in range(count):
        picked = cyclic[0]
        for step in range(1, count):
            picked = jnp.where((here + step) % count == place, cyclic[step], picked)
        ordered.append(picked)
    return jnp.stack(ordered, axis)


class Weights:
    def __init__(self, arrays, spots):
        self.arrays = arrays
        self.spots = spots

    def load(self, place, refs, matrices):
        for source, first, rows, at, block, row, matrix in self.spots:
            start = row if at is None else pl.multiple_of(place[at] * block, block) + row
            matrices[matrix][pl.ds(start, rows), :] = refs[source][first : first + rows, :]


def in_pieces(block):
    sizes = grid_sizes()
    return sizes["y"] == 2 and sizes["x"] == 2 and block % 32 == 0


def from_neighbours(block):
    return [block, shifted(block, "x", 1), shifted(block, "y", 1)]


def from_corner(upper, lower):
    return [shifted(upper, "y", 1), shifted(lower, "x", 1)]


def gather_whole(block):
    block = in_order(block, received(block, "x"), "x", 0)
    block = in_order(block, received(block, "y"), "y", 0)
    block = in_order(block, received(block, "c"), "c", 2)
    return block.reshape(-1, block.shape[-1])


def piece_spots(neighbours, corners, block, first, matrix):
    spots = [(source, first, block, FIRST_AT + n, block, 0, matrix) for n, source in enumerate(neighbours)]
    if len(corners) == 4:
        half = block // 2
        for n, source in enumerate(corners):
            spots.append((source, 0, half, FIRST_AT + 6 + n % 2, block, (n // 2) * half, matrix))
    else:
        for n, source in enumerate(corners):
            spots.append((source, 0, block, FIRST_AT + 6 + n, block, 0, matrix))
    return spots


def with_twins(arrays):
    return [array for own in arrays for array in (own, swapped(own))]


def run(name, kernel, inputs, outputs, scratch=(), flops=0, weights=(), aliases=()):
    inputs = list(inputs)
    for group in weights:
        inputs += vmem(*group.arrays)
    size = sum(math.prod(array.shape) * array.dtype.itemsize for array, _ in inputs)
    arrays = [
        pltpu.with_memory_space_constraint(array, space) if space == pltpu.VMEM else array
        for array, space in inputs
    ]
    shapes = [
        jax.ShapeDtypeStruct(*output[:2]) if len(output) > 2 else pltpu.VMEM(*output) for output in outputs
    ]
    return pl.pallas_call(
        kernel,
        name=name,
        in_specs=[pl.BlockSpec(memory_space=space) for _, space in inputs],
        out_specs=[pl.BlockSpec(memory_space=pltpu.VMEM) for _ in outputs],
        out_shape=shapes,
        scratch_shapes=list(scratch),
        input_output_aliases=dict(aliases),
        compiler_params=pltpu.CompilerParams(vmem_limit_bytes=24 * MiB),
        cost_estimate=pl.CostEstimate(flops=flops, bytes_accessed=size // 2, transcendentals=0),
    )(*arrays)


def vmem(*arrays):
    return [(array, pltpu.VMEM) for array in arrays]


def dot(left, right, dims=NN):
    return lax.dot_general(left, right, dims, preferred_element_type=F32)


def scale_of(values):
    return lax.rsqrt(jnp.mean(values * values, axis=-1, keepdims=True) + 1e-06)


def norm_back(values, gain, grad):
    scale = scale_of(values)
    weighted = grad * gain
    middle = jnp.mean(values * weighted, axis=-1, keepdims=True)
    return (
        scale * weighted - values * (scale * scale * scale * middle),
        jnp.sum(grad * values * scale, axis=0, keepdims=True),
    )


def split_rows(matrix, core, keep, send):
    count, rows, _ = keep.shape
    if rows % 16:
        matrix = matrix.astype(F32)
    pieces = [matrix[n * rows : (n + 1) * rows].astype(keep.dtype) for n in range(2 * count)]

    @pl.when(core == 0)
    def _():
        for n in range(count):
            keep[n] = pieces[2 * n]
            send[n] = pieces[2 * n + 1]

    @pl.when(core == 1)
    def _():
        for n in range(count):
            keep[n] = pieces[2 * n + 1]
            send[n] = pieces[2 * n]


def lanes_of(pair, column=0):
    return pl.ds(pl.multiple_of(column + pair * LANES, LANES), LANES)


def head_mask(rows, head):
    lanes = lax.broadcasted_iota(jnp.int32, (rows, LANES), 1)
    return (lanes >= 64) if head else (lanes < 64)


def attend(q_ref, k_ref, v_ref, columns, allowed, bias, prob_ref, out_ref):
    rows = q_ref.shape[0]
    cols = k_ref.shape[0]

    def step(pair, carry):
        q = q_ref[:, lanes_of(pair, columns[0])]
        k = k_ref[:, lanes_of(pair, columns[1])]
        v = v_ref[:, lanes_of(pair, columns[2])]
        result = None
        for head in range(2):
            mine = head_mask(rows, head)
            scores = dot(jnp.where(mine, q, jnp.zeros_like(q)), k, NT)
            if bias is not None:
                row = jnp.broadcast_to(bias[pl.ds(2 * pair + head, 1), :], (rows, cols))
                scores = scores + pltpu.roll(row, 0, 1, stride=1, stride_axis=0)
            scores = jnp.where(allowed[...] > 0, scores, -1e9)
            weights = jnp.exp(scores - jnp.max(scores, axis=1, keepdims=True))
            probs = (weights * (1.0 / jnp.sum(weights, axis=1, keepdims=True))).astype(LOW)
            prob_ref[2 * pair + head] = probs
            part = dot(probs, v)
            result = part if head == 0 else jnp.where(mine, part, result)
        out_ref[:, lanes_of(pair)] = result.astype(LOW)
        return carry

    lax.fori_loop(0, PAIRS, step, 0)


def attend_back(q_ref, k_ref, v_ref, columns, g_ref, prob_ref, outs, dist_ref):
    rows = q_ref.shape[0]
    cols = k_ref.shape[0]

    def step(pair, carry):
        q = q_ref[:, lanes_of(pair, columns[0])]
        k = k_ref[:, lanes_of(pair, columns[1])]
        v = v_ref[:, lanes_of(pair, columns[2])]
        g = g_ref[:, lanes_of(pair)]
        if dist_ref is not None:
            i = lax.broadcasted_iota(jnp.int32, (rows, rows), 0)
            j = lax.broadcasted_iota(jnp.int32, (rows, rows), 1)
            flip = (i + j == rows - 1).astype(LOW)
        grads = None
        for head in range(2):
            mine = head_mask(rows, head)
            low_probs = prob_ref[2 * pair + head]
            probs = low_probs.astype(F32)
            moved = probs * dot(jnp.where(mine, g, jnp.zeros_like(g)), v, NT)
            low_scores = (moved - probs * jnp.sum(moved, axis=1, keepdims=True)).astype(LOW)
            if dist_ref is not None:
                lined = pltpu.roll(dot(flip, low_scores), 1, 1, stride=1, stride_axis=0)
                dist_ref[pl.ds(2 * pair + head, 1), :] = jnp.sum(lined, axis=0, keepdims=True)
            new = (dot(low_scores, k), dot(low_scores, q, TN), dot(low_probs, g, TN))
            grads = new if head == 0 else tuple(jnp.where(mine, b, a) for a, b in zip(grads, new))
        for (ref, column), grad in zip(outs, grads):
            ref[:, lanes_of(pair, column)] = grad.astype(LOW)
        return carry

    lax.fori_loop(0, PAIRS, step, 0)


def head_lanes(group, heads):
    head = lax.broadcasted_iota(jnp.int32, (16, LANES), 0)
    lane = lax.broadcasted_iota(jnp.int32, (16, LANES), 1)
    return ((head < heads) & (lane == TABLE_LANE + group * heads + head)).astype(F32)


def self_forward(place, tokens, row_ids, col_ids, pad, hot, weights, cut, block):
    rows, width = tokens.shape
    count = len(weights.arrays)
    heads = 2 * PAIRS
    groups = hot.shape[0]
    blocks = (width // block) // 2

    def kernel(place, tok, row_ids, col_ids, pad, hot, *refs):
        pieces, refs = refs[:count], refs[count:]
        qk, v, probs, out, nt_keep, nt_send, at_keep, at_send, gains, matrix, allowed, bias, att = refs
        weights.load(place, pieces, [matrix])
        i = lax.broadcasted_iota(jnp.int32, (rows, rows), 0)
        j = lax.broadcasted_iota(jnp.int32, (rows, rows), 1)
        same = (row_ids[...] == col_ids[...]) & (j <= i) & ((pad[...] == 1) | (i == j))
        allowed[...] = same.astype(F32)
        residual = tok[...].astype(F32)
        scaled = residual * scale_of(residual)
        extra = matrix[:, 2 * width : cut].astype(F32)
        gains[...] = extra.T[:8]
        normed = (scaled * gains[0:1, :]).astype(LOW)
        total = None
        for group in range(groups):
            table = dot(extra[: hot.shape[1]], head_lanes(group, heads), NT)
            part = dot(table.astype(LOW), hot[group], TN)
            total = part if total is None else total + part
        bias[...] = total
        split_rows(normed.T, place[2], nt_keep, nt_send)
        qk[...] = dot(normed, matrix[:, : 2 * width]).astype(LOW)
        v[...] = dot(normed, matrix[:, cut : cut + width]).astype(LOW)
        attend(qk, qk, v, (0, width, 0), allowed, bias, probs, att)
        attended = att[...]
        split_rows(attended.T, place[2], at_keep, at_send)
        out[...] = residual + dot(attended, matrix[:, cut + width :])

    halves = ((blocks, block, rows), LOW)
    return run(
        "self_forward",
        kernel,
        [(place, pltpu.SMEM)] + vmem(tokens, row_ids, col_ids, pad, hot),
        [
            ((rows, 2 * width), LOW),
            ((rows, width), LOW),
            ((heads, rows, rows), LOW),
            ((rows, width), F32),
            halves,
            halves,
            halves,
            halves,
            ((8, width), F32),
            ((width, cut + 2 * width), LOW),
        ],
        [
            pltpu.VMEM((rows, rows), F32),
            pltpu.VMEM((16, rows), F32),
            pltpu.VMEM((rows, width), LOW),
        ],
        flops=8 * rows * width * width,
        weights=[weights],
    )


def cross_forward(place, after_self, memory, gains, row_ids, col_ids, weights, block):
    rows, width = after_self.shape
    mem_rows = memory.shape[0]
    count = len(weights.arrays)
    blocks = (width // block) // 2

    def kernel(place, x, mem, gains, row_ids, col_ids, *refs):
        pieces, refs = refs[:count], refs[count:]
        q, kv, probs, out, nt_keep, nt_send, at_keep, at_send, mt_keep, mt_send, matrix, allowed, att = refs
        weights.load(place, pieces, [matrix])
        allowed[...] = (row_ids[...] == col_ids[...]).astype(F32)
        residual = x[...]
        normed = (residual * scale_of(residual) * gains[1:2, :]).astype(LOW)
        split_rows(normed.T, place[2], nt_keep, nt_send)
        split_rows(mem[...].T, place[2], mt_keep, mt_send)
        kv[...] = dot(mem[...], matrix[:, 2 * width :]).astype(LOW)
        q[...] = dot(normed, matrix[:, :width]).astype(LOW)
        attend(q, kv, kv, (0, 0, width), allowed, None, probs, att)
        attended = att[...]
        split_rows(attended.T, place[2], at_keep, at_send)
        out[...] = residual + dot(attended, matrix[:, width : 2 * width])

    halves = ((blocks, block, rows), LOW)
    mem_halves = ((blocks, block, mem_rows), LOW)
    return run(
        "cross_forward",
        kernel,
        [(place, pltpu.SMEM)] + vmem(after_self, memory, gains, row_ids, col_ids),
        [
            ((rows, width), LOW),
            ((mem_rows, 2 * width), LOW),
            ((2 * PAIRS, rows, mem_rows), LOW),
            ((rows, width), F32),
            halves,
            halves,
            halves,
            halves,
            mem_halves,
            mem_halves,
            ((width, 4 * width), LOW),
        ],
        [
            pltpu.VMEM((rows, mem_rows), F32),
            pltpu.VMEM((rows, width), LOW),
        ],
        flops=8 * rows * width * width,
        weights=[weights],
    )


def hidden_early(place, weights, width, ff):
    count = len(weights.arrays)

    def kernel(place, *refs):
        weights.load(place, refs[:count], refs[count:])

    return run(
        "hidden_early",
        kernel,
        [(place, pltpu.SMEM)],
        [((width, ff), LOW), ((ff, width), LOW)],
        weights=[weights],
    )


def hidden_first(place, after_cross, out_grad, gains, m_in, m_out, weights, block):
    rows, width = after_cross.shape
    ff = m_in.shape[1]
    count = len(weights.arrays)
    blocks = (width // block) // 2
    ff_block = ff // (2 * blocks)
    factor = math.sqrt(2.0 / math.pi)

    def kernel(place, x, og, gains, m_in_before, m_out_before, *refs):
        pieces, refs = refs[:count], refs[count:]
        act, gu, nt_keep, nt_send, at_keep, at_send, m_in, m_out = refs[:8]
        weights.load(place, pieces, [m_in, m_out])
        residual = x[...]
        normed = (residual * scale_of(residual) * gains[2:3, :]).astype(LOW)
        split_rows(normed.T, place[2], nt_keep, nt_send)
        grad = og[...]
        for start in range(0, ff, CHUNK):
            stop = start + CHUNK
            u = dot(normed, m_in[:, start:stop])
            ga = dot(grad, m_out[start:stop, :], NT).astype(LOW).astype(F32)
            square = u * u
            t = jnp.tanh(factor * u * (1.0 + 0.044715 * square))
            half = 0.5 * (1.0 + t)
            a = (u * half).astype(LOW)
            slope = half + (0.5 * factor) * u * (1.0 - t * t) * (1.0 + 3 * 0.044715 * square)
            gu[:, start:stop] = (slope * ga).astype(LOW)
            act[:, start:stop] = a
            turned = a.T
            for first in range(start, stop, ff_block):
                n = first // ff_block
                piece = turned[first - start : first - start + ff_block]

                @pl.when(place[2] == n % 2)
                def _(n=n, piece=piece):
                    at_keep[n // 2] = piece

                @pl.when(place[2] != n % 2)
                def _(n=n, piece=piece):
                    at_send[n // 2] = piece

    halves = ((blocks, block, rows), LOW)
    ff_halves = ((blocks, ff_block, rows), LOW)
    return run(
        "hidden_first",
        kernel,
        [(place, pltpu.SMEM)] + vmem(after_cross, out_grad, gains, m_in, m_out),
        [
            ((rows, ff), LOW),
            ((rows, ff), LOW),
            halves,
            halves,
            ff_halves,
            ff_halves,
            (m_in.shape, LOW),
            (m_out.shape, LOW),
        ],
        flops=4 * rows * width * ff,
        weights=[weights],
        aliases={4: 6, 5: 7},
    )


def hidden_second(after_cross, out_grad, gains, act, gu, m_in, m_out):
    rows, width = after_cross.shape
    ff = m_in.shape[1]

    def kernel(x, og, gains, act, gu, m_in, m_out, out, back_out, gain_out):
        residual = x[...]
        back, gain = norm_back(residual, gains[2:3, :], dot(gu[...], m_in[...], NT))
        back_out[...] = og[...].astype(F32) + back
        gain_out[...] = gain
        out[...] = (residual + dot(act[...], m_out[...])).astype(LOW)

    return run(
        "hidden_second",
        kernel,
        vmem(after_cross, out_grad, gains, act, gu, m_in, m_out),
        [((rows, width), LOW, None), ((rows, width), F32), ((1, width), F32)],
        flops=4 * rows * width * ff,
    )


def cross_backward(grad, after_self, gains, q, kv, probs, matrix):
    rows, width = after_self.shape
    mem_rows = kv.shape[0]

    def kernel(grad, x, gains, q, kv, probs, matrix, tok_out, mem_out, mem_grad, back_out, gain_out, att):
        branch = grad[...].astype(LOW)
        tok_out[:, width:] = branch
        att[...] = dot(branch, matrix[:, width : 2 * width], NT).astype(LOW)
        outs = ((tok_out, 0), (mem_out, 0), (mem_out, width))
        attend_back(q, kv, kv, (0, 0, width), att, probs, outs, None)
        back, gain = norm_back(x[...], gains[1:2, :], dot(tok_out[:, :width], matrix[:, :width], NT))
        back_out[...] = grad[...] + back
        gain_out[...] = gain
        mem_grad[...] = dot(mem_out[...], matrix[:, 2 * width :], NT)

    return run(
        "cross_backward",
        kernel,
        vmem(grad, after_self, gains, q, kv, probs, matrix),
        [
            ((rows, 2 * width), LOW),
            ((mem_rows, 2 * width), LOW),
            ((mem_rows, width), F32, None),
            ((rows, width), F32),
            ((1, width), F32),
        ],
        [pltpu.VMEM((rows, width), LOW)],
        flops=8 * rows * width * width,
    )


def self_backward(place, grad, tokens, gains, cross_gain, hidden_gain, qk, v, probs, hot, matrix, cut, block):
    rows, width = tokens.shape
    heads = 2 * PAIRS
    groups = hot.shape[0]
    blocks = (width // block) // 2

    def kernel(place, grad, tok, gains, cross_gain, hidden_gain, qk, v, probs, hot, matrix, *refs):
        out, tok_grad, extra_keep, extra_send, att, dist, parts = refs
        branch = grad[...].astype(LOW)
        out[:, 3 * width :] = branch
        att[...] = dot(branch, matrix[:, cut + width :], NT).astype(LOW)
        outs = ((out, 0), (out, width), (out, 2 * width))
        dist[...] = jnp.zeros_like(dist)
        attend_back(qk, qk, v, (0, width, 0), att, probs, outs, dist)
        normed_grad = dot(out[:, : 2 * width], matrix[:, : 2 * width], NT)
        normed_grad = normed_grad + dot(out[:, 2 * width : 3 * width], matrix[:, cut : cut + width], NT)
        back, gain = norm_back(tok[...].astype(F32), gains[0:1, :], normed_grad)
        tok_grad[...] = grad[...] + back
        parts[...] = jnp.zeros_like(parts)
        parts[0:1, :] = gain
        parts[1:2, :] = cross_gain[...]
        parts[2:3, :] = hidden_gain[...]
        columns = parts[...].T
        table = None
        for group in range(groups):
            sums = lax.dot_general(
                hot[group].astype(F32), dist[...], NT, precision=lax.Precision.HIGHEST, preferred_element_type=F32
            )
            part = lax.dot_general(
                sums, head_lanes(group, heads), NN, precision=lax.Precision.HIGHEST, preferred_element_type=F32
            )
            table = part if table is None else table + part
        columns = columns + jnp.concatenate([table] * (2 * blocks), axis=0)
        split_rows(columns, place[2], extra_keep, extra_send)

    halves = ((blocks, block, LANES), LOW)
    return run(
        "self_backward",
        kernel,
        [(place, pltpu.SMEM)]
        + vmem(grad, tokens, gains, cross_gain, hidden_gain, qk, v, probs, hot, matrix),
        [((rows, 4 * width), LOW), ((rows, width), F32, None), halves, halves],
        [
            pltpu.VMEM((rows, width), LOW),
            pltpu.VMEM((16, rows), F32),
            pltpu.VMEM((LANES, width), F32),
        ],
        flops=8 * rows * width * width,
    )


def weight_grads(place, lefts, rights, sections, cols, extras=()):
    sizes = grid_sizes()
    counts = (sizes["y"], sizes["x"])
    left_count, right_count = len(lefts), len(rights)
    block = [None, None]
    for section in sections:
        block[section[4]] = lefts[section[0]][0].shape[1]

    def kernel(place, *refs):
        refs = list(refs)
        left = [(refs.pop(0), refs.pop(0)) for _ in range(left_count)]
        right = [(refs.pop(0), refs.pop(0)) for _ in range(right_count)]
        extra = [refs.pop(0) for _ in extras]
        outs = (refs[: counts[0]], refs[counts[0] :])
        for half in range(2):
            mine, across = counts[half], counts[1 - half]
            here = place[half]
            for step in range(mine):
                for other in range(across):
                    index = ((here + step) % mine) * across + other
                    if half == 1:
                        index = other * mine + (here + step) % mine
                    target = outs[half][step]
                    for l, r, column, width, where, at in sections:
                        if where != half:
                            continue
                        for first in range(0, width, 768):
                            size = min(768, width - first)
                            own = dot(left[l][0][index], right[r][0][:, column + first : column + first + size])
                            far = dot(left[l][1][index], right[r][1][:, column + first : column + first + size])
                            target[other, :, at + first : at + first + size] = (own + far).astype(LOW)
                    if extras and half == 0:
                        target[other, :, cols[0] - LANES :] = (
                            extra[0][index].astype(F32) + extra[1][index].astype(F32)
                        ).astype(LOW)

    arrays = [array for pair in lefts for array in pair] + [array for pair in rights for array in pair]
    outputs = [((counts[1], block[0], cols[0]), LOW)] * counts[0]
    outputs += [((counts[0], block[1], cols[1]), LOW)] * counts[1]
    return run(
        "weight_grads",
        kernel,
        [(place, pltpu.SMEM)] + vmem(*arrays, *extras),
        outputs,
        flops=sum(2 * lefts[s[0]][0].size * s[3] for s in sections),
    )


def add_stage(place, firsts, seconds):
    sizes = grid_sizes()
    counts = (sizes["x"], sizes["y"])

    def kernel(place, *refs):
        halves = (refs[: len(firsts)], refs[len(firsts) : len(firsts) + len(seconds)])
        outs = refs[len(firsts) + len(seconds) :]
        outs = (outs[: counts[0]], outs[counts[0] :])
        for half in range(2):
            here = place[1 - half]
            for step in range(counts[half]):
                index = (here + step) % counts[half]
                total = halves[half][0][index].astype(F32)
                for part in halves[half][1:]:
                    total = total + part[index].astype(F32)
                outs[half][step][...] = total.astype(LOW)

    outputs = [(firsts[0].shape[1:], LOW)] * counts[0] + [(seconds[0].shape[1:], LOW)] * counts[1]
    return run("add_stage", kernel, [(place, pltpu.SMEM)] + vmem(*firsts, *seconds), outputs)


def add_last(place, firsts, seconds, by_z):
    sizes = grid_sizes()
    if by_z:
        count = sizes["z"]
        share = firsts[0].shape[0] // count
        firsts = [part.reshape(count, share, part.shape[-1]) for part in firsts]
        seconds = [part.reshape(count, share, part.shape[-1]) for part in seconds]
        cut = firsts[0].shape[-1]
        outputs = [((share, cut + seconds[0].shape[-1]), LOW)] * count
    else:
        outputs = [(firsts[0].shape, LOW), (seconds[0].shape, LOW)]

    def kernel(place, *refs):
        halves = (refs[: len(firsts)], refs[len(firsts) : len(firsts) + len(seconds)])
        outs = refs[len(firsts) + len(seconds) :]
        for half, parts in enumerate(halves):
            if not by_z:
                total = parts[0][...].astype(F32)
                for part in parts[1:]:
                    total = total + part[...].astype(F32)
                outs[half][...] = total.astype(LOW)
                continue
            for step in range(count):
                index = (place[3] + step) % count
                total = parts[0][index].astype(F32)
                for part in parts[1:]:
                    total = total + part[index].astype(F32)
                total = total.astype(LOW)
                if half == 0:
                    outs[step][:, :cut] = total
                else:
                    outs[step][:, cut:] = total

    return run("add_last", kernel, [(place, pltpu.SMEM)] + vmem(*firsts, *seconds), outputs)


def sent(parts, dim):
    return [parts[0]] + [shifted(part, dim, step) for step, part in enumerate(parts) if step]


def segment_ids(length_row, slot_count):
    ends = jnp.cumsum(length_row).astype(jnp.int32)
    places = jnp.arange(slot_count, dtype=jnp.int32)
    return jnp.sum((places[:, None] >= ends[None, :]).astype(jnp.int32), axis=1).astype(jnp.int32)


def local(
    tokens, memory, doc_lengths, mem_lengths, pad_mask,
    self_query, self_key, self_value, self_output, self_gain, bias_table,
    cross_query, cross_key, cross_value, cross_output, cross_gain,
    hidden_in, hidden_out, hidden_gain, out_grad,
):
    sizes = grid_sizes()
    here = grid_place()
    ny, nx, nz = sizes["y"], sizes["x"], sizes["z"]
    rows, width = tokens.shape
    mem_rows = memory.shape[0]
    ff = hidden_in.shape[1]
    share = self_query.shape[0]
    ff_share = hidden_out.shape[0]
    table_rows, heads = bias_table.shape
    block = nz * share
    ff_block = nz * ff_share
    cut = 2 * width + LANES

    spots = []
    for step in range(4):
        y = (here["y"] + step // 2) % ny
        x = (here["x"] + step % 2) % nx
        for core in range(2):
            spots.append((y * nx + x) * 2 + (here["c"] + core) % 2)
    place = jnp.stack([here["y"], here["x"], here["c"], here["z"]] + spots).astype(jnp.int32)

    hot = jnp.asarray(table_hot(rows, nz, share, table_rows)).astype(LOW)
    groups = hot.shape[0]
    table = jnp.pad(bias_table, ((0, groups * share - table_rows), (0, 0)))
    table = jnp.transpose(table.reshape(groups, share, heads), (1, 0, 2)).reshape(share, groups * heads)
    extra = jnp.concatenate(
        [
            self_gain[:, None],
            cross_gain[:, None],
            hidden_gain[:, None],
            jnp.zeros((share, TABLE_LANE - 3), LOW),
            table,
            jnp.zeros((share, LANES - TABLE_LANE - groups * heads), LOW),
        ],
        axis=1,
    )
    self_own = jnp.concatenate([self_query, self_key, extra, self_value, self_output], axis=1)
    self_others = received(self_own, "z")
    self_z = in_order(self_own, self_others, "z", 0).reshape(block, -1)
    wide_out = jnp.transpose(hidden_out.reshape(ff // width, share, width), (1, 0, 2)).reshape(share, ff)
    rest = jnp.concatenate(
        [
            jnp.concatenate([cross_query, cross_output, cross_key, cross_value], axis=1),
            hidden_in,
            wide_out,
        ],
        axis=0,
    )
    rest = lax.all_gather(rest, "narrow", axis=0, tiled=True)

    def ordered(rest):
        parts = rest.reshape(nz, 3, share, ff)
        both = jnp.transpose(parts[:, :2], (1, 0, 2, 3)).reshape(2 * block, ff)
        out = jnp.transpose(parts[:, 2].reshape(nz, share, ff // width, width), (0, 2, 1, 3))
        return both, out.reshape(ff_block, width)

    seg_ids = segment_ids(doc_lengths[0], rows)
    mem_ids = segment_ids(mem_lengths[0], mem_rows)
    pieces = in_pieces(block)
    half = block // 2
    if pieces:
        near = from_neighbours(self_z)
        corner = from_corner(near[1][:half], near[2][half:])
        both, out_z = ordered(after(rest, *corner))
        both_near = from_neighbours(both)
        out_near = from_neighbours(out_z)
        w_self = Weights(
            with_twins(near) + with_twins(corner), piece_spots(range(6), range(6, 10), block, 0, 0)
        )
    else:
        w_self = Weights([gather_whole(self_z)], [(0, 0, width, None, 0, 0, 0)])

    qk, v, self_probs, after_self, sn_keep, sn_send, sa_keep, sa_send, gains, m_self = self_forward(
        place, tokens, seg_ids[:, None], seg_ids[None], pad_mask[None], hot, w_self, cut, block
    )
    if pieces:
        corner = from_corner(after(both_near[1][:half], after_self), after(both_near[2][half:block], after_self))
        both_twins = with_twins(both_near)
        out_twins = with_twins(out_near)
        w_cross = Weights(both_twins + with_twins(corner), piece_spots(range(6), range(6, 10), block, 0, 0))
        last = from_corner(after(both_near[1][block:], *corner), after(out_near[2], *corner))
        spots = piece_spots(range(6), (), block, block, 0) + piece_spots(range(6, 12), (), ff_block, 0, 1)
        m_in, m_out = hidden_early(place, Weights(both_twins + out_twins, spots), width, ff)
        cross_in = after(after_self, m_in)
    else:
        both, out_z = ordered(rest)
        w_cross = Weights([gather_whole(both[:block])], [(0, 0, width, None, 0, 0, 0)])
        m_in, m_out = gather_whole(both[block:]), gather_whole(out_z)
        cross_in = after_self
    q, kv, cross_probs, after_cross, cn_keep, cn_send, ca_keep, ca_send, mt_keep, mt_send, m_cross = cross_forward(
        place, cross_in, memory, gains, seg_ids[:, None], mem_ids[None], w_cross, block
    )
    if pieces:
        last = with_twins([after(array, after_cross) for array in last])
        spots = piece_spots((), (0, 1), block, 0, 0) + piece_spots((), (2, 3), ff_block, 0, 1)
        w_last = Weights(last, spots)
    else:
        w_last = Weights([], [])
    sn_far, sa_far = swapped(sn_send), swapped(sa_send)
    cn_far, ca_far, mt_far = swapped(cn_send), swapped(ca_send), swapped(mt_send)
    og_far = swapped(out_grad)

    act, gu, hn_keep, hn_send, ha_keep, ha_send, m_in, m_out = hidden_first(
        place, after_cross, out_grad, gains, m_in, m_out, w_last, block
    )
    hn_far, ha_far, gu_far = swapped(hn_send), swapped(ha_send), swapped(gu)
    layer_out, grad, hidden_gain_part = hidden_second(after_cross, out_grad, gains, act, gu, m_in, m_out)
    hn_keep = after(hn_keep, grad)
    ff_parts = weight_grads(
        place,
        [(hn_keep, hn_far), (ha_keep, ha_far)],
        [(gu, gu_far), (out_grad, og_far)],
        [(0, 0, 0, ff, 0, 0), (1, 1, 0, width, 1, 0)],
        (ff, width),
    )
    ff_first, ff_second = ff_parts[:ny], ff_parts[ny:]
    ff_first, ff_second = sent(ff_first, "y"), sent(ff_second, "x")

    grad = after(grad, *ff_parts)
    cross_tok, cross_mem, memory_grad, grad, cross_gain_part = cross_backward(
        grad, after_self, gains, q, kv, cross_probs, m_cross
    )
    cross_tok_far, cross_mem_far = swapped(cross_tok), swapped(cross_mem)
    cross_parts = weight_grads(
        place,
        [(cn_keep, cn_far), (ca_keep, ca_far), (mt_keep, mt_far)],
        [(cross_tok, cross_tok_far), (cross_mem, cross_mem_far)],
        [
            (0, 0, 0, width, 0, 0),
            (1, 0, width, width, 0, width),
            (2, 1, 0, 2 * width, 1, 0),
        ],
        (2 * width, 2 * width),
    )
    cross_first, cross_second = cross_parts[:ny], cross_parts[ny:]
    ff_first = [after(ff_first[0], *cross_parts)] + ff_first[1:]
    ff_parts = add_stage(place, ff_first, ff_second)
    ff_first, ff_second = ff_parts[:nx], ff_parts[nx:]
    ff_first, ff_second = sent(ff_first, "x"), sent(ff_second, "y")
    cross_first, cross_second = sent(cross_first, "y"), sent(cross_second, "x")

    grad = after(grad, *ff_parts)
    self_grads, tokens_grad, extra_keep, extra_send = self_backward(
        place, grad, tokens, gains, cross_gain_part, hidden_gain_part, qk, v, self_probs, hot, m_self, cut, block
    )
    self_grads_far, extra_far = swapped(self_grads), swapped(extra_send)
    ff_first = [after(ff_first[0], self_grads)] + ff_first[1:]
    ff_first, ff_second = add_last(place, ff_first, ff_second, False)
    ff_total = jnp.concatenate(
        [
            jnp.transpose(ff_first.reshape(nz, share, ff // width, width), (0, 2, 1, 3)).reshape(nz, ff_share, width),
            ff_second.reshape(nz, ff_share, width),
        ],
        axis=1,
    ).reshape(-1, width)
    ff_total = lax.psum_scatter(ff_total, "narrow", scatter_dimension=0, tiled=True)
    cross_first = [after(cross_first[0], self_grads)] + cross_first[1:]
    cross_parts = add_stage(place, cross_first, cross_second)
    cross_first, cross_second = cross_parts[:nx], cross_parts[nx:]
    cross_first, cross_second = sent(cross_first, "x"), sent(cross_second, "y")
    sn_keep = after(sn_keep, ff_first, *cross_parts)
    self_parts = weight_grads(
        place,
        [(sn_keep, sn_far), (sa_keep, sa_far)],
        [(self_grads, self_grads_far)],
        [
            (0, 0, 0, 2 * width, 0, 0),
            (0, 0, 2 * width, width, 1, 0),
            (1, 0, 3 * width, width, 1, width),
        ],
        (cut, 2 * width),
        (extra_keep, extra_far),
    )
    self_first, self_second = self_parts[:ny], self_parts[ny:]
    self_first, self_second = sent(self_first, "y"), sent(self_second, "x")
    cross_first = [after(cross_first[0], *self_parts)] + cross_first[1:]
    cross_parts = add_last(place, cross_first, cross_second, True)
    cross_total = sum(part.astype(F32) for part in sent(cross_parts, "z"))
    self_first = [after(self_first[0], *cross_parts)] + self_first[1:]
    self_parts = add_stage(place, self_first, self_second)
    self_first, self_second = self_parts[:nx], self_parts[nx:]
    self_first, self_second = sent(self_first, "x"), sent(self_second, "y")
    self_parts = add_last(place, self_first, self_second, True)
    self_total = sum(part.astype(F32) for part in sent(self_parts, "z"))

    ff_total = ff_total.astype(F32)
    in_grad = jnp.transpose(ff_total[:ff_share].reshape(ff // width, share, width), (1, 0, 2)).reshape(share, ff)
    last = self_total[:, 2 * width : cut]
    table_grad = last[:, TABLE_LANE : TABLE_LANE + groups * heads].reshape(share, groups, heads)
    table_grad = jnp.transpose(table_grad, (1, 0, 2)).reshape(groups * share, heads)[:table_rows]
    return (
        layer_out,
        tokens_grad,
        memory_grad,
        self_total[:, :width],
        self_total[:, width : 2 * width],
        self_total[:, cut : cut + width],
        self_total[:, cut + width :],
        last[:, 0],
        table_grad,
        cross_total[:, :width],
        cross_total[:, 2 * width : 3 * width],
        cross_total[:, 3 * width :],
        cross_total[:, width : 2 * width],
        last[:, 1],
        in_grad,
        ff_total[ff_share:],
        last[:, 2],
    )


def solution(mesh):
    rows = P(("wide", "narrow"), None)
    line = P(("wide", "narrow"))
    table = P("narrow", None)
    return jax.shard_map(
        local,
        mesh=mesh,
        in_specs=(
            (rows,) * 4 + (line,) + (rows,) * 4 + (line, table) + (rows,) * 4 + (line,) + (rows,) * 2 + (line, rows)
        ),
        out_specs=(rows,) * 7 + (line, table) + (rows,) * 4 + (line,) + (rows,) * 2 + (line,),
        check_vma=False,
    )
```

```python
import math

import jax
import jax.numpy as jnp
import numpy as np
from jax import lax
from jax.experimental import pallas as pl
from jax.experimental.pallas import tpu as pltpu
from jax.sharding import PartitionSpec as P

BUCKETS = 32
REACH = 128
LOW = jnp.bfloat16
F32 = jnp.float32
NN = (((1,), (0,)), ((), ()))
NT = (((1,), (1,)), ((), ()))
TN = (((0,), (0,)), ((), ()))
PAIRS = 6
LANES = 128
TABLE_LANE = 16
CHUNK = 384
MiB = 1024 * 1024
FIRST_AT = 4
ORDER_AT = 12
EARLY = 0.75
EARLY_GRAD = 0.5


def bucket_edges(bucket_count, far_reach):
    exact_span = bucket_count // 2
    edge_list = list(range(1, exact_span + 1))
    for target in range(exact_span + 1, bucket_count):
        distance = exact_span
        while (
            exact_span
            + int(
                math.log(distance / exact_span)
                / math.log(far_reach / exact_span)
                * (bucket_count - exact_span)
            )
            < target
        ):
            distance += 1
        edge_list.append(distance)
    return edge_list


def rolled_one_hot(rows):
    edges = np.array(bucket_edges(BUCKETS, REACH))
    distances = (rows - np.arange(rows)) % rows
    buckets = (distances[:, None] >= edges[None, :]).sum(axis=1)
    return (np.arange(BUCKETS)[:, None] == buckets[None, :]).astype(np.float32)


def table_hot(rows, blocks, share, table_rows):
    one_hot = rolled_one_hot(rows)
    groups = -(-table_rows // share)
    hot = np.zeros((groups, blocks * share, rows), np.float32)
    for block in range(blocks):
        for row in range(table_rows):
            hot[row // share, block * share + row % share] = one_hot[block * table_rows + row]
    return hot


def grid_sizes():
    wide = lax.axis_size("wide")
    inner = wide // 2
    across = 1
    while across * across < inner:
        across *= 2
    return {"y": inner // across, "x": across, "c": 2, "z": lax.axis_size("narrow")}


def grid_place():
    sizes = grid_sizes()
    wide = lax.axis_index("wide")
    return {
        "y": wide // (2 * sizes["x"]),
        "x": (wide // 2) % sizes["x"],
        "c": wide % 2,
        "z": lax.axis_index("narrow"),
    }


def shifted(array, dim, step):
    sizes = grid_sizes()
    count = sizes[dim]
    if dim == "z":
        return lax.ppermute(array, "narrow", [(i, (i + step) % count) for i in range(count)])
    stride = {"y": 2 * sizes["x"], "x": 2, "c": 1}[dim]
    pairs = []
    for source in range(lax.axis_size("wide")):
        place = (source // stride) % count
        pairs.append((source, source + ((place + step) % count - place) * stride))
    return lax.ppermute(array, "wide", pairs)


def after(value, *earlier):
    return lax.optimization_barrier((value, *earlier))[0]


def received(block, dim):
    count = grid_sizes()[dim]
    return [shifted(block, dim, count - step) for step in range(1, count)]


def swapped(array):
    return shifted(array, "c", 1)


def in_order(block, others, dim, axis):
    here = grid_place()[dim]
    cyclic = [block] + others
    count = len(cyclic)
    ordered = []
    for place in range(count):
        picked = cyclic[0]
        for step in range(1, count):
            picked = jnp.where((here + step) % count == place, cyclic[step], picked)
        ordered.append(picked)
    return jnp.stack(ordered, axis)


class Weights:
    def __init__(self, arrays, spots):
        self.arrays = arrays
        self.spots = spots

    def load(self, place, refs, matrices, sems, ranges=None):
        waits = []
        count = 0
        for low, high in ranges or [(0, None)]:
            copies = []
            for source, first, column, at, block, row, rows, matrix, there, cols in self.spots:
                start = row if at is None else pl.multiple_of(place[at] * block, block) + row
                from_column, to_column, size = column + low, there + low, (high or cols) - low
                copies.append(
                    pltpu.make_async_copy(
                        refs[source].at[pl.ds(first, rows), pl.ds(from_column, size)],
                        matrices[matrix].at[pl.ds(start, rows), pl.ds(to_column, size)],
                        sems.at[count],
                    )
                )
                count += 1
            for copy in copies:
                copy.start()
            waits.append(lambda copies=copies: [copy.wait() for copy in copies])
        return waits

    def sems(self, ranges=1):
        return [pltpu.SemaphoreType.DMA((max(len(self.spots) * ranges, 1),))]


def fetch(sources, targets, sems):
    copies = [pltpu.make_async_copy(a, b, sems.at[n]) for n, (a, b) in enumerate(zip(sources, targets))]
    for copy in copies:
        copy.start()
    return [copy.wait for copy in copies]


def in_pieces(block):
    sizes = grid_sizes()
    return sizes["y"] == 2 and sizes["x"] == 2 and block % 32 == 0


def from_neighbours(block):
    return [block, shifted(block, "x", 1), shifted(block, "y", 1)]


def from_corner(upper, lower):
    return [shifted(upper, "y", 1), shifted(lower, "x", 1)]


def gather_pieces(block, *earlier, near=None):
    near = near or from_neighbours(block)
    half = block.shape[0] // 2
    twins = [swapped(near[0])]
    near_x, near_y = (after(array, twins[0], *earlier) for array in near[1:])
    corner = [shifted(near_x[:half], "y", 1), shifted(near_y[half:], "x", 1)]
    twins += [swapped(near_x), swapped(near_y)]
    return near, twins, corner


def pairs(near, twins):
    return [array for pair in zip(near, twins) for array in pair]


def gather_whole(block):
    block = in_order(block, received(block, "x"), "x", 0)
    block = in_order(block, received(block, "y"), "y", 0)
    block = in_order(block, received(block, "c"), "c", 2)
    return block.reshape(-1, block.shape[-1])


def near_spots(sources, block, column, matrix, there, cols):
    return [
        (source, 0, column, FIRST_AT + n, block, 0, block, matrix, there, cols) for n, source in enumerate(sources)
    ]


def half_spots(sources, block, column, matrix, there, cols):
    half = block // 2
    return [
        (source, 0, column, FIRST_AT + 6 + n % 2, block, (n // 2) * half, half, matrix, there, cols)
        for n, source in enumerate(sources)
    ]


def folded_spots(spots, block, column, groups, width, matrix):
    return [
        (source, first, column + g * width, at, groups * block, g * block + row, rows, matrix, 0, width)
        for source, first, _, at, _, row, rows, *_ in spots
        for g in range(groups)
    ]


def with_twins(arrays):
    return [array for own in arrays for array in (own, swapped(own))]


def run(name, kernel, inputs, outputs, scratch=(), flops=0, weights=(), aliases=()):
    inputs = list(inputs)
    for group in weights:
        inputs += [(array, pltpu.HBM) for array in group.arrays]
    size = sum(math.prod(array.shape) * array.dtype.itemsize for array, _ in inputs)
    arrays = [
        array if space == pltpu.SMEM else pltpu.with_memory_space_constraint(array, space)
        for array, space in inputs
    ]
    shapes = [
        jax.ShapeDtypeStruct(*output[:2]) if len(output) > 2 else pltpu.VMEM(*output) for output in outputs
    ]
    return pl.pallas_call(
        kernel,
        name=name,
        in_specs=[pl.BlockSpec(memory_space=space) for _, space in inputs],
        out_specs=[pl.BlockSpec(memory_space=pltpu.VMEM) for _ in outputs],
        out_shape=shapes,
        scratch_shapes=list(scratch),
        input_output_aliases=dict(aliases),
        compiler_params=pltpu.CompilerParams(vmem_limit_bytes=24 * MiB),
        cost_estimate=pl.CostEstimate(flops=flops, bytes_accessed=size // 2, transcendentals=0),
    )(*arrays)


def vmem(*arrays):
    return [(array, pltpu.VMEM) for array in arrays]


def dot(left, right, dims=NN):
    return lax.dot_general(left, right, dims, preferred_element_type=F32)


def scale_of(values):
    return lax.rsqrt(jnp.mean(values * values, axis=-1, keepdims=True) + 1e-06)


def norm_back(values, gain, grad):
    scale = scale_of(values)
    weighted = grad * gain
    middle = jnp.mean(values * weighted, axis=-1, keepdims=True)
    return (
        scale * weighted - values * (scale * scale * scale * middle),
        jnp.sum(grad * values * scale, axis=0, keepdims=True),
    )


def split_rows(matrix, core, keep, send):
    count, rows, _ = keep.shape
    if rows % 16:
        matrix = matrix.astype(F32)
    pieces = [matrix[n * rows : (n + 1) * rows].astype(keep.dtype) for n in range(2 * count)]

    @pl.when(core == 0)
    def _():
        for n in range(count):
            keep[n] = pieces[2 * n]
            send[n] = pieces[2 * n + 1]

    @pl.when(core == 1)
    def _():
        for n in range(count):
            keep[n] = pieces[2 * n + 1]
            send[n] = pieces[2 * n]


def lanes_of(pair, column=0):
    return pl.ds(pl.multiple_of(column + pair * LANES, LANES), LANES)


def head_mask(rows, head):
    lanes = lax.broadcasted_iota(jnp.int32, (rows, LANES), 1)
    return (lanes >= 64) if head else (lanes < 64)


def attend(q_ref, k_ref, v_ref, columns, allowed, bias, prob_ref, out_ref):
    rows = q_ref.shape[0]
    cols = k_ref.shape[0]

    def step(pair, carry):
        q = q_ref[:, lanes_of(pair, columns[0])]
        k = k_ref[:, lanes_of(pair, columns[1])]
        v = v_ref[:, lanes_of(pair, columns[2])]
        result = None
        for head in range(2):
            mine = head_mask(rows, head)
            scores = dot(jnp.where(mine, q, jnp.zeros_like(q)), k, NT)
            if bias is not None:
                row = jnp.broadcast_to(bias[pl.ds(2 * pair + head, 1), :], (rows, cols))
                scores = scores + pltpu.roll(row, 0, 1, stride=1, stride_axis=0)
            scores = jnp.where(allowed[...] > 0, scores, -1e9)
            weights = jnp.exp(scores - jnp.max(scores, axis=1, keepdims=True))
            probs = (weights * (1.0 / jnp.sum(weights, axis=1, keepdims=True))).astype(LOW)
            prob_ref[2 * pair + head] = probs
            part = dot(probs, v)
            result = part if head == 0 else jnp.where(mine, part, result)
        out_ref[:, lanes_of(pair)] = result.astype(LOW)
        return carry

    lax.fori_loop(0, PAIRS, step, 0)


def attend_back(q_ref, k_ref, v_ref, columns, g_ref, prob_ref, outs, dist_ref):
    rows = q_ref.shape[0]
    cols = k_ref.shape[0]

    def step(pair, carry):
        q = q_ref[:, lanes_of(pair, columns[0])]
        k = k_ref[:, lanes_of(pair, columns[1])]
        v = v_ref[:, lanes_of(pair, columns[2])]
        g = g_ref[:, lanes_of(pair)]
        if dist_ref is not None:
            i = lax.broadcasted_iota(jnp.int32, (rows, rows), 0)
            j = lax.broadcasted_iota(jnp.int32, (rows, rows), 1)
            flip = (i + j == rows - 1).astype(LOW)
        grads = None
        for head in range(2):
            mine = head_mask(rows, head)
            low_probs = prob_ref[2 * pair + head]
            probs = low_probs.astype(F32)
            moved = probs * dot(jnp.where(mine, g, jnp.zeros_like(g)), v, NT)
            low_scores = (moved - probs * jnp.sum(moved, axis=1, keepdims=True)).astype(LOW)
            if dist_ref is not None:
                lined = pltpu.roll(dot(flip, low_scores), 1, 1, stride=1, stride_axis=0)
                dist_ref[pl.ds(2 * pair + head, 1), :] = jnp.sum(lined, axis=0, keepdims=True)
            new = (dot(low_scores, k), dot(low_scores, q, TN), dot(low_probs, g, TN))
            grads = new if head == 0 else tuple(jnp.where(mine, b, a) for a, b in zip(grads, new))
        for (ref, column), grad in zip(outs, grads):
            ref[:, lanes_of(pair, column)] = grad.astype(LOW)
        return carry

    lax.fori_loop(0, PAIRS, step, 0)


def head_lanes(group, heads):
    head = lax.broadcasted_iota(jnp.int32, (16, LANES), 0)
    lane = lax.broadcasted_iota(jnp.int32, (16, LANES), 1)
    return ((head < heads) & (lane == TABLE_LANE + group * heads + head)).astype(F32)


def self_forward(place, tokens, row_ids, col_ids, pad, hot, weights, cut, block):
    rows, width = tokens.shape
    count = len(weights.arrays)
    heads = 2 * PAIRS
    groups = hot.shape[0]
    blocks = (width // block) // 2

    def kernel(place, tok, row_ids, col_ids, pad, hot, *refs):
        pieces, refs = refs[:count], refs[count:]
        qk, v, probs, out, keep, send, gains, matrix, allowed, bias, att, sems = refs
        wait, wait_late = weights.load(place, pieces, [matrix], sems, [(0, cut), (cut, cut + 2 * width)])
        i = lax.broadcasted_iota(jnp.int32, (rows, rows), 0)
        j = lax.broadcasted_iota(jnp.int32, (rows, rows), 1)
        same = (row_ids[...] == col_ids[...]) & (j <= i) & ((pad[...] == 1) | (i == j))
        allowed[...] = same.astype(F32)
        residual = tok[...].astype(F32)
        scaled = residual * scale_of(residual)
        wait()
        extra = matrix[:, 2 * width : cut].astype(F32)
        gains[...] = extra.T[:8]
        normed = (scaled * gains[0:1, :]).astype(LOW)
        total = None
        for group in range(groups):
            table = dot(extra[: hot.shape[1]], head_lanes(group, heads), NT)
            part = dot(table.astype(LOW), hot[group], TN)
            total = part if total is None else total + part
        bias[...] = total
        split_rows(normed.T, place[2], keep.at[0], send.at[0])
        qk[...] = dot(normed, matrix[:, : 2 * width]).astype(LOW)
        wait_late()
        v[...] = dot(normed, matrix[:, cut : cut + width]).astype(LOW)
        attend(qk, qk, v, (0, width, 0), allowed, bias, probs, att)
        attended = att[...]
        split_rows(attended.T, place[2], keep.at[1], send.at[1])
        out[...] = residual + dot(attended, matrix[:, cut + width :])

    halves = ((2, blocks, block, rows), LOW)
    return run(
        "self_forward",
        kernel,
        [(place, pltpu.SMEM)] + vmem(tokens, row_ids, col_ids, pad, hot),
        [
            ((rows, 2 * width), LOW, None),
            ((rows, width), LOW, None),
            ((heads, rows, rows), LOW, None),
            ((rows, width), F32, None),
            halves,
            halves,
            ((8, width), F32),
        ],
        [
            pltpu.VMEM((width, cut + 2 * width), LOW),
            pltpu.VMEM((rows, rows), F32),
            pltpu.VMEM((16, rows), F32),
            pltpu.VMEM((rows, width), LOW),
        ]
        + weights.sems(2),
        flops=8 * rows * width * width,
        weights=[weights],
    )


def cross_forward(place, after_self, memory, gains, row_ids, col_ids, weights, block):
    rows, width = after_self.shape
    mem_rows = memory.shape[0]
    count = len(weights.arrays)
    blocks = (width // block) // 2

    def kernel(place, x, mem, gains, row_ids, col_ids, *refs):
        pieces, refs = refs[:count], refs[count:]
        q, kv, probs, out, keep, send, matrix, allowed, att, sems = refs
        wait, wait_late = weights.load(place, pieces, [matrix], sems, [(2 * width, 4 * width), (0, 2 * width)])
        allowed[...] = (row_ids[...] == col_ids[...]).astype(F32)
        residual = x[...]
        normed = (residual * scale_of(residual) * gains[1:2, :]).astype(LOW)
        split_rows(normed.T, place[2], keep.at[0], send.at[0])
        split_rows(mem[...].T, place[2], keep.at[2], send.at[2])
        wait()
        kv[...] = dot(mem[...], matrix[:, 2 * width :]).astype(LOW)
        wait_late()
        q[...] = dot(normed, matrix[:, :width]).astype(LOW)
        attend(q, kv, kv, (0, 0, width), allowed, None, probs, att)
        attended = att[...]
        split_rows(attended.T, place[2], keep.at[1], send.at[1])
        out[...] = residual + dot(attended, matrix[:, width : 2 * width])

    halves = ((3, blocks, block, rows), LOW)
    return run(
        "cross_forward",
        kernel,
        [(place, pltpu.SMEM)] + vmem(after_self, memory, gains, row_ids, col_ids),
        [
            ((rows, width), LOW, None),
            ((mem_rows, 2 * width), LOW, None),
            ((2 * PAIRS, rows, mem_rows), LOW, None),
            ((rows, width), F32),
            halves,
            halves,
        ],
        [
            pltpu.VMEM((width, 4 * width), LOW),
            pltpu.VMEM((rows, mem_rows), F32),
            pltpu.VMEM((rows, width), LOW),
        ]
        + weights.sems(2),
        flops=8 * rows * width * width,
        weights=[weights],
    )


def hidden_order(nz, share, groups):
    units = np.arange(CHUNK).reshape(-1, nz, groups, share)
    order = np.transpose(units, (0, 2, 1, 3)).reshape(-1)
    matrix = np.zeros((CHUNK, CHUNK), np.float32)
    matrix[order, np.arange(CHUNK)] = 1.0
    return jnp.asarray(matrix).astype(LOW)


def reorder(array, order, dims, kind):
    def kernel(array, order, out):
        for start in range(0, array.shape[1], CHUNK):
            out[:, start : start + CHUNK] = dot(array[:, start : start + CHUNK], order[...], dims).astype(kind)

    return run("reorder", kernel, vmem(array, order), [(array.shape, kind, None)])[0]


def hidden_early(place, weights, width, ff):
    count = len(weights.arrays)

    def kernel(place, *refs):
        weights.load(place, refs[:count], refs[count : count + 2], refs[count + 2])[0]()

    return run(
        "hidden_early",
        kernel,
        [(place, pltpu.SMEM)],
        [((width, ff), LOW), ((ff, width), LOW)],
        weights.sems(),
        weights=[weights],
    )


def hidden_first(place, after_cross, out_grad, gains, m_in, m_out, weights, block):
    rows, width = after_cross.shape
    ff = m_in.shape[1]
    count = len(weights.arrays)
    blocks = (width // block) // 2
    ff_block = ff // (2 * blocks)
    factor = math.sqrt(2.0 / math.pi)

    def kernel(place, x, og, gains, m_in_before, m_out_before, *refs):
        pieces, refs = refs[:count], refs[count:]
        act, gu, keep, send, m_in, m_out, sems = refs
        (wait,) = weights.load(place, pieces, [m_in, m_out], sems)
        residual = x[...]
        normed = (residual * scale_of(residual) * gains[2:3, :]).astype(LOW)
        split_rows(normed.T, place[2], keep.at[:, :block], send.at[:, :block])
        grad = og[...]
        wait()
        for start in range(0, ff, CHUNK):
            stop = start + CHUNK
            u = dot(normed, m_in[:, start:stop])
            ga = dot(grad, m_out[start:stop, :], NT).astype(LOW).astype(F32)
            square = u * u
            t = jnp.tanh(factor * u * (1.0 + 0.044715 * square))
            half = 0.5 * (1.0 + t)
            a = (u * half).astype(LOW)
            slope = half + (0.5 * factor) * u * (1.0 - t * t) * (1.0 + 3 * 0.044715 * square)
            gu[:, start:stop] = (slope * ga).astype(LOW)
            act[:, start:stop] = a
            turned = a.T
            for first in range(start, stop, ff_block):
                n = first // ff_block
                piece = turned[first - start : first - start + ff_block]

                @pl.when(place[2] == n % 2)
                def _(n=n, piece=piece):
                    keep[n // 2, block:] = piece

                @pl.when(place[2] != n % 2)
                def _(n=n, piece=piece):
                    send[n // 2, block:] = piece

    halves = ((blocks, block + ff_block, rows), LOW)
    return run(
        "hidden_first",
        kernel,
        [(place, pltpu.SMEM)] + vmem(after_cross, out_grad, gains, m_in, m_out),
        [
            ((rows, ff), LOW),
            ((rows, ff), LOW),
            halves,
            halves,
            (m_in.shape, LOW),
            (m_out.shape, LOW),
        ],
        weights.sems(),
        flops=4 * rows * width * ff,
        weights=[weights],
        aliases={4: 4, 5: 5},
    )


def hidden_second(after_cross, out_grad, gains, act, gu, m_in, m_out):
    rows, width = after_cross.shape
    ff = m_in.shape[1]

    def kernel(x, og, gains, act, gu, m_in, m_out, out, back_out, branch, gain_out):
        residual = x[...]
        back, gain = norm_back(residual, gains[2:3, :], dot(gu[...], m_in[...], NT))
        grad = og[...].astype(F32) + back
        back_out[...] = grad
        branch[...] = grad.astype(LOW)
        gain_out[...] = gain
        out[...] = (residual + dot(act[...], m_out[...])).astype(LOW)

    return run(
        "hidden_second",
        kernel,
        vmem(after_cross, out_grad, gains, act, gu, m_in, m_out),
        [((rows, width), LOW, None), ((rows, width), F32, None), ((rows, width), LOW, None), ((1, width), F32)],
        flops=4 * rows * width * ff,
    )


def cross_backward(place, grad, branch, after_self, gains, q, kv, probs, weights):
    rows, width = after_self.shape
    mem_rows = kv.shape[0]

    count = len(weights.arrays)

    def kernel(place, gains, *refs):
        far, refs = refs[:6], refs[6:]
        pieces, refs = refs[:count], refs[count:]
        out, mem_grad, back_out, gain_out, branch, grad, x, q, kv, probs, matrix, att, own_sems, sems = refs
        ranges = [(width, 2 * width), (0, width), (2 * width, 4 * width)]
        branch_wait = fetch(far[:1], (branch,), own_sems)
        loaded = weights.load(place, pieces, [matrix], sems, ranges)
        waits = fetch(far[1:], (kv, probs, q, x, grad), own_sems.at[pl.ds(1, 5)])
        branch_wait[0]()
        loaded[0]()
        att[...] = dot(branch[...], matrix[:, width : 2 * width], NT).astype(LOW)
        outs = ((out, 0), (out, width), (out, 2 * width))
        for wait in waits:
            wait()
        attend_back(q, kv, kv, (0, 0, width), att, probs, outs, None)
        loaded[1]()
        loaded[2]()
        back, gain = norm_back(x[...], gains[1:2, :], dot(out[:, :width], matrix[:, :width], NT))
        total = grad[...] + back
        back_out[...] = total
        out[:, 3 * width :] = total.astype(LOW)
        gain_out[...] = gain
        mem_grad[...] = dot(out[:, width : 3 * width], matrix[:, 2 * width :], NT)

    return run(
        "cross_backward",
        kernel,
        [(place, pltpu.SMEM)]
        + vmem(gains)
        + [(array, pltpu.HBM) for array in (branch, kv, probs, q, after_self, grad)],
        [
            ((rows, 4 * width), LOW),
            ((mem_rows, width), F32, None),
            ((rows, width), F32),
            ((1, width), F32),
        ],
        [
            pltpu.VMEM((rows, width), LOW),
            pltpu.VMEM((rows, width), F32),
            pltpu.VMEM((rows, width), F32),
            pltpu.VMEM((rows, width), LOW),
            pltpu.VMEM((mem_rows, 2 * width), LOW),
            pltpu.VMEM((2 * PAIRS, rows, mem_rows), LOW),
            pltpu.VMEM((width, 4 * width), LOW),
            pltpu.VMEM((rows, width), LOW),
            pltpu.SemaphoreType.DMA((6,)),
        ]
        + weights.sems(3),
        flops=8 * rows * width * width,
        weights=[weights],
    )


def self_backward(place, grad, cross_grads, tokens, gains, cross_gain, hidden_gain, qk, v, probs, hot, weights, cut, block):
    rows, width = tokens.shape
    count = len(weights.arrays)
    heads = 2 * PAIRS
    groups = hot.shape[0]
    blocks = (width // block) // 2

    def kernel(place, grad, before, tok, gains, cross_gain, hidden_gain, hot, qk_far, v_far, probs_far, *refs):
        pieces, refs = refs[:count], refs[count:]
        out, out_v, tok_grad, extra_keep, extra_send, qk, v, probs, matrix, att, dist, parts, own_sems, sems = refs
        ranges = [(cut + width, cut + 2 * width), (0, cut + width)]
        loaded = weights.load(place, pieces, [matrix], sems, ranges)
        waits = fetch((v_far, probs_far, qk_far), (v, probs, qk), own_sems)
        loaded[0]()
        att[...] = dot(before[:, 3 * width :], matrix[:, cut + width :], NT).astype(LOW)
        outs = ((out, 0), (out, width), (out_v, 0))
        dist[...] = jnp.zeros_like(dist)
        for wait in waits:
            wait()
        attend_back(qk, qk, v, (0, width, 0), att, probs, outs, dist)
        loaded[1]()
        normed_grad = dot(out[...], matrix[:, : 2 * width], NT)
        normed_grad = normed_grad + dot(out_v[...], matrix[:, cut : cut + width], NT)
        back, gain = norm_back(tok[...].astype(F32), gains[0:1, :], normed_grad)
        tok_grad[...] = grad[...] + back
        parts[...] = jnp.zeros_like(parts)
        parts[0:1, :] = gain
        parts[1:2, :] = cross_gain[...]
        parts[2:3, :] = hidden_gain[...]
        columns = parts[...].T
        table = None
        for group in range(groups):
            sums = lax.dot_general(
                hot[group].astype(F32), dist[...], NT, precision=lax.Precision.HIGHEST, preferred_element_type=F32
            )
            part = lax.dot_general(
                sums, head_lanes(group, heads), NN, precision=lax.Precision.HIGHEST, preferred_element_type=F32
            )
            table = part if table is None else table + part
        columns = columns + jnp.concatenate([table] * (2 * blocks), axis=0)
        split_rows(columns, place[2], extra_keep, extra_send)

    halves = ((blocks, block, LANES), LOW)
    return run(
        "self_backward",
        kernel,
        [(place, pltpu.SMEM)]
        + vmem(grad, cross_grads, tokens, gains, cross_gain, hidden_gain, hot)
        + [(array, pltpu.HBM) for array in (qk, v, probs)],
        [((rows, 2 * width), LOW), ((rows, width), LOW), ((rows, width), F32, None), halves, halves],
        [
            pltpu.VMEM((rows, 2 * width), LOW),
            pltpu.VMEM((rows, width), LOW),
            pltpu.VMEM((heads, rows, rows), LOW),
            pltpu.VMEM((width, cut + 2 * width), LOW),
            pltpu.VMEM((rows, width), LOW),
            pltpu.VMEM((16, rows), F32),
            pltpu.VMEM((LANES, width), F32),
            pltpu.SemaphoreType.DMA((3,)),
        ]
        + weights.sems(2),
        flops=8 * rows * width * width,
        weights=[weights],
    )


def weight_grads(place, lefts, rights, sections, cols, extras=(), straight=()):
    sizes = grid_sizes()
    counts = (sizes["y"], sizes["x"])
    blocks = counts[0] * counts[1]
    nz = sizes["z"]
    left_count, right_count = len(lefts), len(rights)
    block = min(section[0][3] for section in (*sections, *straight))
    across_z = sum(section[3] * (section[0][3] // block) for section in straight)
    tokens = rights[0][0].shape[0]
    most = max(section[0][3] for section in (*sections, *straight))

    def kernel(place, *refs):
        refs = list(refs)
        left = [(refs.pop(0), refs.pop(0)) for _ in range(left_count)]
        right = [(refs.pop(0), refs.pop(0)) for _ in range(right_count)]
        extra = [refs.pop(0) for _ in extras]
        gathered = refs.pop()
        outs = (refs[: counts[0]], refs[counts[0] : counts[0] + counts[1]])
        out_z = refs[-1]

        def place_of(half, n):
            step, other = n // counts[1 - half], n % counts[1 - half]
            there = (place[half] + step) % counts[half]
            return there * counts[1] + other if half == 0 else other * counts[1] + there

        def products(section, order):
            (l, n, row, rows), r, column, width = section[:4]
            joined = rows % 16 == 0 and row % 16 == 0
            if joined:
                for k in range(blocks):
                    for side in range(2):
                        gathered[k * rows : (k + 1) * rows, side * tokens : (side + 1) * tokens] = left[l][side][
                            n, order(k), row : row + rows, :
                        ]
            for first in range(0, width, 768):
                size = min(768, width - first)
                own, far = (ref[:, column + first : column + first + size] for ref in right[r])
                if joined:
                    total = dot(gathered[: blocks * rows, :tokens], own)
                    total = total + dot(gathered[: blocks * rows, tokens:], far)
                for k in range(blocks):
                    if joined:
                        yield first, size, k, total[k * rows : (k + 1) * rows]
                        continue
                    own_rows, far_rows = (ref[n, order(k), row : row + rows, :] for ref in left[l])
                    yield first, size, k, dot(own_rows, own) + dot(far_rows, far)

        for section in straight:
            for first, size, index, total in products(section, lambda k: k):
                for g in range(section[0][3] // block):
                    at = section[5] + g * section[3] + first
                    for z in range(nz):
                        row = g * block + z * block // nz
                        part = total[row : row + block // nz]
                        out_z[z, index, :, at : at + size] = part.astype(LOW)
        for section in sections:
            groups = section[0][3] // block
            half = section[4]
            for first, size, k, total in products(section, lambda k: place_of(half, k)):
                for g in range(groups):
                    at = section[5] + g * section[3] + first
                    part = total[g * block : (g + 1) * block].astype(LOW)
                    outs[half][k // counts[1 - half]][k % counts[1 - half], :, at : at + size] = part
        for k in range(blocks if extras else 0):
            index = place_of(0, k)
            both = extra[0][index].astype(F32) + extra[1][index].astype(F32)
            outs[0][k // counts[1]][k % counts[1], :, cols[0] - LANES :] = both.astype(LOW)

    arrays = [array for pair in lefts for array in pair] + [array for pair in rights for array in pair]
    outputs = []
    if sections:
        outputs += [((counts[1], block, cols[0]), LOW)] * counts[0]
        outputs += [((counts[0], block, cols[1]), LOW)] * counts[1]
    if straight:
        outputs.append(((nz, blocks, block // nz, across_z), LOW, None))
    return run(
        "weight_grads",
        kernel,
        [(place, pltpu.SMEM)] + vmem(*arrays, *extras),
        outputs,
        [pltpu.VMEM((blocks * most, 2 * tokens), LOW)],
        flops=sum(4 * s[0][3] * blocks * rights[0][0].shape[0] * s[3] for s in (*sections, *straight)),
    )


def add_stage(place, firsts, seconds):
    sizes = grid_sizes()
    counts = (sizes["x"], sizes["y"])

    def kernel(place, *refs):
        halves = (refs[: len(firsts)], refs[len(firsts) : len(firsts) + len(seconds)])
        outs = refs[len(firsts) + len(seconds) :]
        outs = (outs[: counts[0]], outs[counts[0] :])
        for half in range(2):
            here = place[1 - half]
            for step in range(counts[half]):
                index = (here + step) % counts[half]
                total = halves[half][0][index].astype(F32)
                for part in halves[half][1:]:
                    total = total + part[index].astype(F32)
                outs[half][step][...] = total.astype(LOW)

    outputs = [(firsts[0].shape[1:], LOW)] * counts[0] + [(seconds[0].shape[1:], LOW)] * counts[1]
    return run("add_stage", kernel, [(place, pltpu.SMEM)] + vmem(*firsts, *seconds), outputs)


def add_last(place, halves):
    count = grid_sizes()["z"]
    share = halves[0][0].shape[0] // count
    halves = [[part.reshape(count, share, part.shape[-1]) for part in parts] for parts in halves]
    cols = [parts[0].shape[-1] for parts in halves]

    def kernel(place, *refs):
        refs = list(refs)
        first = 0
        inputs = [[refs.pop(0) for _ in parts] for parts in halves]
        for parts, size in zip(inputs, cols):
            for step in range(count):
                index = (place[3] + step) % count
                total = parts[0][index].astype(F32)
                for part in parts[1:]:
                    total = total + part[index].astype(F32)
                refs[step][:, first : first + size] = total.astype(LOW)
            first += size

    return run(
        "add_last",
        kernel,
        [(place, pltpu.SMEM)] + vmem(*[part for parts in halves for part in parts]),
        [((share, sum(cols)), LOW)] * count,
    )


def mirrored(place, count):
    return place - place % count + count - 1 - place % count


def halving_order(place, count):
    order = [place]
    while len(order) < count:
        size = count // len(order)
        order += [mirrored(block, size) for block in order]
    return order


def halve(place, sides, count, first):
    have = sides[0][0].shape[0]
    half = have // 2
    cols = [parts[0].shape[2] for parts in sides]
    shape = (half, sides[0][0].shape[1], sum(cols))

    def kernel(place, *refs):
        refs = list(refs)
        inputs = [[refs.pop(0) for _ in parts] for parts in sides]
        order = halving_order(place[3], have) if first else range(have)
        for n in range(have):
            at = 0
            for parts, size in zip(inputs, cols):
                total = parts[0][order[n]].astype(F32)
                for part in parts[1:]:
                    total = total + part[order[n]].astype(F32)
                refs[n // half][n % half, :, at : at + size] = total.astype(LOW)
                at += size

    arrays = [part for parts in sides for part in parts]
    keep, send = run("halve", kernel, [(place, pltpu.SMEM)] + vmem(*arrays), [(shape, LOW), (shape, LOW)])
    pairs = [(i, mirrored(i, count)) for i in range(grid_sizes()["z"])]
    return keep, lax.ppermute(send, "narrow", pairs)


def by_blocks(parts):
    count = grid_sizes()["z"]
    return [part.reshape(count, part.shape[0] // count, part.shape[1]) for part in parts]


def total_of(parts):
    return sum(part.astype(F32) for part in parts)


def scatter_along(parts, dim):
    count, here = grid_sizes()[dim], grid_place()[dim]
    kept = [lax.dynamic_index_in_dim(part, here, 0, keepdims=False) for part in parts]
    for step in range(1, count):
        there = (here + step) % count
        part = total_of([lax.dynamic_index_in_dim(part, there, 0, keepdims=False) for part in parts])
        kept.append(shifted(part.astype(LOW), dim, step))
    return kept


def sent(parts, dim):
    return [parts[0]] + [shifted(part, dim, step) for step, part in enumerate(parts) if step]


def segment_ids(length_row, slot_count):
    ends = jnp.cumsum(length_row).astype(jnp.int32)
    places = jnp.arange(slot_count, dtype=jnp.int32)
    return jnp.sum((places[:, None] >= ends[None, :]).astype(jnp.int32), axis=1).astype(jnp.int32)


def local(
    tokens, memory, doc_lengths, mem_lengths, pad_mask,
    self_query, self_key, self_value, self_output, self_gain, bias_table,
    cross_query, cross_key, cross_value, cross_output, cross_gain,
    hidden_in, hidden_out, hidden_gain, out_grad,
):
    sizes = grid_sizes()
    here = grid_place()
    ny, nx, nz = sizes["y"], sizes["x"], sizes["z"]
    rows, width = tokens.shape
    mem_rows = memory.shape[0]
    ff = hidden_in.shape[1]
    share = self_query.shape[0]
    ff_share = hidden_out.shape[0]
    table_rows, heads = bias_table.shape
    block = nz * share
    ff_block = nz * ff_share
    cut = 2 * width + LANES

    spots = []
    for step in range(4):
        y = (here["y"] + step // 2) % ny
        x = (here["x"] + step % 2) % nx
        for core in range(2):
            spots.append((y * nx + x) * 2 + (here["c"] + core) % 2)
    for n in range(4):
        spots += [2 * n + here["c"], 2 * n + 1 - here["c"]]
    place = jnp.stack([here["y"], here["x"], here["c"], here["z"]] + spots).astype(jnp.int32)
    pieces = in_pieces(block)
    half = block // 2

    hot = jnp.asarray(table_hot(rows, nz, share, table_rows)).astype(LOW)
    groups = hot.shape[0]
    table = jnp.pad(bias_table, ((0, groups * share - table_rows), (0, 0)))
    table = jnp.transpose(table.reshape(groups, share, heads), (1, 0, 2)).reshape(share, groups * heads)
    extra = jnp.concatenate(
        [
            self_gain[:, None],
            cross_gain[:, None],
            hidden_gain[:, None],
            jnp.zeros((share, TABLE_LANE - 3), LOW),
            table,
            jnp.zeros((share, LANES - TABLE_LANE - groups * heads), LOW),
        ],
        axis=1,
    )
    self_own = jnp.concatenate([self_query, self_key, extra, self_value, self_output], axis=1)
    self_others = received(self_own, "z")
    self_z = in_order(self_own, self_others, "z", 0).reshape(block, -1)
    folds = ff // width
    order = hidden_order(nz, share, folds)
    wide_out = jnp.transpose(hidden_out.reshape(folds, share, width), (1, 0, 2)).reshape(share, ff)
    hidden_own = reorder(hidden_in, order, NN, LOW)
    early_cols = int(ff * EARLY) // LANES * LANES if pieces else 0
    rest = jnp.concatenate(
        [cross_query, cross_output, cross_key, cross_value, hidden_own[:, early_cols:], wide_out], axis=1
    )
    rest = lax.all_gather(after(rest, self_others[0]), "narrow", axis=0, tiled=True)

    seg_ids = segment_ids(doc_lengths[0], rows)
    mem_ids = segment_ids(mem_lengths[0], mem_rows)
    if pieces:
        in_own = hidden_own[:, :early_cols]
        in_x, in_y = shifted(in_own, "x", 1), shifted(in_own, "y", 1)
        in_xy = shifted(in_x, "y", 1)
        in_all = in_order(
            in_order(in_own, [in_x], "x", 0), [in_order(in_y, [in_xy], "x", 0)], "y", 0
        ).reshape(4, share, early_cols)
        near, twins, corner = gather_pieces(self_z)
        in_all = lax.all_gather(after(in_all, rest, *corner), "narrow", axis=0, tiled=False)
        w_self = Weights(
            pairs(near, twins) + with_twins(corner),
            near_spots(range(6), block, 0, 0, 0, cut + 2 * width)
            + half_spots(range(6, 10), block, 0, 0, 0, cut + 2 * width),
        )
        rest_near = from_neighbours(after(rest, *twins, *corner))
    else:
        w_self = Weights([gather_whole(self_z)], [(0, 0, 0, None, 0, 0, width, 0, 0, cut + 2 * width)])

    og_far = swapped(out_grad)
    qk, v, self_probs, after_self, s_keep, s_send, gains = self_forward(
        place, after(tokens, og_far), seg_ids[:, None], seg_ids[None], pad_mask[None], hot, w_self, cut, block
    )
    s_far = swapped(s_send)
    if pieces:
        twin = swapped(rest_near[0])
        rest_x, rest_y = (after(array, after_self, s_far, twin) for array in rest_near[1:])
        corner = from_corner(rest_x[:half, :ff], rest_y[half:, :ff])
        upper, lower = rest_x[:half, ff:], rest_y[half:, ff:]
        rest_arrays = [rest_near[0], twin] + with_twins([rest_x, rest_y])
        w_cross = Weights(
            rest_arrays + with_twins(corner),
            near_spots(range(6), block, 0, 0, 0, ff) + half_spots(range(6, 10), block, 0, 0, 0, ff),
        )
        last = from_corner(upper, lower)
        cross_in = after(after_self, s_far, upper, lower)
    else:
        rest = gather_whole(rest)
        w_cross = Weights([rest], [(0, 0, 0, None, 0, 0, width, 0, 0, ff)])
        m_in = rest[:, ff : 2 * ff]
        m_out = jnp.transpose(rest[:, 2 * ff :].reshape(-1, block, folds, width), (0, 2, 1, 3)).reshape(ff, width)
        cross_in = after_self
    q, kv, cross_probs, after_cross, c_keep, c_send = cross_forward(
        place, cross_in, memory, gains, seg_ids[:, None], mem_ids[None], w_cross, block
    )
    c_far = swapped(c_send)
    if pieces:
        late_cols = ff - early_cols
        spots = folded_spots(near_spots(range(6), block, 0, 1, 0, 0), block, ff + late_cols, folds, width, 1)
        if late_cols:
            spots += near_spots(range(6), block, ff, 0, early_cols, late_cols)
        early = list(rest_arrays)
        in_all = jnp.transpose(after(in_all, *corner), (1, 0, 2, 3)).reshape(4 * block, early_cols)
        for twin, array in enumerate((in_all, swapped(in_all))):
            spots += [
                (6 + twin, n * block, 0, ORDER_AT + 2 * n + twin, block, 0, block, 0, 0, early_cols) for n in range(4)
            ]
            early.append(array)
        m_in, m_out = hidden_early(after(place, after_cross, c_far), Weights(early, spots), width, ff)
        last = with_twins([after(array, after_cross) for array in last])
        spots = folded_spots(half_spots(range(4), block, 0, 1, 0, 0), block, late_cols, folds, width, 1)
        if late_cols:
            spots += half_spots(range(4), block, 0, 0, early_cols, late_cols)
        w_last = Weights(last, spots)
    else:
        w_last = Weights([], [])

    act, gu, h_keep, h_send, m_in, m_out = hidden_first(
        place, after(after_cross, c_far), out_grad, gains, m_in, m_out, w_last, block
    )
    h_far, gu_far = swapped(h_send), swapped(gu)
    layer_out, grad, branch, hidden_gain_part = hidden_second(after_cross, out_grad, gains, act, gu, m_in, m_out)
    h_keep = after(h_keep, grad)
    side = width // 2
    early_grads = int(ff * EARLY_GRAD) // LANES * LANES if pieces else 0
    late = (ff - early_grads) // 2
    if pieces:
        in_early = weight_grads(
            place,
            [(h_keep[None], h_far[None])],
            [(gu, gu_far), (out_grad, og_far)],
            [],
            (0, 0),
            straight=[
                ((0, 0, 0, block), 0, 0, early_grads, 2, 0),
                ((0, 0, block, ff_block), 1, 0, width, 2, early_grads),
            ],
        )[0]
        grad = after(grad, in_early)
        in_early = lax.psum_scatter(in_early, "narrow", scatter_dimension=0, tiled=True)
        out_sections = []
    else:
        out_sections = [
            ((2, 0, block, ff_block), 3, 0, side, 0, 2 * width + side + late),
            ((2, 0, block, ff_block), 3, side, side, 1, 2 * width + side + late),
        ]
    cross_cols = 2 * width + side + late + (folds * side if out_sections else 0)

    branch_far = swapped(branch)
    cross_grads, memory_grad, grad, cross_gain_part = cross_backward(
        place, grad, after(branch, branch_far), after_self, gains, q, kv, cross_probs, w_cross
    )
    cross_parts = weight_grads(
        place,
        [(c_keep, c_far), (s_keep, s_far), (h_keep[None], h_far[None])],
        [(cross_grads, swapped(cross_grads)), (branch, branch_far), (gu, gu_far), (out_grad, og_far)],
        [
            ((0, 0, 0, block), 0, 0, width, 0, 0),
            ((0, 1, 0, block), 1, 0, width, 0, width),
            ((1, 1, 0, block), 0, 3 * width, side, 0, 2 * width),
            ((2, 0, 0, block), 2, early_grads, late, 0, 2 * width + side),
            ((0, 2, 0, block), 0, width, 2 * width, 1, 0),
            ((1, 1, 0, block), 0, 3 * width + side, side, 1, 2 * width),
            ((2, 0, 0, block), 2, early_grads + late, late, 1, 2 * width + side),
            *out_sections,
        ],
        (cross_cols, cross_cols),
    )
    cross_first, cross_second = cross_parts[:ny], cross_parts[ny:]
    cross_first, cross_second = sent(cross_first, "y"), sent(cross_second, "x")

    grad = after(grad, *cross_parts)
    self_grads, self_dv, tokens_grad, extra_keep, extra_send = self_backward(
        place, grad, cross_grads, tokens, gains, cross_gain_part, hidden_gain_part, qk, v,
        self_probs, hot, w_self, cut, block,
    )
    self_parts = weight_grads(
        place,
        [(s_keep, s_far)],
        [(self_grads, swapped(self_grads)), (self_dv, swapped(self_dv))],
        [
            ((0, 0, 0, block), 0, 0, width, 0, 0),
            ((0, 0, 0, block), 0, width, side, 0, width),
            ((0, 0, 0, block), 0, width + side, side, 1, 0),
            ((0, 0, 0, block), 1, 0, width, 1, side),
        ],
        (width + side + LANES, width + side),
        (extra_keep, swapped(extra_send)),
    )
    self_first, self_second = self_parts[:ny], self_parts[ny:]
    self_first, self_second = sent(self_first, "y"), sent(self_second, "x")
    cross_first = [after(cross_first[0], *self_parts)] + cross_first[1:]
    cross_parts = add_stage(place, cross_first, cross_second)
    cross_first, cross_second = cross_parts[:nx], cross_parts[nx:]
    cross_first, cross_second = sent(cross_first, "x"), sent(cross_second, "y")
    cross_parts = halve(place, [by_blocks(cross_first), by_blocks(cross_second)], 2, True)
    self_first = [after(self_first[0], cross_parts[0])] + self_first[1:]
    self_parts = add_stage(place, self_first, self_second)
    self_first, self_second = self_parts[:nx], self_parts[nx:]
    self_first, self_second = sent(self_first, "x"), sent(self_second, "y")
    if pieces:
        in_early = after(in_early, *self_parts).reshape(ny, nx, share, early_grads + folds * width)
        in_early = scatter_along([in_early], "y")
    count = 2
    while count < nz:
        count *= 2
        earlier = (*self_parts, *in_early) if pieces else self_parts
        cross_parts = halve(place, [[after(part, *earlier) for part in cross_parts]], count, False)
    self_first = [after(self_first[0], cross_parts[0])] + self_first[1:]
    self_sums = add_last(place, (self_first, self_second))
    if pieces:
        in_early = total_of(scatter_along([after(part, cross_parts[0]) for part in in_early], "x"))
    cross_total = total_of([part[0] for part in cross_parts])
    self_total = total_of(sent(self_sums, "z"))

    at = 2 * width + side
    in_parts = [cross_total[:, n + at : n + at + late] for n in (0, cross_cols)]
    if pieces:
        in_parts = [in_early[:, :early_grads]] + in_parts
        out_part = in_early[:, early_grads:].reshape(share, folds, width)
    else:
        out_part = jnp.concatenate(
            [cross_total[:, n + at + late : n + cross_cols].reshape(share, folds, side) for n in (0, cross_cols)],
            axis=2,
        )
    in_grad = reorder(jnp.concatenate([part.astype(LOW) for part in in_parts], axis=1), order, NT, F32)
    out_part = jnp.transpose(out_part, (1, 0, 2)).reshape(ff_share, width)
    first_cols = width + side + LANES
    last = self_total[:, width + side : first_cols]
    table_grad = last[:, TABLE_LANE : TABLE_LANE + groups * heads].reshape(share, groups, heads)
    table_grad = jnp.transpose(table_grad, (1, 0, 2)).reshape(groups * share, heads)[:table_rows]
    key_grad = jnp.concatenate(
        [self_total[:, width : width + side], self_total[:, first_cols : first_cols + side]], axis=1
    )
    output_grad = jnp.concatenate(
        [cross_total[:, n + 2 * width : n + 2 * width + side] for n in (0, cross_cols)], axis=1
    )
    return (
        layer_out,
        tokens_grad,
        memory_grad,
        self_total[:, :width],
        key_grad,
        self_total[:, first_cols + side :],
        output_grad,
        last[:, 0],
        table_grad,
        cross_total[:, :width],
        cross_total[:, cross_cols : cross_cols + width],
        cross_total[:, cross_cols + width : cross_cols + 2 * width],
        cross_total[:, width : 2 * width],
        last[:, 1],
        in_grad,
        out_part.astype(F32),
        last[:, 2],
    )


def solution(mesh):
    rows = P(("wide", "narrow"), None)
    line = P(("wide", "narrow"))
    table = P("narrow", None)
    return jax.shard_map(
        local,
        mesh=mesh,
        in_specs=(
            (rows,) * 4 + (line,) + (rows,) * 4 + (line, table) + (rows,) * 4 + (line,) + (rows,) * 2 + (line, rows)
        ),
        out_specs=(rows,) * 7 + (line, table) + (rows,) * 4 + (line,) + (rows,) * 2 + (line,),
        check_vma=False,
    )
```

```python
import math

import jax
import jax.numpy as jnp
import numpy as np
from jax import lax
from jax.experimental import pallas as pl
from jax.experimental.pallas import tpu as pltpu
from jax.sharding import PartitionSpec as P

BUCKETS = 32
REACH = 128
LOW = jnp.bfloat16
F32 = jnp.float32
NN = (((1,), (0,)), ((), ()))
NT = (((1,), (1,)), ((), ()))
TN = (((0,), (0,)), ((), ()))
PAIRS = 6
LANES = 128
TABLE_LANE = 16
CHUNK = 384
MiB = 1024 * 1024
FIRST_AT = 4
ORDER_AT = 12
EARLY = 0.5
EARLY_GRAD = 0.5


def bucket_edges(bucket_count, far_reach):
    exact_span = bucket_count // 2
    edge_list = list(range(1, exact_span + 1))
    for target in range(exact_span + 1, bucket_count):
        distance = exact_span
        while (
            exact_span
            + int(
                math.log(distance / exact_span)
                / math.log(far_reach / exact_span)
                * (bucket_count - exact_span)
            )
            < target
        ):
            distance += 1
        edge_list.append(distance)
    return edge_list


def distance_one_hot(rows):
    edges = np.array(bucket_edges(BUCKETS, REACH))
    buckets = (np.arange(rows)[:, None] >= edges[None, :]).sum(axis=1)
    return (np.arange(BUCKETS)[:, None] == buckets[None, :]).astype(np.float32)


def table_hot(rows, blocks, share, table_rows):
    one_hot = distance_one_hot(rows)
    groups = -(-table_rows // share)
    hot = np.zeros((groups, blocks * share, rows), np.float32)
    for block in range(blocks):
        for row in range(table_rows):
            hot[row // share, block * share + row % share] = one_hot[block * table_rows + row]
    return hot


def grid_sizes():
    wide = lax.axis_size("wide")
    inner = wide // 2
    across = 1
    while across * across < inner:
        across *= 2
    return {"y": inner // across, "x": across, "c": 2, "z": lax.axis_size("narrow")}


def grid_place():
    sizes = grid_sizes()
    wide = lax.axis_index("wide")
    return {
        "y": wide // (2 * sizes["x"]),
        "x": (wide // 2) % sizes["x"],
        "c": wide % 2,
        "z": lax.axis_index("narrow"),
    }


def shifted(array, dim, step):
    sizes = grid_sizes()
    count = sizes[dim]
    if dim == "z":
        return lax.ppermute(array, "narrow", [(i, (i + step) % count) for i in range(count)])
    stride = {"y": 2 * sizes["x"], "x": 2, "c": 1}[dim]
    pairs = []
    for source in range(lax.axis_size("wide")):
        place = (source // stride) % count
        pairs.append((source, source + ((place + step) % count - place) * stride))
    return lax.ppermute(array, "wide", pairs)


def after(value, *earlier):
    return lax.optimization_barrier((value, *earlier))[0]


def received(block, dim):
    count = grid_sizes()[dim]
    return [shifted(block, dim, count - step) for step in range(1, count)]


def swapped(array):
    return shifted(array, "c", 1)


def in_order(block, others, dim, axis):
    here = grid_place()[dim]
    cyclic = [block] + others
    count = len(cyclic)
    ordered = []
    for place in range(count):
        picked = cyclic[0]
        for step in range(1, count):
            picked = jnp.where((here + step) % count == place, cyclic[step], picked)
        ordered.append(picked)
    return jnp.stack(ordered, axis)


class Weights:
    def __init__(self, arrays, spots):
        self.arrays = arrays
        self.spots = spots

    def load(self, place, refs, matrices, sems, ranges=None, lazy=False):
        waits = []
        count = 0
        for low, high in ranges or [(0, None)]:
            copies = []
            for source, first, column, at, block, row, rows, matrix, there, cols in self.spots:
                start = row if at is None else pl.multiple_of(place[at] * block, block) + row
                from_column, to_column, size = column + low, there + low, (high or cols) - low
                copies.append(
                    pltpu.make_async_copy(
                        refs[source].at[pl.ds(first, rows), pl.ds(from_column, size)],
                        matrices[matrix].at[pl.ds(start, rows), pl.ds(to_column, size)],
                        sems.at[count],
                    )
                )
                count += 1
            waits.append((copies, lambda copies=copies: [copy.wait() for copy in copies]))
            if not lazy:
                for copy in copies:
                    copy.start()
        if lazy:
            return waits
        return [wait for _, wait in waits]

    def sems(self, ranges=1):
        return [pltpu.SemaphoreType.DMA((max(len(self.spots) * ranges, 1),))]


def fetch(sources, targets, sems):
    copies = [pltpu.make_async_copy(a, b, sems.at[n]) for n, (a, b) in enumerate(zip(sources, targets))]
    for copy in copies:
        copy.start()
    return [copy.wait for copy in copies]


def in_pieces(block):
    sizes = grid_sizes()
    return sizes["y"] == 2 and sizes["x"] == 2 and block % 32 == 0


def from_neighbours(block):
    return [block, shifted(block, "x", 1), shifted(block, "y", 1)]


def from_corner(upper, lower):
    return [shifted(upper, "y", 1), shifted(lower, "x", 1)]


def gather_pieces(block, *earlier, near=None):
    near = near or from_neighbours(block)
    half = block.shape[0] // 2
    twins = [swapped(near[0])]
    near_x, near_y = (after(array, twins[0], *earlier) for array in near[1:])
    corner = [shifted(near_x[:half], "y", 1), shifted(near_y[half:], "x", 1)]
    twins += [swapped(near_x), swapped(near_y)]
    return near, twins, corner


def pairs(near, twins):
    return [array for pair in zip(near, twins) for array in pair]


def gather_whole(block):
    block = in_order(block, received(block, "x"), "x", 0)
    block = in_order(block, received(block, "y"), "y", 0)
    block = in_order(block, received(block, "c"), "c", 2)
    return block.reshape(-1, block.shape[-1])


def near_spots(sources, block, column, matrix, there, cols):
    return [
        (source, 0, column, FIRST_AT + n, block, 0, block, matrix, there, cols) for n, source in enumerate(sources)
    ]


def half_spots(sources, block, column, matrix, there, cols):
    half = block // 2
    return [
        (source, 0, column, FIRST_AT + 6 + n % 2, block, (n // 2) * half, half, matrix, there, cols)
        for n, source in enumerate(sources)
    ]


def folded_spots(spots, block, column, groups, width, matrix):
    return [
        (source, first, column + g * width, at, groups * block, g * block + row, rows, matrix, 0, width)
        for source, first, _, at, _, row, rows, *_ in spots
        for g in range(groups)
    ]


def with_twins(arrays):
    return [array for own in arrays for array in (own, swapped(own))]


def run(name, kernel, inputs, outputs, scratch=(), flops=0, weights=(), aliases=()):
    inputs = list(inputs)
    for group in weights:
        inputs += [(array, pltpu.HBM) for array in group.arrays]
    size = sum(math.prod(array.shape) * array.dtype.itemsize for array, _ in inputs)
    arrays = [
        array if space == pltpu.SMEM else pltpu.with_memory_space_constraint(array, space)
        for array, space in inputs
    ]
    shapes = [
        jax.ShapeDtypeStruct(*output[:2]) if len(output) > 2 else pltpu.VMEM(*output) for output in outputs
    ]
    return pl.pallas_call(
        kernel,
        name=name,
        in_specs=[pl.BlockSpec(memory_space=space) for _, space in inputs],
        out_specs=[pl.BlockSpec(memory_space=pltpu.VMEM) for _ in outputs],
        out_shape=shapes,
        scratch_shapes=list(scratch),
        input_output_aliases=dict(aliases),
        compiler_params=pltpu.CompilerParams(vmem_limit_bytes=24 * MiB),
        cost_estimate=pl.CostEstimate(flops=flops, bytes_accessed=size // 2, transcendentals=0),
    )(*arrays)


def vmem(*arrays):
    return [(array, pltpu.VMEM) for array in arrays]


def dot(left, right, dims=NN):
    return lax.dot_general(left, right, dims, preferred_element_type=F32)


def scale_of(values):
    return lax.rsqrt(jnp.mean(values * values, axis=-1, keepdims=True) + 1e-06)


def norm_back(values, gain, grad):
    scale = scale_of(values)
    weighted = grad * gain
    middle = jnp.mean(values * weighted, axis=-1, keepdims=True)
    return (
        scale * weighted - values * (scale * scale * scale * middle),
        jnp.sum(grad * values * scale, axis=0, keepdims=True),
    )


def split_rows(matrix, core, keep, send):
    count, rows, _ = keep.shape
    if rows % 16:
        matrix = matrix.astype(F32)
    pieces = [matrix[n * rows : (n + 1) * rows].astype(keep.dtype) for n in range(2 * count)]

    @pl.when(core == 0)
    def _():
        for n in range(count):
            keep[n] = pieces[2 * n]
            send[n] = pieces[2 * n + 1]

    @pl.when(core == 1)
    def _():
        for n in range(count):
            keep[n] = pieces[2 * n + 1]
            send[n] = pieces[2 * n]


def lanes_of(pair, column=0):
    return pl.ds(pl.multiple_of(column + pair * LANES, LANES), LANES)


def head_mask(rows, head):
    lanes = lax.broadcasted_iota(jnp.int32, (rows, LANES), 1)
    return (lanes >= 64) if head else (lanes < 64)


def attend(q_ref, k_ref, v_ref, columns, allowed, bias, prob_ref, out_ref):
    rows = q_ref.shape[0]
    cols = k_ref.shape[0]

    def step(pair, carry):
        q = q_ref[:, lanes_of(pair, columns[0])]
        k = k_ref[:, lanes_of(pair, columns[1])]
        v_turned = v_ref[:, lanes_of(pair, columns[2])].T
        for head in range(2):
            mine = head_mask(rows, head)
            scores = dot(k, jnp.where(mine, q, jnp.zeros_like(q)), NT)
            if bias is not None:
                row = jnp.broadcast_to(bias[pl.ds(2 * pair + head, 1), :], (cols, rows))
                scores = scores + pltpu.roll(row, 0, 1, stride=1, stride_axis=0)
            scores = jnp.where(allowed[...] > 0, scores, -1e9)
            weights = jnp.exp(scores - jnp.max(scores, axis=0, keepdims=True))
            probs = (weights * (1.0 / jnp.sum(weights, axis=0, keepdims=True))).astype(LOW)
            prob_ref[2 * pair + head] = probs
            part = dot(v_turned[head * 64 : head * 64 + 64], probs)
            first = pl.multiple_of(pair * LANES + head * 64, 64)
            out_ref[pl.ds(first, 64), :] = part.astype(LOW)
        return carry

    lax.fori_loop(0, PAIRS, step, 0)


def attend_back(q_ref, k_ref, v_ref, columns, g_ref, prob_ref, outs, dist_ref):
    rows = q_ref.shape[0]
    cols = k_ref.shape[0]

    def step(pair, carry):
        q = q_ref[:, lanes_of(pair, columns[0])]
        k = k_ref[:, lanes_of(pair, columns[1])]
        v = v_ref[:, lanes_of(pair, columns[2])]
        g = g_ref[:, lanes_of(pair)]
        k_turned = k.T
        if dist_ref is not None:
            i = lax.broadcasted_iota(jnp.int32, (cols, cols), 0)
            j = lax.broadcasted_iota(jnp.int32, (cols, cols), 1)
            flip = (i + j == cols - 1).astype(LOW)
        grads = None
        query_parts = []
        for head in range(2):
            mine = head_mask(cols, head)
            low_probs = prob_ref[2 * pair + head]
            probs = low_probs.astype(F32)
            moved = probs * dot(v, jnp.where(head_mask(rows, head), g, jnp.zeros_like(g)), NT)
            low_scores = (moved - probs * jnp.sum(moved, axis=0, keepdims=True)).astype(LOW)
            if dist_ref is not None:
                lined = pltpu.roll(dot(flip, low_scores), 1, 1, stride=1, stride_axis=0)
                dist_ref[pl.ds(2 * pair + head, 1), :] = jnp.sum(lined, axis=0, keepdims=True)
            query_parts.append(dot(k_turned[head * 64 : head * 64 + 64], low_scores))
            new = (dot(low_scores, q), dot(low_probs, g))
            grads = new if head == 0 else tuple(jnp.where(mine, b, a) for a, b in zip(grads, new))
        query_grad = jnp.concatenate(query_parts, axis=0).T
        for (ref, column), grad in zip(outs, (query_grad, *grads)):
            ref[:, lanes_of(pair, column)] = grad.astype(LOW)
        return carry

    lax.fori_loop(0, PAIRS, step, 0)


def head_lanes(group, heads):
    head = lax.broadcasted_iota(jnp.int32, (16, LANES), 0)
    lane = lax.broadcasted_iota(jnp.int32, (16, LANES), 1)
    return ((head < heads) & (lane == TABLE_LANE + group * heads + head)).astype(F32)


def self_forward(place, tokens, row_ids, col_ids, pad, hot, weights, cut, block):
    rows, width = tokens.shape
    count = len(weights.arrays)
    heads = 2 * PAIRS
    groups = hot.shape[0]
    blocks = (width // block) // 2

    def kernel(place, tok, row_ids, col_ids, pad, hot, *refs):
        pieces, refs = refs[:count], refs[count:]
        qk, v, probs, out, keep, send, gains, matrix, allowed, bias, att, sems = refs
        wait, wait_late = weights.load(place, pieces, [matrix], sems, [(0, cut), (cut, cut + 2 * width)])
        i = lax.broadcasted_iota(jnp.int32, (rows, rows), 0)
        j = lax.broadcasted_iota(jnp.int32, (rows, rows), 1)
        same = (row_ids[...] == col_ids[...]) & (i <= j) & ((pad[...] == 1) | (i == j))
        allowed[...] = same.astype(F32)
        residual = tok[...].astype(F32)
        scaled = residual * scale_of(residual)
        wait()
        extra = matrix[:, 2 * width : cut].astype(F32)
        gains[...] = extra.T[:8]
        normed = (scaled * gains[0:1, :]).astype(LOW)
        total = None
        for group in range(groups):
            table = dot(extra[: hot.shape[1]], head_lanes(group, heads), NT)
            part = dot(table.astype(LOW), hot[group], TN)
            total = part if total is None else total + part
        bias[...] = total
        split_rows(normed.T, place[2], keep.at[0], send.at[0])
        qk[...] = dot(normed, matrix[:, : 2 * width]).astype(LOW)
        wait_late()
        v[...] = dot(normed, matrix[:, cut : cut + width]).astype(LOW)
        attend(qk, qk, v, (0, width, 0), allowed, bias, probs, att)
        attended = att[...]
        split_rows(attended, place[2], keep.at[1], send.at[1])
        out[...] = residual + dot(attended, matrix[:, cut + width :], TN)

    halves = ((2, blocks, block, rows), LOW)
    return run(
        "self_forward",
        kernel,
        [(place, pltpu.SMEM)] + vmem(tokens, row_ids, col_ids, pad, hot),
        [
            ((rows, 2 * width), LOW, None),
            ((rows, width), LOW, None),
            ((heads, rows, rows), LOW, None),
            ((rows, width), F32, None),
            halves,
            halves,
            ((8, width), F32),
        ],
        [
            pltpu.VMEM((width, cut + 2 * width), LOW),
            pltpu.VMEM((rows, rows), F32),
            pltpu.VMEM((16, rows), F32),
            pltpu.VMEM((width, rows), LOW),
        ]
        + weights.sems(2),
        flops=8 * rows * width * width,
        weights=[weights],
    )


def cross_forward(place, after_self, memory, gains, row_ids, col_ids, weights, block):
    rows, width = after_self.shape
    mem_rows = memory.shape[0]
    count = len(weights.arrays)
    blocks = (width // block) // 2

    def kernel(place, x, mem, gains, row_ids, col_ids, *refs):
        pieces, refs = refs[:count], refs[count:]
        q, kv, probs, out, keep, send, matrix, allowed, att, sems = refs
        wait, wait_late = weights.load(place, pieces, [matrix], sems, [(2 * width, 4 * width), (0, 2 * width)])
        allowed[...] = (row_ids[...] == col_ids[...]).astype(F32)
        residual = x[...]
        normed = (residual * scale_of(residual) * gains[1:2, :]).astype(LOW)
        split_rows(normed.T, place[2], keep.at[0], send.at[0])
        split_rows(mem[...].T, place[2], keep.at[2], send.at[2])
        wait()
        kv[...] = dot(mem[...], matrix[:, 2 * width :]).astype(LOW)
        wait_late()
        q[...] = dot(normed, matrix[:, :width]).astype(LOW)
        attend(q, kv, kv, (0, 0, width), allowed, None, probs, att)
        attended = att[...]
        split_rows(attended, place[2], keep.at[1], send.at[1])
        out[...] = residual + dot(attended, matrix[:, width : 2 * width], TN)

    halves = ((3, blocks, block, rows), LOW)
    return run(
        "cross_forward",
        kernel,
        [(place, pltpu.SMEM)] + vmem(after_self, memory, gains, row_ids, col_ids),
        [
            ((rows, width), LOW, None),
            ((mem_rows, 2 * width), LOW, None),
            ((2 * PAIRS, mem_rows, rows), LOW, None),
            ((rows, width), F32),
            halves,
            halves,
        ],
        [
            pltpu.VMEM((width, 4 * width), LOW),
            pltpu.VMEM((mem_rows, rows), F32),
            pltpu.VMEM((width, rows), LOW),
        ]
        + weights.sems(2),
        flops=8 * rows * width * width,
        weights=[weights],
    )


def hidden_order(nz, share, groups):
    units = np.arange(CHUNK).reshape(-1, nz, groups, share)
    order = np.transpose(units, (0, 2, 1, 3)).reshape(-1)
    matrix = np.zeros((CHUNK, CHUNK), np.float32)
    matrix[order, np.arange(CHUNK)] = 1.0
    return jnp.asarray(matrix).astype(LOW)


def reorder(array, order, dims, kind):
    def kernel(array, order, out):
        for start in range(0, array.shape[1], CHUNK):
            out[:, start : start + CHUNK] = dot(array[:, start : start + CHUNK], order[...], dims).astype(kind)

    return run("reorder", kernel, vmem(array, order), [(array.shape, kind, None)])[0]


def hidden_early(place, weights, width, ff):
    count = len(weights.arrays)

    def kernel(place, *refs):
        weights.load(place, refs[:count], refs[count : count + 2], refs[count + 2])[0]()

    return run(
        "hidden_early",
        kernel,
        [(place, pltpu.SMEM)],
        [((width, ff), LOW), ((ff, width), LOW)],
        weights.sems(),
        weights=[weights],
    )


def hidden_first(place, after_cross, out_grad, gains, m_in, m_out, weights, block):
    rows, width = after_cross.shape
    ff = m_in.shape[1]
    count = len(weights.arrays)
    blocks = (width // block) // 2
    ff_block = ff // (2 * blocks)
    factor = math.sqrt(2.0 / math.pi)

    def kernel(place, x, og, gains, m_in_before, m_out_before, *refs):
        pieces, refs = refs[:count], refs[count:]
        act, gu, keep, send, m_in, m_out, sems = refs
        (wait,) = weights.load(place, pieces, [m_in, m_out], sems)
        residual = x[...]
        normed = (residual * scale_of(residual) * gains[2:3, :]).astype(LOW)
        split_rows(normed.T, place[2], keep.at[:, :block], send.at[:, :block])
        grad = og[...]
        wait()
        for start in range(0, ff, CHUNK):
            stop = start + CHUNK
            u = dot(normed, m_in[:, start:stop])
            ga = dot(grad, m_out[start:stop, :], NT)
            square = u * u
            t = jnp.tanh(factor * u * (1.0 + 0.044715 * square))
            half = 0.5 * (1.0 + t)
            a = (u * half).astype(LOW)
            slope = half + (0.5 * factor) * u * (1.0 - t * t) * (1.0 + 3 * 0.044715 * square)
            gu[:, start:stop] = (slope * ga).astype(LOW)
            act[:, start:stop] = a
            turned = a.T
            for first in range(start, stop, ff_block):
                n = first // ff_block
                piece = turned[first - start : first - start + ff_block]

                @pl.when(place[2] == n % 2)
                def _(n=n, piece=piece):
                    keep[n // 2, block:] = piece

                @pl.when(place[2] != n % 2)
                def _(n=n, piece=piece):
                    send[n // 2, block:] = piece

    halves = ((blocks, block + ff_block, rows), LOW)
    return run(
        "hidden_first",
        kernel,
        [(place, pltpu.SMEM)] + vmem(after_cross, out_grad, gains, m_in, m_out),
        [
            ((rows, ff), LOW),
            ((rows, ff), LOW),
            halves,
            halves,
            (m_in.shape, LOW),
            (m_out.shape, LOW),
        ],
        weights.sems(),
        flops=4 * rows * width * ff,
        weights=[weights],
        aliases={4: 4, 5: 5},
    )


def hidden_second(after_cross, out_grad, gains, act, gu, m_in, m_out):
    rows, width = after_cross.shape
    ff = m_in.shape[1]

    def kernel(x, og, gains, act, gu, m_in, m_out, out, back_out, branch, gain_out):
        residual = x[...]
        back, gain = norm_back(residual, gains[2:3, :], dot(gu[...], m_in[...], NT))
        grad = og[...].astype(F32) + back
        back_out[...] = grad
        branch[...] = grad.astype(LOW)
        gain_out[...] = gain
        out[...] = (residual + dot(act[...], m_out[...])).astype(LOW)

    return run(
        "hidden_second",
        kernel,
        vmem(after_cross, out_grad, gains, act, gu, m_in, m_out),
        [((rows, width), LOW, None), ((rows, width), F32, None), ((rows, width), LOW, None), ((1, width), F32)],
        flops=4 * rows * width * ff,
    )


def cross_backward(place, grad, branch, after_self, gains, q, kv, probs, weights):
    rows, width = after_self.shape
    mem_rows = kv.shape[0]

    count = len(weights.arrays)

    def kernel(place, gains, *refs):
        far, refs = refs[:6], refs[6:]
        pieces, refs = refs[:count], refs[count:]
        out, mem_grad, back_out, gain_out, branch, grad, x, q, kv, probs, matrix, att, own_sems, sems = refs
        ranges = [(width, 2 * width), (0, width), (2 * width, 4 * width)]
        branch_wait = fetch(far[:1], (branch,), own_sems)
        loaded = weights.load(place, pieces, [matrix], sems, ranges, True)
        for copy in loaded[0][0]:
            copy.start()
        waits = fetch(far[1:4], (kv, probs, q), own_sems.at[pl.ds(1, 3)])
        for copy in loaded[1][0] + loaded[2][0]:
            copy.start()
        late_waits = fetch(far[4:], (x, grad), own_sems.at[pl.ds(4, 2)])
        branch_wait[0]()
        loaded[0][1]()
        att[...] = dot(branch[...], matrix[:, width : 2 * width], NT).astype(LOW)
        outs = ((out, 0), (out, width), (out, 2 * width))
        for wait in waits:
            wait()
        attend_back(q, kv, kv, (0, 0, width), att, probs, outs, None)
        loaded[1][1]()
        loaded[2][1]()
        for wait in late_waits:
            wait()
        back, gain = norm_back(x[...], gains[1:2, :], dot(out[:, :width], matrix[:, :width], NT))
        total = grad[...] + back
        back_out[...] = total
        out[:, 3 * width :] = total.astype(LOW)
        gain_out[...] = gain
        mem_grad[...] = dot(out[:, width : 3 * width], matrix[:, 2 * width :], NT)

    return run(
        "cross_backward",
        kernel,
        [(place, pltpu.SMEM)]
        + vmem(gains)
        + [(array, pltpu.HBM) for array in (branch, kv, probs, q, after_self, grad)],
        [
            ((rows, 4 * width), LOW),
            ((mem_rows, width), F32, None),
            ((rows, width), F32),
            ((1, width), F32),
        ],
        [
            pltpu.VMEM((rows, width), LOW),
            pltpu.VMEM((rows, width), F32),
            pltpu.VMEM((rows, width), F32),
            pltpu.VMEM((rows, width), LOW),
            pltpu.VMEM((mem_rows, 2 * width), LOW),
            pltpu.VMEM((2 * PAIRS, mem_rows, rows), LOW),
            pltpu.VMEM((width, 4 * width), LOW),
            pltpu.VMEM((rows, width), LOW),
            pltpu.SemaphoreType.DMA((6,)),
        ]
        + weights.sems(3),
        flops=8 * rows * width * width,
        weights=[weights],
    )


def self_backward(place, grad, cross_grads, tokens, gains, cross_gain, hidden_gain, qk, v, probs, hot, weights, cut, block):
    rows, width = tokens.shape
    count = len(weights.arrays)
    heads = 2 * PAIRS
    groups = hot.shape[0]
    blocks = (width // block) // 2
    under = width // 2 * LANES // width

    def kernel(place, grad, before, tok, gains, cross_gain, hidden_gain, hot, qk_far, v_far, probs_far, *refs):
        pieces, refs = refs[:count], refs[count:]
        out_q, out_k, out_v, tok_grad, extra_keep, extra_send, qk, v, probs, matrix, att, dist, parts, own_sems, sems = refs
        ranges = [(cut + width, cut + 2 * width), (0, cut + width)]
        loaded = weights.load(place, pieces, [matrix], sems, ranges, True)
        for copy in loaded[0][0]:
            copy.start()
        waits = fetch((v_far, probs_far, qk_far), (v, probs, qk), own_sems)
        for copy in loaded[1][0]:
            copy.start()
        loaded[0][1]()
        att[...] = dot(before[:, 3 * width :], matrix[:, cut + width :], NT).astype(LOW)
        outs = ((out_q, 0), (out_k, 0), (out_v.at[:rows], 0))
        dist[...] = jnp.zeros_like(dist)
        for wait in waits:
            wait()
        attend_back(qk, qk, v, (0, width, 0), att, probs, outs, dist)
        loaded[1][1]()
        normed_grad = dot(out_q[...], matrix[:, :width], NT) + dot(out_k[...], matrix[:, width : 2 * width], NT)
        normed_grad = normed_grad + dot(out_v[:rows, :], matrix[:, cut : cut + width], NT)
        back, gain = norm_back(tok[...].astype(F32), gains[0:1, :], normed_grad)
        tok_grad[...] = grad[...] + back
        parts[...] = jnp.zeros_like(parts)
        parts[0:1, :] = gain
        parts[1:2, :] = cross_gain[...]
        parts[2:3, :] = hidden_gain[...]
        columns = parts[...].T
        table = None
        for group in range(groups):
            sums = lax.dot_general(
                hot[group].astype(F32), dist[...], NT, precision=lax.Precision.HIGHEST, preferred_element_type=F32
            )
            part = lax.dot_general(
                sums, head_lanes(group, heads), NN, precision=lax.Precision.HIGHEST, preferred_element_type=F32
            )
            table = part if table is None else table + part
        columns = columns + jnp.concatenate([table] * (2 * blocks), axis=0)
        split_rows(columns, place[2], extra_keep, extra_send)
        sending = extra_send[...].astype(F32).reshape(width // 2, LANES)
        for n in range(width // LANES):
            out_v[rows:, n * LANES : (n + 1) * LANES] = sending[n * under : (n + 1) * under].astype(LOW)

    halves = ((blocks, block, LANES), LOW)
    return run(
        "self_backward",
        kernel,
        [(place, pltpu.SMEM)]
        + vmem(grad, cross_grads, tokens, gains, cross_gain, hidden_gain, hot)
        + [(array, pltpu.HBM) for array in (qk, v, probs)],
        [((rows, width), LOW)] * 2 + [((rows + under, width), LOW), ((rows, width), F32, None), halves],
        [
            pltpu.VMEM(halves[0], LOW),
            pltpu.VMEM((rows, 2 * width), LOW),
            pltpu.VMEM((rows, width), LOW),
            pltpu.VMEM((heads, rows, rows), LOW),
            pltpu.VMEM((width, cut + 2 * width), LOW),
            pltpu.VMEM((rows, width), LOW),
            pltpu.VMEM((16, rows), F32),
            pltpu.VMEM((LANES, width), F32),
            pltpu.SemaphoreType.DMA((3,)),
        ]
        + weights.sems(2),
        flops=8 * rows * width * width,
        weights=[weights],
    )


def weight_grads(place, lefts, rights, sections, cols, extras=(), straight=()):
    sizes = grid_sizes()
    counts = (sizes["y"], sizes["x"])
    blocks = counts[0] * counts[1]
    nz = sizes["z"]
    left_count, right_count = len(lefts), len(rights)
    block = min(section[0][3] for section in (*sections, *straight))
    across_z = sum(section[3] * (section[0][3] // block) for section in straight)
    tokens = rights[0][0].shape[0]
    most = max(section[0][3] for section in (*sections, *straight))

    def kernel(place, *refs):
        refs = list(refs)
        left = [(refs.pop(0), refs.pop(0)) for _ in range(left_count)]
        right = [(refs.pop(0), refs.pop(0)) for _ in range(right_count)]
        extra = [refs.pop(0) for _ in extras]
        far_extra, gathered = refs.pop(), refs.pop()
        outs = (refs[: counts[0]], refs[counts[0] : counts[0] + counts[1]])
        out_z = refs[-1]

        def place_of(half, n):
            step, other = n // counts[1 - half], n % counts[1 - half]
            there = (place[half] + step) % counts[half]
            return there * counts[1] + other if half == 0 else other * counts[1] + there

        def products(section, order):
            (l, n, row, rows), r, column, width = section[:4]
            joined = rows % 16 == 0 and row % 16 == 0
            if joined:
                for k in range(blocks):
                    for side in range(2):
                        gathered[k * rows : (k + 1) * rows, side * tokens : (side + 1) * tokens] = left[l][side][
                            n, order(k), row : row + rows, :
                        ]
            for first in range(0, width, 768):
                size = min(768, width - first)
                own, far = (ref[:tokens, column + first : column + first + size] for ref in right[r])
                if joined:
                    total = dot(gathered[: blocks * rows, :tokens], own)
                    total = total + dot(gathered[: blocks * rows, tokens:], far)
                for k in range(blocks):
                    if joined:
                        yield first, size, k, total[k * rows : (k + 1) * rows]
                        continue
                    own_rows, far_rows = (ref[n, order(k), row : row + rows, :] for ref in left[l])
                    yield first, size, k, dot(own_rows, own) + dot(far_rows, far)

        for section in straight:
            for first, size, index, total in products(section, lambda k: k):
                for g in range(section[0][3] // block):
                    at = section[5] + g * section[3] + first
                    for z in range(nz):
                        row = g * block + z * block // nz
                        part = total[row : row + block // nz]
                        out_z[z, index, :, at : at + size] = part.astype(LOW)
        for section in sections:
            groups = section[0][3] // block
            half = section[4]
            for first, size, k, total in products(section, lambda k: place_of(half, k)):
                for g in range(groups):
                    at = section[5] + g * section[3] + first
                    part = total[g * block : (g + 1) * block].astype(LOW)
                    outs[half][k // counts[1 - half]][k % counts[1 - half], :, at : at + size] = part
        if extras:
            sent_ref = right[-1][1]
            under = sent_ref.shape[0] - tokens
            for n in range(blocks * block // under):
                far_extra[n * under : (n + 1) * under, :] = sent_ref[tokens:, n * LANES : (n + 1) * LANES].astype(F32)
        for k in range(blocks if extras else 0):
            index = place_of(0, k)
            start = pl.multiple_of(index * block, 8)
            both = extra[0][index].astype(F32) + far_extra[pl.ds(start, block), :]
            outs[0][k // counts[1]][k % counts[1], :, cols[0] - LANES :] = both.astype(LOW)

    arrays = [array for pair in lefts for array in pair] + [array for pair in rights for array in pair]
    outputs = []
    if sections:
        outputs += [((counts[1], block, cols[0]), LOW)] * counts[0]
        outputs += [((counts[0], block, cols[1]), LOW)] * counts[1]
    if straight:
        outputs.append(((nz, blocks, block // nz, across_z), LOW, None))
    return run(
        "weight_grads",
        kernel,
        [(place, pltpu.SMEM)] + vmem(*arrays, *extras),
        outputs,
        [pltpu.VMEM((blocks * most, 2 * tokens), LOW), pltpu.VMEM((blocks * block, LANES), F32)],
        flops=sum(4 * s[0][3] * blocks * rights[0][0].shape[0] * s[3] for s in (*sections, *straight)),
    )


def add_stage(place, firsts, seconds):
    sizes = grid_sizes()
    counts = (sizes["x"], sizes["y"])

    def kernel(place, *refs):
        halves = (refs[: len(firsts)], refs[len(firsts) : len(firsts) + len(seconds)])
        outs = refs[len(firsts) + len(seconds) :]
        outs = (outs[: counts[0]], outs[counts[0] :])
        for half in range(2):
            here = place[1 - half]
            for step in range(counts[half]):
                index = (here + step) % counts[half]
                total = halves[half][0][index].astype(F32)
                for part in halves[half][1:]:
                    total = total + part[index].astype(F32)
                outs[half][step][...] = total.astype(LOW)

    outputs = [(firsts[0].shape[1:], LOW)] * counts[0] + [(seconds[0].shape[1:], LOW)] * counts[1]
    return run("add_stage", kernel, [(place, pltpu.SMEM)] + vmem(*firsts, *seconds), outputs)


def add_last(place, halves):
    count = grid_sizes()["z"]
    share = halves[0][0].shape[0] // count
    halves = [[part.reshape(count, share, part.shape[-1]) for part in parts] for parts in halves]
    cols = [parts[0].shape[-1] for parts in halves]

    def kernel(place, *refs):
        refs = list(refs)
        first = 0
        inputs = [[refs.pop(0) for _ in parts] for parts in halves]
        for parts, size in zip(inputs, cols):
            for step in range(count):
                index = (place[3] + step) % count
                total = parts[0][index].astype(F32)
                for part in parts[1:]:
                    total = total + part[index].astype(F32)
                refs[step][:, first : first + size] = total.astype(LOW)
            first += size

    return run(
        "add_last",
        kernel,
        [(place, pltpu.SMEM)] + vmem(*[part for parts in halves for part in parts]),
        [((share, sum(cols)), LOW)] * count,
    )


def mirrored(place, count):
    return place - place % count + count - 1 - place % count


def halving_order(place, count):
    order = [place]
    while len(order) < count:
        size = count // len(order)
        order += [mirrored(block, size) for block in order]
    return order


def halve(place, sides, count, first):
    have = sides[0][0].shape[0]
    half = have // 2
    cols = [parts[0].shape[2] for parts in sides]
    shape = (half, sides[0][0].shape[1], sum(cols))

    def kernel(place, *refs):
        refs = list(refs)
        inputs = [[refs.pop(0) for _ in parts] for parts in sides]
        order = halving_order(place[3], have) if first else range(have)
        for n in range(have):
            at = 0
            for parts, size in zip(inputs, cols):
                total = parts[0][order[n]].astype(F32)
                for part in parts[1:]:
                    total = total + part[order[n]].astype(F32)
                refs[n // half][n % half, :, at : at + size] = total.astype(LOW)
                at += size

    arrays = [part for parts in sides for part in parts]
    keep, send = run("halve", kernel, [(place, pltpu.SMEM)] + vmem(*arrays), [(shape, LOW), (shape, LOW)])
    pairs = [(i, mirrored(i, count)) for i in range(grid_sizes()["z"])]
    return keep, lax.ppermute(send, "narrow", pairs)


def by_blocks(parts):
    count = grid_sizes()["z"]
    return [part.reshape(count, part.shape[0] // count, part.shape[1]) for part in parts]


def finish_first(place, cross, early, order, early_cols, late, width, ff):
    share, cols = cross[0].shape[1:]
    cols = cols // 2
    side = width // 2
    folds = ff // width

    def kernel(place, near, far, kept, kept_far, other, order, c_query, c_key, c_value, c_output, s_output, h_in, h_out):
        total = near[0].astype(F32) + far[0].astype(F32)
        c_query[...] = total[:, :width]
        c_output[...] = total[:, width : 2 * width]
        s_output[:, :side] = total[:, 2 * width : 2 * width + side]
        c_key[...] = total[:, cols : cols + width]
        c_value[...] = total[:, cols + width : cols + 2 * width]
        s_output[:, side:] = total[:, cols + 2 * width : cols + 2 * width + side]
        x = place[1]
        first = kept[x].astype(F32) + kept_far[x].astype(F32) + other[...].astype(F32)
        for n in range(folds):
            h_out[n * share : (n + 1) * share, :] = first[:, early_cols + n * width : early_cols + (n + 1) * width]
        at = 2 * width + side
        pieces = [(first, 0, early_cols), (total, at, late), (total, cols + at, late)]
        start = 0
        for source, column, count in pieces:
            for n in range(0, count, CHUNK):
                part = source[:, column + n : column + n + CHUNK].astype(LOW)
                h_in[:, start : start + CHUNK] = dot(part, order[...], NT)
                start += CHUNK

    square = ((share, width), F32, None)
    return run(
        "finish_first",
        kernel,
        [(place, pltpu.SMEM)] + vmem(*cross, *early, order),
        [square] * 5 + [((share, ff), F32, None), ((share * folds, width), F32, None)],
    )


def finish_second(parts, width):
    share = parts[0].shape[0]
    side = width // 2
    cut = width + side + LANES

    def kernel(*refs):
        parts, (query, key, value, small) = refs[:-4], refs[-4:]
        total = parts[0][...].astype(F32)
        for part in parts[1:]:
            total = total + part[...].astype(F32)
        query[...] = total[:, :width]
        key[:, :side] = total[:, width : width + side]
        key[:, side:] = total[:, cut : cut + side]
        value[...] = total[:, cut + side :]
        small[...] = total[:, width + side : cut]

    square = ((share, width), F32, None)
    return run("finish_second", kernel, vmem(*parts), [square] * 3 + [((share, LANES), F32, None)])


def total_of(parts):
    return sum(part.astype(F32) for part in parts)


def scatter_along(parts, dim):
    count, here = grid_sizes()[dim], grid_place()[dim]
    kept = [lax.dynamic_index_in_dim(part, here, 0, keepdims=False) for part in parts]
    for step in range(1, count):
        there = (here + step) % count
        part = total_of([lax.dynamic_index_in_dim(part, there, 0, keepdims=False) for part in parts])
        kept.append(shifted(part.astype(LOW), dim, step))
    return kept


def sent(parts, dim):
    return [parts[0]] + [shifted(part, dim, step) for step, part in enumerate(parts) if step]


def segment_ids(length_row, slot_count):
    ends = jnp.cumsum(length_row).astype(jnp.int32)
    places = jnp.arange(slot_count, dtype=jnp.int32)
    return jnp.sum((places[:, None] >= ends[None, :]).astype(jnp.int32), axis=1).astype(jnp.int32)


def local(
    tokens, memory, doc_lengths, mem_lengths, pad_mask,
    self_query, self_key, self_value, self_output, self_gain, bias_table,
    cross_query, cross_key, cross_value, cross_output, cross_gain,
    hidden_in, hidden_out, hidden_gain, out_grad,
):
    sizes = grid_sizes()
    here = grid_place()
    ny, nx, nz = sizes["y"], sizes["x"], sizes["z"]
    rows, width = tokens.shape
    mem_rows = memory.shape[0]
    ff = hidden_in.shape[1]
    share = self_query.shape[0]
    ff_share = hidden_out.shape[0]
    table_rows, heads = bias_table.shape
    block = nz * share
    ff_block = nz * ff_share
    cut = 2 * width + LANES

    spots = []
    for step in range(4):
        y = (here["y"] + step // 2) % ny
        x = (here["x"] + step % 2) % nx
        for core in range(2):
            spots.append((y * nx + x) * 2 + (here["c"] + core) % 2)
    for n in range(4):
        spots += [2 * n + here["c"], 2 * n + 1 - here["c"]]
    place = jnp.stack([here["y"], here["x"], here["c"], here["z"]] + spots).astype(jnp.int32)
    pieces = in_pieces(block)
    half = block // 2

    hot = jnp.asarray(table_hot(rows, nz, share, table_rows)).astype(LOW)
    groups = hot.shape[0]
    table = jnp.pad(bias_table, ((0, groups * share - table_rows), (0, 0)))
    table = jnp.transpose(table.reshape(groups, share, heads), (1, 0, 2)).reshape(share, groups * heads)
    extra = jnp.concatenate(
        [
            self_gain[:, None],
            cross_gain[:, None],
            hidden_gain[:, None],
            jnp.zeros((share, TABLE_LANE - 3), LOW),
            table,
            jnp.zeros((share, LANES - TABLE_LANE - groups * heads), LOW),
        ],
        axis=1,
    )
    self_own = jnp.concatenate([self_query, self_key, extra, self_value, self_output], axis=1)
    self_others = received(self_own, "z")
    self_z = in_order(self_own, self_others, "z", 0).reshape(block, -1)
    folds = ff // width
    order = hidden_order(nz, share, folds)
    wide_out = jnp.transpose(hidden_out.reshape(folds, share, width), (1, 0, 2)).reshape(share, ff)
    hidden_own = reorder(hidden_in, order, NN, LOW)
    early_cols = int(ff * EARLY) // LANES * LANES if pieces else 0
    rest = jnp.concatenate(
        [cross_query, cross_output, cross_key, cross_value, hidden_own[:, early_cols:], wide_out], axis=1
    )
    rest = lax.all_gather(after(rest, self_others[0]), "narrow", axis=0, tiled=True)

    seg_ids = segment_ids(doc_lengths[0], rows)
    mem_ids = segment_ids(mem_lengths[0], mem_rows)
    if pieces:
        in_own = hidden_own[:, :early_cols]
        in_x, in_y = shifted(in_own, "x", 1), shifted(in_own, "y", 1)
        in_xy = shifted(in_x, "y", 1)
        in_all = in_order(
            in_order(in_own, [in_x], "x", 0), [in_order(in_y, [in_xy], "x", 0)], "y", 0
        ).reshape(4, share, early_cols)
        near, twins, corner = gather_pieces(self_z)
        in_all = lax.all_gather(after(in_all, rest, *corner), "narrow", axis=0, tiled=False)
        w_self = Weights(
            pairs(near, twins) + with_twins(corner),
            near_spots(range(6), block, 0, 0, 0, cut + 2 * width)
            + half_spots(range(6, 10), block, 0, 0, 0, cut + 2 * width),
        )
        rest_near = from_neighbours(after(rest, *twins, *corner))
    else:
        w_self = Weights([gather_whole(self_z)], [(0, 0, 0, None, 0, 0, width, 0, 0, cut + 2 * width)])

    og_far = swapped(out_grad)
    qk, v, self_probs, after_self, s_keep, s_send, gains = self_forward(
        place, after(tokens, og_far), seg_ids[:, None], seg_ids[None], pad_mask[:, None], hot, w_self, cut, block
    )
    s_far = swapped(s_send)
    if pieces:
        twin = swapped(rest_near[0])
        rest_x, rest_y = (after(array, after_self, s_far, twin) for array in rest_near[1:])
        corner = from_corner(rest_x[:half, :ff], rest_y[half:, :ff])
        upper, lower = rest_x[:half, ff:], rest_y[half:, ff:]
        in_all = jnp.transpose(after(in_all, twin), (1, 0, 2, 3)).reshape(4 * block, early_cols)
        corner = [after(array, upper, lower, in_all) for array in corner]
        rest_arrays = [rest_near[0], twin] + with_twins([rest_x, rest_y])
        w_cross = Weights(
            rest_arrays + with_twins(corner),
            near_spots(range(6), block, 0, 0, 0, ff) + half_spots(range(6, 10), block, 0, 0, 0, ff),
        )
        last = from_corner(upper, lower)
        cross_in = after(after_self, s_far, upper, lower)
    else:
        rest = gather_whole(rest)
        w_cross = Weights([rest], [(0, 0, 0, None, 0, 0, width, 0, 0, ff)])
        m_in = rest[:, ff : 2 * ff]
        m_out = jnp.transpose(rest[:, 2 * ff :].reshape(-1, block, folds, width), (0, 2, 1, 3)).reshape(ff, width)
        cross_in = after_self
    q, kv, cross_probs, after_cross, c_keep, c_send = cross_forward(
        place, cross_in, memory, gains, mem_ids[:, None], seg_ids[None], w_cross, block
    )
    c_far = swapped(c_send)
    if pieces:
        late_cols = ff - early_cols
        spots = folded_spots(near_spots(range(6), block, 0, 1, 0, 0), block, ff + late_cols, folds, width, 1)
        if late_cols:
            spots += near_spots(range(6), block, ff, 0, early_cols, late_cols)
        early = list(rest_arrays)
        for twin, array in enumerate((in_all, swapped(in_all))):
            spots += [
                (6 + twin, n * block, 0, ORDER_AT + 2 * n + twin, block, 0, block, 0, 0, early_cols) for n in range(4)
            ]
            early.append(array)
        m_in, m_out = hidden_early(after(place, after_cross), Weights(early, spots), width, ff)
        last = with_twins([after(array, after_cross) for array in last])
        spots = folded_spots(half_spots(range(4), block, 0, 1, 0, 0), block, late_cols, folds, width, 1)
        if late_cols:
            spots += half_spots(range(4), block, 0, 0, early_cols, late_cols)
        w_last = Weights(last, spots)
    else:
        w_last = Weights([], [])

    act, gu, h_keep, h_send, m_in, m_out = hidden_first(
        place, after(after_cross, c_far), out_grad, gains, m_in, m_out, w_last, block
    )
    h_far, gu_far = swapped(h_send), swapped(gu)
    layer_out, grad, branch, hidden_gain_part = hidden_second(after_cross, out_grad, gains, act, gu, m_in, m_out)
    h_keep = after(h_keep, grad)
    side = width // 2
    early_grads = int(ff * EARLY_GRAD) // LANES * LANES if pieces else 0
    late = (ff - early_grads) // 2
    if pieces:
        in_early = weight_grads(
            place,
            [(h_keep[None], h_far[None])],
            [(gu, gu_far), (out_grad, og_far)],
            [],
            (0, 0),
            straight=[
                ((0, 0, 0, block), 0, 0, early_grads, 2, 0),
                ((0, 0, block, ff_block), 1, 0, width, 2, early_grads),
            ],
        )[0]
        grad = after(grad, in_early)
        in_early = lax.psum_scatter(in_early, "narrow", scatter_dimension=0, tiled=True)
        out_sections = []
    else:
        out_sections = [
            ((2, 0, block, ff_block), 3, 0, side, 0, 2 * width + side + late),
            ((2, 0, block, ff_block), 3, side, side, 1, 2 * width + side + late),
        ]
    cross_cols = 2 * width + side + late + (folds * side if out_sections else 0)

    branch_far = swapped(branch)
    cross_grads, memory_grad, grad, cross_gain_part = cross_backward(
        place, grad, after(branch, branch_far), after_self, gains, q, kv, cross_probs, w_cross
    )
    cross_parts = weight_grads(
        place,
        [(c_keep, c_far), (s_keep, s_far), (h_keep[None], h_far[None])],
        [(cross_grads, swapped(cross_grads)), (branch, branch_far), (gu, gu_far), (out_grad, og_far)],
        [
            ((0, 0, 0, block), 0, 0, width, 0, 0),
            ((0, 1, 0, block), 1, 0, width, 0, width),
            ((1, 1, 0, block), 0, 3 * width, side, 0, 2 * width),
            ((2, 0, 0, block), 2, early_grads, late, 0, 2 * width + side),
            ((0, 2, 0, block), 0, width, 2 * width, 1, 0),
            ((1, 1, 0, block), 0, 3 * width + side, side, 1, 2 * width),
            ((2, 0, 0, block), 2, early_grads + late, late, 1, 2 * width + side),
            *out_sections,
        ],
        (cross_cols, cross_cols),
    )
    cross_first, cross_second = cross_parts[:ny], cross_parts[ny:]
    cross_first, cross_second = sent(cross_first, "y"), sent(cross_second, "x")

    grad = after(grad, *cross_parts)
    self_dq, self_dk, self_dv, tokens_grad, extra_keep = self_backward(
        place, grad, cross_grads, tokens, gains, cross_gain_part, hidden_gain_part, qk, v,
        self_probs, hot, w_self, cut, block,
    )
    self_parts = weight_grads(
        place,
        [(s_keep, s_far)],
        [(self_dq, swapped(self_dq)), (self_dk, swapped(self_dk)), (self_dv, swapped(self_dv))],
        [
            ((0, 0, 0, block), 0, 0, width, 0, 0),
            ((0, 0, 0, block), 1, 0, side, 0, width),
            ((0, 0, 0, block), 1, side, side, 1, 0),
            ((0, 0, 0, block), 2, 0, width, 1, side),
        ],
        (width + side + LANES, width + side),
        (extra_keep,),
    )
    self_first, self_second = self_parts[:ny], self_parts[ny:]
    self_first, self_second = sent(self_first, "y"), sent(self_second, "x")
    cross_first = [after(cross_first[0], *self_parts)] + cross_first[1:]
    cross_parts = add_stage(place, cross_first, cross_second)
    cross_first, cross_second = cross_parts[:nx], cross_parts[nx:]
    cross_first, cross_second = sent(cross_first, "x"), sent(cross_second, "y")
    cross_parts = halve(place, [by_blocks(cross_first), by_blocks(cross_second)], 2, True)
    self_first = [after(self_first[0], cross_parts[0])] + self_first[1:]
    self_parts = add_stage(place, self_first, self_second)
    self_first, self_second = self_parts[:nx], self_parts[nx:]
    self_first, self_second = sent(self_first, "x"), sent(self_second, "y")
    if pieces:
        in_early = after(in_early, *self_parts).reshape(ny, nx, share, early_grads + folds * width)
        in_early = scatter_along([in_early], "y")
    count = 2
    while count < nz:
        count *= 2
        earlier = (*self_parts, *in_early) if pieces else self_parts
        cross_parts = halve(place, [[after(part, *earlier) for part in cross_parts]], count, False)
    self_first = [after(self_first[0], cross_parts[0])] + self_first[1:]
    self_sums = add_last(place, (self_first, self_second))
    self_parts = sent(self_sums, "z")
    if pieces:
        in_early = [after(part, cross_parts[0]) for part in in_early]
        there = total_of([lax.dynamic_index_in_dim(part, 1 - here["x"], 0, keepdims=False) for part in in_early])
        in_early.append(shifted(there.astype(LOW), "x", 1))
        *cross_grads, in_grad, out_part = finish_first(
            place, cross_parts, in_early, order, early_grads, late, width, ff
        )
        self_parts = [after(self_parts[0], in_grad)] + self_parts[1:]
    else:
        cross_total = total_of([part[0] for part in cross_parts])
        at = 2 * width + side
        halves = [cross_total[:, n : n + cross_cols] for n in (0, cross_cols)]
        in_grad = jnp.concatenate([part[:, at : at + late].astype(LOW) for part in halves], axis=1)
        in_grad = reorder(in_grad, order, NT, F32)
        out_part = jnp.concatenate([part[:, at + late :].reshape(share, folds, side) for part in halves], axis=2)
        out_part = jnp.transpose(out_part, (1, 0, 2)).reshape(ff_share, width)
        cross_grads = [
            halves[0][:, :width],
            halves[1][:, :width],
            halves[1][:, width : 2 * width],
            halves[0][:, width : 2 * width],
            jnp.concatenate([part[:, 2 * width : at] for part in halves], axis=1),
        ]
    query_grad, key_grad, value_grad, last = finish_second(self_parts, width)
    table_grad = last[:, TABLE_LANE : TABLE_LANE + groups * heads].reshape(share, groups, heads)
    table_grad = jnp.transpose(table_grad, (1, 0, 2)).reshape(groups * share, heads)[:table_rows]
    return (
        layer_out,
        tokens_grad,
        memory_grad,
        query_grad,
        key_grad,
        value_grad,
        cross_grads[4],
        last[:, 0],
        table_grad,
        *cross_grads[:4],
        last[:, 1],
        in_grad,
        out_part,
        last[:, 2],
    )


def solution(mesh):
    rows = P(("wide", "narrow"), None)
    line = P(("wide", "narrow"))
    table = P("narrow", None)
    return jax.shard_map(
        local,
        mesh=mesh,
        in_specs=(
            (rows,) * 4 + (line,) + (rows,) * 4 + (line, table) + (rows,) * 4 + (line,) + (rows,) * 2 + (line, rows)
        ),
        out_specs=(rows,) * 7 + (line, table) + (rows,) * 4 + (line,) + (rows,) * 2 + (line,),
        check_vma=False,
    )
```

```python
import math

import jax
import jax.numpy as jnp
import numpy as np
from jax import lax
from jax.experimental import pallas as pl
from jax.experimental.pallas import tpu as pltpu
from jax.sharding import PartitionSpec as P

BUCKETS = 32
REACH = 128
LOW = jnp.bfloat16
F32 = jnp.float32
NN = (((1,), (0,)), ((), ()))
NT = (((1,), (1,)), ((), ()))
TN = (((0,), (0,)), ((), ()))
PAIRS = 6
LANES = 128
TABLE_LANE = 16
CHUNK = 384
MiB = 1024 * 1024
FIRST_AT = 4
ORDER_AT = 12
EARLY = 0.5
EARLY_GRAD = 0.25


def bucket_edges(bucket_count, far_reach):
    exact_span = bucket_count // 2
    edge_list = list(range(1, exact_span + 1))
    for target in range(exact_span + 1, bucket_count):
        distance = exact_span
        while (
            exact_span
            + int(
                math.log(distance / exact_span)
                / math.log(far_reach / exact_span)
                * (bucket_count - exact_span)
            )
            < target
        ):
            distance += 1
        edge_list.append(distance)
    return edge_list


def distance_one_hot(rows):
    edges = np.array(bucket_edges(BUCKETS, REACH))
    buckets = (np.arange(rows)[:, None] >= edges[None, :]).sum(axis=1)
    return (np.arange(BUCKETS)[:, None] == buckets[None, :]).astype(np.float32)


def table_hot(rows, blocks, share, table_rows):
    one_hot = distance_one_hot(rows)
    groups = -(-table_rows // share)
    hot = np.zeros((groups, blocks * share, rows), np.float32)
    for block in range(blocks):
        for row in range(table_rows):
            hot[row // share, block * share + row % share] = one_hot[block * table_rows + row]
    return hot


def grid_sizes():
    wide = lax.axis_size("wide")
    inner = wide // 2
    across = 1
    while across * across < inner:
        across *= 2
    return {"y": inner // across, "x": across, "c": 2, "z": lax.axis_size("narrow")}


def grid_place():
    sizes = grid_sizes()
    wide = lax.axis_index("wide")
    return {
        "y": wide // (2 * sizes["x"]),
        "x": (wide // 2) % sizes["x"],
        "c": wide % 2,
        "z": lax.axis_index("narrow"),
    }


def shifted(array, dim, step):
    sizes = grid_sizes()
    count = sizes[dim]
    if dim == "z":
        return lax.ppermute(array, "narrow", [(i, (i + step) % count) for i in range(count)])
    stride = {"y": 2 * sizes["x"], "x": 2, "c": 1}[dim]
    pairs = []
    for source in range(lax.axis_size("wide")):
        place = (source // stride) % count
        pairs.append((source, source + ((place + step) % count - place) * stride))
    return lax.ppermute(array, "wide", pairs)


def after(value, *earlier):
    return lax.optimization_barrier((value, *earlier))[0]


def received(block, dim):
    count = grid_sizes()[dim]
    return [shifted(block, dim, count - step) for step in range(1, count)]


def swapped(array):
    return shifted(array, "c", 1)


def in_order(block, others, dim, axis):
    here = grid_place()[dim]
    cyclic = [block] + others
    count = len(cyclic)
    ordered = []
    for place in range(count):
        picked = cyclic[0]
        for step in range(1, count):
            picked = jnp.where((here + step) % count == place, cyclic[step], picked)
        ordered.append(picked)
    return jnp.stack(ordered, axis)


class Weights:
    def __init__(self, arrays, spots):
        self.arrays = arrays
        self.spots = spots

    def load(self, place, refs, matrices, sems, ranges=None, lazy=False):
        waits = []
        count = 0
        for low, high in ranges or [(0, None)]:
            copies = []
            for source, first, column, at, block, row, rows, matrix, there, cols in self.spots:
                start = row if at is None else pl.multiple_of(place[at] * block, block) + row
                from_column, to_column, size = column + low, there + low, (high or cols) - low
                copies.append(
                    pltpu.make_async_copy(
                        refs[source].at[pl.ds(first, rows), pl.ds(from_column, size)],
                        matrices[matrix].at[pl.ds(start, rows), pl.ds(to_column, size)],
                        sems.at[count],
                    )
                )
                count += 1
            waits.append((copies, lambda copies=copies: [copy.wait() for copy in copies]))
            if not lazy:
                for copy in copies:
                    copy.start()
        if lazy:
            return waits
        return [wait for _, wait in waits]

    def sems(self, ranges=1):
        return [pltpu.SemaphoreType.DMA((max(len(self.spots) * ranges, 1),))]


def fetch(sources, targets, sems):
    copies = [pltpu.make_async_copy(a, b, sems.at[n]) for n, (a, b) in enumerate(zip(sources, targets))]
    for copy in copies:
        copy.start()
    return [copy.wait for copy in copies]


def in_pieces(block):
    sizes = grid_sizes()
    return sizes["y"] == 2 and sizes["x"] == 2 and block % 32 == 0


def from_neighbours(block):
    return [block, shifted(block, "x", 1), shifted(block, "y", 1)]


def from_corner(upper, lower):
    return [shifted(upper, "y", 1), shifted(lower, "x", 1)]


def gather_pieces(block, *earlier, near=None):
    near = near or from_neighbours(block)
    half = block.shape[0] // 2
    twins = [swapped(near[0])]
    near_x, near_y = (after(array, twins[0], *earlier) for array in near[1:])
    corner = [shifted(near_x[:half], "y", 1), shifted(near_y[half:], "x", 1)]
    twins += [swapped(near_x), swapped(near_y)]
    return near, twins, corner


def pairs(near, twins):
    return [array for pair in zip(near, twins) for array in pair]


def gather_whole(block):
    block = in_order(block, received(block, "x"), "x", 0)
    block = in_order(block, received(block, "y"), "y", 0)
    block = in_order(block, received(block, "c"), "c", 2)
    return block.reshape(-1, block.shape[-1])


def near_spots(sources, block, column, matrix, there, cols):
    return [
        (source, 0, column, FIRST_AT + n, block, 0, block, matrix, there, cols) for n, source in enumerate(sources)
    ]


def half_spots(sources, block, column, matrix, there, cols):
    half = block // 2
    return [
        (source, 0, column, FIRST_AT + 6 + n % 2, block, (n // 2) * half, half, matrix, there, cols)
        for n, source in enumerate(sources)
    ]


def folded_spots(spots, block, column, groups, width, matrix):
    return [
        (source, first, column + g * width, at, groups * block, g * block + row, rows, matrix, 0, width)
        for source, first, _, at, _, row, rows, *_ in spots
        for g in range(groups)
    ]


def with_twins(arrays):
    return [array for own in arrays for array in (own, swapped(own))]


def run(name, kernel, inputs, outputs, scratch=(), flops=0, weights=(), aliases=()):
    inputs = list(inputs)
    for group in weights:
        inputs += [(array, pltpu.HBM) for array in group.arrays]
    size = sum(math.prod(array.shape) * array.dtype.itemsize for array, _ in inputs)
    arrays = [
        array if space == pltpu.SMEM else pltpu.with_memory_space_constraint(array, space)
        for array, space in inputs
    ]
    shapes = [
        jax.ShapeDtypeStruct(*output[:2]) if len(output) > 2 else pltpu.VMEM(*output) for output in outputs
    ]
    return pl.pallas_call(
        kernel,
        name=name,
        in_specs=[pl.BlockSpec(memory_space=space) for _, space in inputs],
        out_specs=[pl.BlockSpec(memory_space=pltpu.VMEM) for _ in outputs],
        out_shape=shapes,
        scratch_shapes=list(scratch),
        input_output_aliases=dict(aliases),
        compiler_params=pltpu.CompilerParams(vmem_limit_bytes=24 * MiB),
        cost_estimate=pl.CostEstimate(flops=flops, bytes_accessed=size // 2, transcendentals=0),
    )(*arrays)


def vmem(*arrays):
    return [(array, pltpu.VMEM) for array in arrays]


def dot(left, right, dims=NN):
    return lax.dot_general(left, right, dims, preferred_element_type=F32)


def scale_of(values):
    return lax.rsqrt(jnp.mean(values * values, axis=-1, keepdims=True) + 1e-06)


def norm_back(values, gain, grad):
    scale = scale_of(values)
    weighted = grad * gain
    middle = jnp.mean(values * weighted, axis=-1, keepdims=True)
    return (
        scale * weighted - values * (scale * scale * scale * middle),
        jnp.sum(grad * values * scale, axis=0, keepdims=True),
    )


def split_rows(matrix, core, keep, send):
    count, rows, _ = keep.shape
    if rows % 16:
        matrix = matrix.astype(F32)
    pieces = [matrix[n * rows : (n + 1) * rows].astype(keep.dtype) for n in range(2 * count)]

    @pl.when(core == 0)
    def _():
        for n in range(count):
            keep[n] = pieces[2 * n]
            send[n] = pieces[2 * n + 1]

    @pl.when(core == 1)
    def _():
        for n in range(count):
            keep[n] = pieces[2 * n + 1]
            send[n] = pieces[2 * n]


def lanes_of(pair, column=0):
    return pl.ds(pl.multiple_of(column + pair * LANES, LANES), LANES)


def head_mask(rows, head):
    lanes = lax.broadcasted_iota(jnp.int32, (rows, LANES), 1)
    return (lanes >= 64) if head else (lanes < 64)


def attend(q_ref, k_ref, v_ref, columns, allowed, bias, prob_ref, out_ref):
    rows = q_ref.shape[0]
    cols = k_ref.shape[0]

    def step(pair, carry):
        q = q_ref[:, lanes_of(pair, columns[0])]
        k = k_ref[:, lanes_of(pair, columns[1])]
        v_turned = v_ref[:, lanes_of(pair, columns[2])].T
        for head in range(2):
            mine = head_mask(rows, head)
            scores = dot(k, jnp.where(mine, q, jnp.zeros_like(q)), NT)
            if bias is not None:
                row = jnp.broadcast_to(bias[pl.ds(2 * pair + head, 1), :], (cols, rows))
                scores = scores + pltpu.roll(row, 0, 1, stride=1, stride_axis=0)
            scores = jnp.where(allowed[...] > 0, scores, -1e9)
            weights = jnp.exp(scores - jnp.max(scores, axis=0, keepdims=True))
            probs = (weights * (1.0 / jnp.sum(weights, axis=0, keepdims=True))).astype(LOW)
            prob_ref[2 * pair + head] = probs
            part = dot(v_turned[head * 64 : head * 64 + 64], probs)
            first = pl.multiple_of(pair * LANES + head * 64, 64)
            out_ref[pl.ds(first, 64), :] = part.astype(LOW)
        return carry

    lax.fori_loop(0, PAIRS, step, 0)


def attend_back(q_ref, k_ref, v_ref, columns, g_ref, prob_ref, outs, dist_ref):
    rows = q_ref.shape[0]
    cols = k_ref.shape[0]

    def step(pair, carry):
        q = q_ref[:, lanes_of(pair, columns[0])]
        k = k_ref[:, lanes_of(pair, columns[1])]
        v = v_ref[:, lanes_of(pair, columns[2])]
        g = g_ref[:, lanes_of(pair)]
        k_turned = k.T
        if dist_ref is not None:
            i = lax.broadcasted_iota(jnp.int32, (cols, cols), 0)
            j = lax.broadcasted_iota(jnp.int32, (cols, cols), 1)
            flip = (i + j == cols - 1).astype(LOW)
        grads = None
        query_parts = []
        for head in range(2):
            mine = head_mask(cols, head)
            low_probs = prob_ref[2 * pair + head]
            probs = low_probs.astype(F32)
            moved = probs * dot(v, jnp.where(head_mask(rows, head), g, jnp.zeros_like(g)), NT)
            low_scores = (moved - probs * jnp.sum(moved, axis=0, keepdims=True)).astype(LOW)
            if dist_ref is not None:
                lined = pltpu.roll(dot(flip, low_scores), 1, 1, stride=1, stride_axis=0)
                dist_ref[pl.ds(2 * pair + head, 1), :] = jnp.sum(lined, axis=0, keepdims=True)
            query_parts.append(dot(k_turned[head * 64 : head * 64 + 64], low_scores))
            new = (dot(low_scores, q), dot(low_probs, g))
            grads = new if head == 0 else tuple(jnp.where(mine, b, a) for a, b in zip(grads, new))
        query_grad = jnp.concatenate(query_parts, axis=0).T
        for (ref, column), grad in zip(outs, (query_grad, *grads)):
            ref[:, lanes_of(pair, column)] = grad.astype(LOW)
        return carry

    lax.fori_loop(0, PAIRS, step, 0)


def head_lanes(group, heads):
    head = lax.broadcasted_iota(jnp.int32, (16, LANES), 0)
    lane = lax.broadcasted_iota(jnp.int32, (16, LANES), 1)
    return ((head < heads) & (lane == TABLE_LANE + group * heads + head)).astype(F32)


def self_forward(place, tokens, row_ids, col_ids, pad, hot, weights, cut, block):
    rows, width = tokens.shape
    count = len(weights.arrays)
    heads = 2 * PAIRS
    groups = hot.shape[0]
    blocks = (width // block) // 2

    def kernel(place, tok, row_ids, col_ids, pad, hot, *refs):
        pieces, refs = refs[:count], refs[count:]
        qk, v, probs, out, keep, send, gains, matrix, allowed, bias, att, sems = refs
        wait, wait_late = weights.load(place, pieces, [matrix], sems, [(0, cut), (cut, cut + 2 * width)])
        i = lax.broadcasted_iota(jnp.int32, (rows, rows), 0)
        j = lax.broadcasted_iota(jnp.int32, (rows, rows), 1)
        same = (row_ids[...] == col_ids[...]) & (i <= j) & ((pad[...] == 1) | (i == j))
        allowed[...] = same.astype(F32)
        residual = tok[...].astype(F32)
        scaled = residual * scale_of(residual)
        wait()
        extra = matrix[:, 2 * width : cut].astype(F32)
        gains[...] = extra.T[:8]
        normed = (scaled * gains[0:1, :]).astype(LOW)
        total = None
        for group in range(groups):
            table = dot(extra[: hot.shape[1]], head_lanes(group, heads), NT)
            part = dot(table.astype(LOW), hot[group], TN)
            total = part if total is None else total + part
        bias[...] = total
        split_rows(normed.T, place[2], keep.at[0], send.at[0])
        qk[...] = dot(normed, matrix[:, : 2 * width]).astype(LOW)
        wait_late()
        v[...] = dot(normed, matrix[:, cut : cut + width]).astype(LOW)
        attend(qk, qk, v, (0, width, 0), allowed, bias, probs, att)
        attended = att[...]
        split_rows(attended, place[2], keep.at[1], send.at[1])
        out[...] = residual + dot(attended, matrix[:, cut + width :], TN)

    halves = ((2, blocks, block, rows), LOW)
    return run(
        "self_forward",
        kernel,
        [(place, pltpu.SMEM)] + vmem(tokens, row_ids, col_ids, pad, hot),
        [
            ((rows, 2 * width), LOW, None),
            ((rows, width), LOW, None),
            ((heads, rows, rows), LOW, None),
            ((rows, width), F32, None),
            halves,
            halves,
            ((8, width), F32),
        ],
        [
            pltpu.VMEM((width, cut + 2 * width), LOW),
            pltpu.VMEM((rows, rows), F32),
            pltpu.VMEM((16, rows), F32),
            pltpu.VMEM((width, rows), LOW),
        ]
        + weights.sems(2),
        flops=8 * rows * width * width,
        weights=[weights],
    )


def cross_forward(place, after_self, memory, gains, row_ids, col_ids, weights, block):
    rows, width = after_self.shape
    mem_rows = memory.shape[0]
    count = len(weights.arrays)
    blocks = (width // block) // 2

    def kernel(place, x, mem, gains, row_ids, col_ids, *refs):
        pieces, refs = refs[:count], refs[count:]
        q, kv, probs, out, keep, send, matrix, allowed, att, sems = refs
        wait, wait_late = weights.load(place, pieces, [matrix], sems, [(2 * width, 4 * width), (0, 2 * width)])
        allowed[...] = (row_ids[...] == col_ids[...]).astype(F32)
        residual = x[...]
        normed = (residual * scale_of(residual) * gains[1:2, :]).astype(LOW)
        split_rows(normed.T, place[2], keep.at[0], send.at[0])
        split_rows(mem[...].T, place[2], keep.at[2], send.at[2])
        wait()
        kv[...] = dot(mem[...], matrix[:, 2 * width :]).astype(LOW)
        wait_late()
        q[...] = dot(normed, matrix[:, :width]).astype(LOW)
        attend(q, kv, kv, (0, 0, width), allowed, None, probs, att)
        attended = att[...]
        split_rows(attended, place[2], keep.at[1], send.at[1])
        out[...] = residual + dot(attended, matrix[:, width : 2 * width], TN)

    halves = ((3, blocks, block, rows), LOW)
    return run(
        "cross_forward",
        kernel,
        [(place, pltpu.SMEM)] + vmem(after_self, memory, gains, row_ids, col_ids),
        [
            ((rows, width), LOW, None),
            ((mem_rows, 2 * width), LOW, None),
            ((2 * PAIRS, mem_rows, rows), LOW, None),
            ((rows, width), F32),
            halves,
            halves,
        ],
        [
            pltpu.VMEM((width, 4 * width), LOW),
            pltpu.VMEM((mem_rows, rows), F32),
            pltpu.VMEM((width, rows), LOW),
        ]
        + weights.sems(2),
        flops=8 * rows * width * width,
        weights=[weights],
    )


def hidden_order(nz, share, groups):
    units = np.arange(CHUNK).reshape(-1, nz, groups, share)
    order = np.transpose(units, (0, 2, 1, 3)).reshape(-1)
    matrix = np.zeros((CHUNK, CHUNK), np.float32)
    matrix[order, np.arange(CHUNK)] = 1.0
    return jnp.asarray(matrix).astype(LOW)


def reorder(array, order, dims, kind):
    def kernel(array, order, out):
        for start in range(0, array.shape[1], CHUNK):
            out[:, start : start + CHUNK] = dot(array[:, start : start + CHUNK], order[...], dims).astype(kind)

    return run("reorder", kernel, vmem(array, order), [(array.shape, kind, None)])[0]


def hidden_early(place, weights, width, ff):
    count = len(weights.arrays)

    def kernel(place, *refs):
        weights.load(place, refs[:count], refs[count : count + 2], refs[count + 2])[0]()

    return run(
        "hidden_early",
        kernel,
        [(place, pltpu.SMEM)],
        [((width, ff), LOW), ((ff, width), LOW)],
        weights.sems(),
        weights=[weights],
    )


def fetching(kernel, arrays):
    count = len(arrays)

    def fetched(*refs):
        sources, outs, refs = refs[:count], refs[count : -count - 1], refs[-count - 1 :]
        for wait in fetch(sources, refs[:-1], refs[-1]):
            wait()
        kernel(*refs[:-1], *outs)

    scratch = [pltpu.VMEM(array.shape, array.dtype) for array in arrays]
    return fetched, scratch + [pltpu.SemaphoreType.DMA((count,))]


def pack_first(squares, gains, table, cut):
    share, width = squares[0].shape
    table_rows, heads = table.shape

    def kernel(query, key, value, output, *refs):
        gains, (table, out, lanes) = refs[:3], refs[3:]
        lanes[...] = jnp.zeros_like(lanes)
        rows = jnp.concatenate([gain[...].astype(F32) for gain in gains] + [jnp.zeros((5, share), F32)], axis=0)
        lanes[:, :8] = rows.T
        for group in range(-(-table_rows // share)):
            part = table[...].astype(F32)[group * share : (group + 1) * share]
            at = TABLE_LANE + group * heads
            lanes[: part.shape[0], at : at + heads] = part
        out[:, :width] = query[...]
        out[:, width : 2 * width] = key[...]
        out[:, 2 * width : cut] = lanes[...].astype(LOW)
        out[:, cut : cut + width] = value[...]
        out[:, cut + width :] = output[...]

    arrays = [*squares, *[gain.reshape(1, share) for gain in gains], table]
    fetched, scratch = fetching(kernel, arrays)
    return run(
        "pack_first",
        fetched,
        [(array, pltpu.HBM) for array in arrays],
        [((share, cut + 2 * width), LOW)],
        [pltpu.VMEM((share, LANES), F32), *scratch],
    )[0]


def pack_rest(squares, hidden_in, hidden_out, order, early_cols):
    share, width = squares[0].shape
    ff = hidden_in.shape[1]
    folds = ff // width
    late = ff - early_cols

    def kernel(*refs):
        squares, (h_in, h_out, order, rest, early) = refs[:4], refs[4:]
        for start in range(0, ff, CHUNK):
            part = dot(h_in[:, start : start + CHUNK], order[...]).astype(LOW)
            if start < early_cols:
                early[:, start : start + CHUNK] = part
            else:
                at = 4 * width + start - early_cols
                rest[:, at : at + CHUNK] = part
        for n, square in enumerate(squares):
            rest[:, n * width : (n + 1) * width] = square[...]
        rows = h_out[...].astype(F32)
        for n in range(folds):
            at = 4 * width + late + n * width
            rest[:, at : at + width] = rows[n * share : (n + 1) * share].astype(LOW)

    arrays = [*squares, hidden_in, hidden_out, order]
    fetched, scratch = fetching(kernel, arrays)
    return run(
        "pack_rest",
        fetched,
        [(array, pltpu.HBM) for array in arrays],
        [((share, 4 * width + late + ff), LOW, None), ((share, early_cols), LOW, None)],
        scratch,
    )


def hidden_first(place, after_cross, out_grad, gains, m_in, m_out, weights, block):
    rows, width = after_cross.shape
    ff = m_in.shape[1]
    count = len(weights.arrays)
    blocks = (width // block) // 2
    ff_block = ff // (2 * blocks)
    factor = math.sqrt(2.0 / math.pi)

    def kernel(place, x, og, gains, m_in_before, m_out_before, *refs):
        pieces, refs = refs[:count], refs[count:]
        act, gu, keep, send, m_in, m_out, sems = refs
        (wait,) = weights.load(place, pieces, [m_in, m_out], sems)
        residual = x[...]
        normed = (residual * scale_of(residual) * gains[2:3, :]).astype(LOW)
        split_rows(normed.T, place[2], keep.at[:, :block], send.at[:, :block])
        grad = og[...]
        wait()
        for start in range(0, ff, CHUNK):
            stop = start + CHUNK
            u = dot(normed, m_in[:, start:stop])
            ga = dot(grad, m_out[start:stop, :], NT)
            square = u * u
            t = jnp.tanh(factor * u * (1.0 + 0.044715 * square))
            half = 0.5 * (1.0 + t)
            a = (u * half).astype(LOW)
            slope = half + (0.5 * factor) * u * (1.0 - t * t) * (1.0 + 3 * 0.044715 * square)
            gu[:, start:stop] = (slope * ga).astype(LOW)
            act[:, start:stop] = a
            turned = a.T
            for first in range(start, stop, ff_block):
                n = first // ff_block
                piece = turned[first - start : first - start + ff_block]

                @pl.when(place[2] == n % 2)
                def _(n=n, piece=piece):
                    keep[n // 2, block:] = piece

                @pl.when(place[2] != n % 2)
                def _(n=n, piece=piece):
                    send[n // 2, block:] = piece

    halves = ((blocks, block + ff_block, rows), LOW)
    return run(
        "hidden_first",
        kernel,
        [(place, pltpu.SMEM)] + vmem(after_cross, out_grad, gains, m_in, m_out),
        [
            ((rows, ff), LOW),
            ((rows, ff), LOW),
            halves,
            halves,
            (m_in.shape, LOW),
            (m_out.shape, LOW),
        ],
        weights.sems(),
        flops=4 * rows * width * ff,
        weights=[weights],
        aliases={4: 4, 5: 5},
    )


def hidden_second(after_cross, out_grad, gains, act, gu, m_in, m_out):
    rows, width = after_cross.shape
    ff = m_in.shape[1]

    def kernel(x, og, gains, act, gu, m_in, m_out, out, back_out, branch, gain_out):
        residual = x[...]
        back, gain = norm_back(residual, gains[2:3, :], dot(gu[...], m_in[...], NT))
        grad = og[...].astype(F32) + back
        back_out[...] = grad
        branch[...] = grad.astype(LOW)
        gain_out[...] = gain
        out[...] = (residual + dot(act[...], m_out[...])).astype(LOW)

    return run(
        "hidden_second",
        kernel,
        vmem(after_cross, out_grad, gains, act, gu, m_in, m_out),
        [((rows, width), LOW, None), ((rows, width), F32, None), ((rows, width), LOW, None), ((1, width), F32)],
        flops=4 * rows * width * ff,
    )


def cross_backward(place, grad, branch, after_self, gains, q, kv, probs, weights):
    rows, width = after_self.shape
    mem_rows = kv.shape[0]

    count = len(weights.arrays)

    def kernel(place, gains, *refs):
        far, refs = refs[:6], refs[6:]
        pieces, refs = refs[:count], refs[count:]
        out, mem_grad, back_out, gain_out, branch, grad, x, q, kv, probs, matrix, att, own_sems, sems = refs
        ranges = [(width, 2 * width), (0, width), (2 * width, 4 * width)]
        branch_wait = fetch(far[:1], (branch,), own_sems)
        loaded = weights.load(place, pieces, [matrix], sems, ranges, True)
        for copy in loaded[0][0]:
            copy.start()
        waits = fetch(far[1:4], (kv, probs, q), own_sems.at[pl.ds(1, 3)])
        for copy in loaded[1][0] + loaded[2][0]:
            copy.start()
        late_waits = fetch(far[4:], (x, grad), own_sems.at[pl.ds(4, 2)])
        branch_wait[0]()
        loaded[0][1]()
        att[...] = dot(branch[...], matrix[:, width : 2 * width], NT).astype(LOW)
        outs = ((out, 0), (out, width), (out, 2 * width))
        for wait in waits:
            wait()
        attend_back(q, kv, kv, (0, 0, width), att, probs, outs, None)
        loaded[1][1]()
        loaded[2][1]()
        for wait in late_waits:
            wait()
        back, gain = norm_back(x[...], gains[1:2, :], dot(out[:, :width], matrix[:, :width], NT))
        total = grad[...] + back
        back_out[...] = total
        out[:, 3 * width :] = total.astype(LOW)
        gain_out[...] = gain
        mem_grad[...] = dot(out[:, width : 3 * width], matrix[:, 2 * width :], NT)

    return run(
        "cross_backward",
        kernel,
        [(place, pltpu.SMEM)]
        + vmem(gains)
        + [(array, pltpu.HBM) for array in (branch, kv, probs, q, after_self, grad)],
        [
            ((rows, 4 * width), LOW),
            ((mem_rows, width), F32, None),
            ((rows, width), F32),
            ((1, width), F32),
        ],
        [
            pltpu.VMEM((rows, width), LOW),
            pltpu.VMEM((rows, width), F32),
            pltpu.VMEM((rows, width), F32),
            pltpu.VMEM((rows, width), LOW),
            pltpu.VMEM((mem_rows, 2 * width), LOW),
            pltpu.VMEM((2 * PAIRS, mem_rows, rows), LOW),
            pltpu.VMEM((width, 4 * width), LOW),
            pltpu.VMEM((rows, width), LOW),
            pltpu.SemaphoreType.DMA((6,)),
        ]
        + weights.sems(3),
        flops=8 * rows * width * width,
        weights=[weights],
    )


def self_backward(place, grad, cross_grads, tokens, gains, cross_gain, hidden_gain, qk, v, probs, hot, weights, cut, block):
    rows, width = tokens.shape
    count = len(weights.arrays)
    heads = 2 * PAIRS
    groups = hot.shape[0]
    blocks = (width // block) // 2
    under = width // 2 * LANES // width

    def kernel(place, grad, before, tok, gains, cross_gain, hidden_gain, hot, qk_far, v_far, probs_far, *refs):
        pieces, refs = refs[:count], refs[count:]
        out_q, out_k, out_v, tok_grad, extra_keep, extra_send, qk, v, probs, matrix, att, dist, parts, own_sems, sems = refs
        ranges = [(cut + width, cut + 2 * width), (0, cut + width)]
        loaded = weights.load(place, pieces, [matrix], sems, ranges, True)
        for copy in loaded[0][0]:
            copy.start()
        waits = fetch((v_far, probs_far, qk_far), (v, probs, qk), own_sems)
        for copy in loaded[1][0]:
            copy.start()
        loaded[0][1]()
        att[...] = dot(before[:, 3 * width :], matrix[:, cut + width :], NT).astype(LOW)
        outs = ((out_q, 0), (out_k, 0), (out_v.at[:rows], 0))
        dist[...] = jnp.zeros_like(dist)
        for wait in waits:
            wait()
        attend_back(qk, qk, v, (0, width, 0), att, probs, outs, dist)
        loaded[1][1]()
        normed_grad = dot(out_q[...], matrix[:, :width], NT) + dot(out_k[...], matrix[:, width : 2 * width], NT)
        normed_grad = normed_grad + dot(out_v[:rows, :], matrix[:, cut : cut + width], NT)
        back, gain = norm_back(tok[...].astype(F32), gains[0:1, :], normed_grad)
        tok_grad[...] = grad[...] + back
        parts[...] = jnp.zeros_like(parts)
        parts[0:1, :] = gain
        parts[1:2, :] = cross_gain[...]
        parts[2:3, :] = hidden_gain[...]
        columns = parts[...].T
        table = None
        for group in range(groups):
            sums = lax.dot_general(
                hot[group].astype(F32), dist[...], NT, precision=lax.Precision.HIGHEST, preferred_element_type=F32
            )
            part = lax.dot_general(
                sums, head_lanes(group, heads), NN, precision=lax.Precision.HIGHEST, preferred_element_type=F32
            )
            table = part if table is None else table + part
        columns = columns + jnp.concatenate([table] * (2 * blocks), axis=0)
        split_rows(columns, place[2], extra_keep, extra_send)
        sending = extra_send[...].astype(F32).reshape(width // 2, LANES)
        for n in range(width // LANES):
            out_v[rows:, n * LANES : (n + 1) * LANES] = sending[n * under : (n + 1) * under].astype(LOW)

    halves = ((blocks, block, LANES), LOW)
    return run(
        "self_backward",
        kernel,
        [(place, pltpu.SMEM)]
        + vmem(grad, cross_grads, tokens, gains, cross_gain, hidden_gain, hot)
        + [(array, pltpu.HBM) for array in (qk, v, probs)],
        [((rows, width), LOW)] * 2 + [((rows + under, width), LOW), ((rows, width), F32, None), halves],
        [
            pltpu.VMEM(halves[0], LOW),
            pltpu.VMEM((rows, 2 * width), LOW),
            pltpu.VMEM((rows, width), LOW),
            pltpu.VMEM((heads, rows, rows), LOW),
            pltpu.VMEM((width, cut + 2 * width), LOW),
            pltpu.VMEM((rows, width), LOW),
            pltpu.VMEM((16, rows), F32),
            pltpu.VMEM((LANES, width), F32),
            pltpu.SemaphoreType.DMA((3,)),
        ]
        + weights.sems(2),
        flops=8 * rows * width * width,
        weights=[weights],
    )


def weight_grads(place, lefts, rights, sections, cols, extras=(), straight=()):
    sizes = grid_sizes()
    counts = (sizes["y"], sizes["x"])
    blocks = counts[0] * counts[1]
    nz = sizes["z"]
    left_count, right_count = len(lefts), len(rights)
    block = min(section[0][3] for section in (*sections, *straight))
    across_z = sum(section[3] * (section[0][3] // block) for section in straight)
    tokens = rights[0][0].shape[0]
    most = max(section[0][3] for section in (*sections, *straight))

    def kernel(place, *refs):
        refs = list(refs)
        left = [(refs.pop(0), refs.pop(0)) for _ in range(left_count)]
        right = [(refs.pop(0), refs.pop(0)) for _ in range(right_count)]
        extra = [refs.pop(0) for _ in extras]
        far_extra, gathered = refs.pop(), refs.pop()
        outs = (refs[: counts[0]], refs[counts[0] : counts[0] + counts[1]])
        out_z = refs[-1]

        def place_of(half, n):
            step, other = n // counts[1 - half], n % counts[1 - half]
            there = (place[half] + step) % counts[half]
            return there * counts[1] + other if half == 0 else other * counts[1] + there

        def products(section, order):
            (l, n, row, rows), r, column, width = section[:4]
            joined = rows % 16 == 0 and row % 16 == 0
            if joined:
                for k in range(blocks):
                    for side in range(2):
                        gathered[k * rows : (k + 1) * rows, side * tokens : (side + 1) * tokens] = left[l][side][
                            n, order(k), row : row + rows, :
                        ]
            for first in range(0, width, 768):
                size = min(768, width - first)
                own, far = (ref[:tokens, column + first : column + first + size] for ref in right[r])
                if joined:
                    total = dot(gathered[: blocks * rows, :tokens], own)
                    total = total + dot(gathered[: blocks * rows, tokens:], far)
                for k in range(blocks):
                    if joined:
                        yield first, size, k, total[k * rows : (k + 1) * rows]
                        continue
                    own_rows, far_rows = (ref[n, order(k), row : row + rows, :] for ref in left[l])
                    yield first, size, k, dot(own_rows, own) + dot(far_rows, far)

        for section in straight:
            for first, size, index, total in products(section, lambda k: k):
                for g in range(section[0][3] // block):
                    at = section[5] + g * section[3] + first
                    for z in range(nz):
                        row = g * block + z * block // nz
                        part = total[row : row + block // nz]
                        out_z[z, index, :, at : at + size] = part.astype(LOW)
        for section in sections:
            groups = section[0][3] // block
            half = section[4]
            for first, size, k, total in products(section, lambda k: place_of(half, k)):
                for g in range(groups):
                    at = section[5] + g * section[3] + first
                    part = total[g * block : (g + 1) * block].astype(LOW)
                    outs[half][k // counts[1 - half]][k % counts[1 - half], :, at : at + size] = part
        if extras:
            sent_ref = right[-1][1]
            under = sent_ref.shape[0] - tokens
            for n in range(blocks * block // under):
                far_extra[n * under : (n + 1) * under, :] = sent_ref[tokens:, n * LANES : (n + 1) * LANES].astype(F32)
        for k in range(blocks if extras else 0):
            index = place_of(0, k)
            start = pl.multiple_of(index * block, 8)
            both = extra[0][index].astype(F32) + far_extra[pl.ds(start, block), :]
            outs[0][k // counts[1]][k % counts[1], :, cols[0] - LANES :] = both.astype(LOW)

    arrays = [array for pair in lefts for array in pair] + [array for pair in rights for array in pair]
    outputs = []
    if sections:
        outputs += [((counts[1], block, cols[0]), LOW)] * counts[0]
        outputs += [((counts[0], block, cols[1]), LOW)] * counts[1]
    if straight:
        outputs.append(((nz, blocks, block // nz, across_z), LOW, None))
    return run(
        "weight_grads",
        kernel,
        [(place, pltpu.SMEM)] + vmem(*arrays, *extras),
        outputs,
        [pltpu.VMEM((blocks * most, 2 * tokens), LOW), pltpu.VMEM((blocks * block, LANES), F32)],
        flops=sum(4 * s[0][3] * blocks * rights[0][0].shape[0] * s[3] for s in (*sections, *straight)),
    )


def add_stage(place, firsts, seconds):
    sizes = grid_sizes()
    counts = (sizes["x"], sizes["y"])

    def kernel(place, *refs):
        refs = list(refs)
        halves = [[[refs.pop(0) for _ in parts] for parts in groups] for groups in (firsts, seconds)]
        outs = (refs[: counts[0]], refs[counts[0] :])
        for half in range(2):
            here = place[1 - half]
            for step in range(counts[half]):
                index = (here + step) % counts[half]
                at = 0
                for parts in halves[half]:
                    total = parts[0][index].astype(F32)
                    for part in parts[1:]:
                        total = total + part[index].astype(F32)
                    outs[half][step][:, at : at + total.shape[1]] = total.astype(LOW)
                    at += total.shape[1]

    outputs = []
    for groups, count in zip((firsts, seconds), counts):
        outputs += [((groups[0][0].shape[1], sum(parts[0].shape[2] for parts in groups)), LOW)] * count
    arrays = [part for groups in (firsts, seconds) for parts in groups for part in parts]
    return run("add_stage", kernel, [(place, pltpu.SMEM)] + vmem(*arrays), outputs)


def add_last(place, halves):
    count = grid_sizes()["z"]
    share = halves[0][0].shape[0] // count
    halves = [[part.reshape(count, share, part.shape[-1]) for part in parts] for parts in halves]
    cols = [parts[0].shape[-1] for parts in halves]

    def kernel(place, *refs):
        refs = list(refs)
        first = 0
        inputs = [[refs.pop(0) for _ in parts] for parts in halves]
        for parts, size in zip(inputs, cols):
            for step in range(count):
                index = (place[3] + step) % count
                total = parts[0][index].astype(F32)
                for part in parts[1:]:
                    total = total + part[index].astype(F32)
                refs[step][:, first : first + size] = total.astype(LOW)
            first += size

    return run(
        "add_last",
        kernel,
        [(place, pltpu.SMEM)] + vmem(*[part for parts in halves for part in parts]),
        [((share, sum(cols)), LOW)] * count,
    )


def mirrored(place, count):
    return place - place % count + count - 1 - place % count


def halving_order(place, count):
    order = [place]
    while len(order) < count:
        size = count // len(order)
        order += [mirrored(block, size) for block in order]
    return order


def halve(place, sides, count, first):
    have = sides[0][0].shape[0]
    half = have // 2
    cols = [parts[0].shape[2] for parts in sides]
    shape = (half, sides[0][0].shape[1], sum(cols))

    def kernel(place, *refs):
        refs = list(refs)
        inputs = [[refs.pop(0) for _ in parts] for parts in sides]
        order = halving_order(place[3], have) if first else range(have)
        for n in range(have):
            at = 0
            for parts, size in zip(inputs, cols):
                total = parts[0][order[n]].astype(F32)
                for part in parts[1:]:
                    total = total + part[order[n]].astype(F32)
                refs[n // half][n % half, :, at : at + size] = total.astype(LOW)
                at += size

    arrays = [part for parts in sides for part in parts]
    keep, send = run("halve", kernel, [(place, pltpu.SMEM)] + vmem(*arrays), [(shape, LOW), (shape, LOW)])
    pairs = [(i, mirrored(i, count)) for i in range(grid_sizes()["z"])]
    return keep, lax.ppermute(send, "narrow", pairs)


def by_blocks(parts):
    count = grid_sizes()["z"]
    return [part.reshape(count, part.shape[0] // count, part.shape[1]) for part in parts]


def finish_first(place, cross, early, order, early_cols, late, width, ff):
    share, cols = cross[0].shape[1:]
    cols = cols // 2
    side = width // 2
    folds = ff // width

    def kernel(place, near, far, kept, kept_far, other, order, c_query, c_key, c_value, c_output, s_output, h_in, h_out):
        total = near[0].astype(F32) + far[0].astype(F32)
        c_query[...] = total[:, :width]
        c_output[...] = total[:, width : 2 * width]
        s_output[:, :side] = total[:, 2 * width : 2 * width + side]
        c_key[...] = total[:, cols : cols + width]
        c_value[...] = total[:, cols + width : cols + 2 * width]
        s_output[:, side:] = total[:, cols + 2 * width : cols + 2 * width + side]
        x = place[1]
        first = kept[x].astype(F32) + kept_far[x].astype(F32) + other[...].astype(F32)
        for n in range(folds):
            h_out[n * share : (n + 1) * share, :] = first[:, early_cols + n * width : early_cols + (n + 1) * width]
        at = 2 * width + side
        pieces = [(first, 0, early_cols), (total, at, late), (total, cols + at, late)]
        start = 0
        for source, column, count in pieces:
            for n in range(0, count, CHUNK):
                part = source[:, column + n : column + n + CHUNK].astype(LOW)
                h_in[:, start : start + CHUNK] = dot(part, order[...], NT)
                start += CHUNK

    square = ((share, width), F32, None)
    return run(
        "finish_first",
        kernel,
        [(place, pltpu.SMEM)] + vmem(*cross, *early, order),
        [square] * 5 + [((share, ff), F32, None), ((share * folds, width), F32, None)],
    )


def finish_second(parts, width):
    share = parts[0].shape[0]
    side = width // 2
    cut = width + side + LANES

    def kernel(*refs):
        parts, (query, key, value, small) = refs[:-4], refs[-4:]
        total = parts[0][...].astype(F32)
        for part in parts[1:]:
            total = total + part[...].astype(F32)
        query[...] = total[:, :width]
        key[:, :side] = total[:, width : width + side]
        key[:, side:] = total[:, cut : cut + side]
        value[...] = total[:, cut + side :]
        small[...] = total[:, width + side : cut]

    square = ((share, width), F32, None)
    return run("finish_second", kernel, vmem(*parts), [square] * 3 + [((share, LANES), F32, None)])


def total_of(parts):
    return sum(part.astype(F32) for part in parts)


def scatter_along(parts, dim):
    count, here = grid_sizes()[dim], grid_place()[dim]
    kept = [lax.dynamic_index_in_dim(part, here, 0, keepdims=False) for part in parts]
    for step in range(1, count):
        there = (here + step) % count
        part = total_of([lax.dynamic_index_in_dim(part, there, 0, keepdims=False) for part in parts])
        kept.append(shifted(part.astype(LOW), dim, step))
    return kept


def sent(parts, dim):
    return [parts[0]] + [shifted(part, dim, step) for step, part in enumerate(parts) if step]


def segment_ids(length_row, slot_count):
    ends = jnp.cumsum(length_row).astype(jnp.int32)
    places = jnp.arange(slot_count, dtype=jnp.int32)
    return jnp.sum((places[:, None] >= ends[None, :]).astype(jnp.int32), axis=1).astype(jnp.int32)


def local(
    tokens, memory, doc_lengths, mem_lengths, pad_mask,
    self_query, self_key, self_value, self_output, self_gain, bias_table,
    cross_query, cross_key, cross_value, cross_output, cross_gain,
    hidden_in, hidden_out, hidden_gain, out_grad,
):
    sizes = grid_sizes()
    here = grid_place()
    ny, nx, nz = sizes["y"], sizes["x"], sizes["z"]
    rows, width = tokens.shape
    mem_rows = memory.shape[0]
    ff = hidden_in.shape[1]
    share = self_query.shape[0]
    ff_share = hidden_out.shape[0]
    table_rows, heads = bias_table.shape
    block = nz * share
    ff_block = nz * ff_share
    cut = 2 * width + LANES

    spots = []
    for step in range(4):
        y = (here["y"] + step // 2) % ny
        x = (here["x"] + step % 2) % nx
        for core in range(2):
            spots.append((y * nx + x) * 2 + (here["c"] + core) % 2)
    for n in range(4):
        spots += [2 * n + here["c"], 2 * n + 1 - here["c"]]
    place = jnp.stack([here["y"], here["x"], here["c"], here["z"]] + spots).astype(jnp.int32)
    pieces = in_pieces(block)
    half = block // 2

    hot = jnp.asarray(table_hot(rows, nz, share, table_rows)).astype(LOW)
    groups = hot.shape[0]
    folds = ff // width
    order = hidden_order(nz, share, folds)
    early_cols = int(ff * EARLY) // LANES * LANES if pieces else 0
    cross_squares = (cross_query, cross_output, cross_key, cross_value)
    if pieces:
        self_own = pack_first(
            (self_query, self_key, self_value, self_output), (self_gain, cross_gain, hidden_gain), bias_table, cut
        )
        rest, in_own = pack_rest(cross_squares, hidden_in, hidden_out, order, early_cols)
    else:
        table = jnp.pad(bias_table, ((0, groups * share - table_rows), (0, 0)))
        table = jnp.transpose(table.reshape(groups, share, heads), (1, 0, 2)).reshape(share, groups * heads)
        extra = jnp.concatenate(
            [
                self_gain[:, None],
                cross_gain[:, None],
                hidden_gain[:, None],
                jnp.zeros((share, TABLE_LANE - 3), LOW),
                table,
                jnp.zeros((share, LANES - TABLE_LANE - groups * heads), LOW),
            ],
            axis=1,
        )
        self_own = jnp.concatenate([self_query, self_key, extra, self_value, self_output], axis=1)
        wide_out = jnp.transpose(hidden_out.reshape(folds, share, width), (1, 0, 2)).reshape(share, ff)
        rest = jnp.concatenate([*cross_squares, reorder(hidden_in, order, NN, LOW), wide_out], axis=1)
    self_others = received(self_own, "z")
    self_z = in_order(self_own, self_others, "z", 0).reshape(block, -1)
    rest = after(rest, self_others[0])
    rest = lax.all_gather(rest, "narrow", axis=0, tiled=True)

    seg_ids = segment_ids(doc_lengths[0], rows)
    mem_ids = segment_ids(mem_lengths[0], mem_rows)
    if pieces:
        in_x, in_y = shifted(in_own, "x", 1), shifted(in_own, "y", 1)
        in_xy = shifted(in_x, "y", 1)
        in_all = in_order(
            in_order(in_own, [in_x], "x", 0), [in_order(in_y, [in_xy], "x", 0)], "y", 0
        ).reshape(4, share, early_cols)
        near, twins, corner = gather_pieces(after(self_z, in_xy))
        in_all = lax.all_gather(after(in_all, rest, *corner), "narrow", axis=0, tiled=False)
        w_self = Weights(
            pairs(near, twins) + with_twins(corner),
            near_spots(range(6), block, 0, 0, 0, cut + 2 * width)
            + half_spots(range(6, 10), block, 0, 0, 0, cut + 2 * width),
        )
        rest_near = from_neighbours(after(rest, *twins, *corner))
    else:
        w_self = Weights([gather_whole(self_z)], [(0, 0, 0, None, 0, 0, width, 0, 0, cut + 2 * width)])

    og_far = swapped(out_grad)
    qk, v, self_probs, after_self, s_keep, s_send, gains = self_forward(
        place, after(tokens, og_far), seg_ids[:, None], seg_ids[None], pad_mask[:, None], hot, w_self, cut, block
    )
    s_far = swapped(s_send)
    if pieces:
        twin = swapped(rest_near[0])
        rest_x, rest_y = (after(array, after_self, s_far, twin) for array in rest_near[1:])
        corner = from_corner(rest_x[:half, :ff], rest_y[half:, :ff])
        upper, lower = rest_x[:half, ff:], rest_y[half:, ff:]
        in_all = jnp.transpose(after(in_all, twin), (1, 0, 2, 3)).reshape(4 * block, early_cols)
        corner = [after(array, upper, lower, in_all) for array in corner]
        rest_arrays = [rest_near[0], twin] + with_twins([rest_x, rest_y])
        w_cross = Weights(
            rest_arrays + with_twins(corner),
            near_spots(range(6), block, 0, 0, 0, ff) + half_spots(range(6, 10), block, 0, 0, 0, ff),
        )
        last = from_corner(upper, lower)
        cross_in = after(after_self, s_far, upper, lower)
    else:
        rest = gather_whole(rest)
        w_cross = Weights([rest], [(0, 0, 0, None, 0, 0, width, 0, 0, ff)])
        m_in = rest[:, ff : 2 * ff]
        m_out = jnp.transpose(rest[:, 2 * ff :].reshape(-1, block, folds, width), (0, 2, 1, 3)).reshape(ff, width)
        cross_in = after_self
    q, kv, cross_probs, after_cross, c_keep, c_send = cross_forward(
        place, cross_in, memory, gains, mem_ids[:, None], seg_ids[None], w_cross, block
    )
    c_far = swapped(c_send)
    if pieces:
        late_cols = ff - early_cols
        spots = folded_spots(near_spots(range(6), block, 0, 1, 0, 0), block, ff + late_cols, folds, width, 1)
        if late_cols:
            spots += near_spots(range(6), block, ff, 0, early_cols, late_cols)
        early = list(rest_arrays)
        for twin, array in enumerate((in_all, swapped(in_all))):
            spots += [
                (6 + twin, n * block, 0, ORDER_AT + 2 * n + twin, block, 0, block, 0, 0, early_cols) for n in range(4)
            ]
            early.append(array)
        m_in, m_out = hidden_early(after(place, after_cross), Weights(early, spots), width, ff)
        last = with_twins([after(array, after_cross) for array in last])
        spots = folded_spots(half_spots(range(4), block, 0, 1, 0, 0), block, late_cols, folds, width, 1)
        if late_cols:
            spots += half_spots(range(4), block, 0, 0, early_cols, late_cols)
        w_last = Weights(last, spots)
    else:
        w_last = Weights([], [])

    act, gu, h_keep, h_send, m_in, m_out = hidden_first(
        place, after(after_cross, c_far), out_grad, gains, m_in, m_out, w_last, block
    )
    h_far, gu_far = swapped(h_send), swapped(gu)
    layer_out, grad, branch, hidden_gain_part = hidden_second(after_cross, out_grad, gains, act, gu, m_in, m_out)
    h_keep = after(h_keep, grad)
    side = width // 2
    early_grads = int(ff * EARLY_GRAD) // LANES * LANES if pieces else 0
    late = (ff - early_grads) // 2
    ff_cols = late + (0 if pieces else folds * side)
    ff_sections = [((0, 0, 0, block), 0, early_grads + n * late, late, n, 0) for n in range(2)]
    straight = []
    if pieces:
        straight = [
            ((0, 0, 0, block), 0, 0, early_grads, 2, 0),
            ((0, 0, block, ff_block), 1, 0, width, 2, early_grads),
        ]
    else:
        ff_sections += [((0, 0, block, ff_block), 1, n * side, side, n, late) for n in range(2)]
    ff_parts = weight_grads(
        place,
        [(h_keep[None], h_far[None])],
        [(gu, gu_far), (out_grad, og_far)],
        ff_sections,
        (ff_cols, ff_cols),
        straight=straight,
    )
    if pieces:
        *ff_parts, in_early = ff_parts
        in_early = lax.psum_scatter(in_early, "narrow", scatter_dimension=0, tiled=True)
    grad = after(grad, *ff_parts)
    ff_first, ff_second = sent(ff_parts[:ny], "y"), sent(ff_parts[ny:], "x")
    cross_cols = 2 * width + side + ff_cols

    branch_far = swapped(branch)
    cross_grads, memory_grad, grad, cross_gain_part = cross_backward(
        place, grad, after(branch, branch_far), after_self, gains, q, kv, cross_probs, w_cross
    )
    cross_parts = weight_grads(
        place,
        [(c_keep, c_far), (s_keep, s_far)],
        [(cross_grads, swapped(after(cross_grads, *ff_first, *ff_second))), (branch, branch_far)],
        [
            ((0, 0, 0, block), 0, 0, width, 0, 0),
            ((0, 1, 0, block), 1, 0, width, 0, width),
            ((1, 1, 0, block), 0, 3 * width, side, 0, 2 * width),
            ((0, 2, 0, block), 0, width, 2 * width, 1, 0),
            ((1, 1, 0, block), 0, 3 * width + side, side, 1, 2 * width),
        ],
        (2 * width + side, 2 * width + side),
    )
    cross_first, cross_second = cross_parts[:ny], cross_parts[ny:]
    cross_first, cross_second = sent(cross_first, "y"), sent(cross_second, "x")

    grad = after(grad, *cross_parts)
    self_dq, self_dk, self_dv, tokens_grad, extra_keep = self_backward(
        place, grad, cross_grads, tokens, gains, cross_gain_part, hidden_gain_part, qk, v,
        self_probs, hot, w_self, cut, block,
    )
    self_parts = weight_grads(
        place,
        [(s_keep, s_far)],
        [(self_dq, swapped(self_dq)), (self_dk, swapped(self_dk)), (self_dv, swapped(self_dv))],
        [
            ((0, 0, 0, block), 0, 0, width, 0, 0),
            ((0, 0, 0, block), 1, 0, side, 0, width),
            ((0, 0, 0, block), 1, side, side, 1, 0),
            ((0, 0, 0, block), 2, 0, width, 1, side),
        ],
        (width + side + LANES, width + side),
        (extra_keep,),
    )
    self_first, self_second = self_parts[:ny], self_parts[ny:]
    self_first, self_second = sent(self_first, "y"), sent(self_second, "x")
    cross_first = [after(cross_first[0], *self_parts)] + cross_first[1:]
    cross_parts = add_stage(place, [cross_first, ff_first], [cross_second, ff_second])
    cross_first, cross_second = cross_parts[:nx], cross_parts[nx:]
    cross_first, cross_second = sent(cross_first, "x"), sent(cross_second, "y")
    cross_parts = halve(place, [by_blocks(cross_first), by_blocks(cross_second)], 2, True)
    self_first = [after(self_first[0], cross_parts[0])] + self_first[1:]
    self_parts = add_stage(place, [self_first], [self_second])
    self_first, self_second = self_parts[:nx], self_parts[nx:]
    self_first, self_second = sent(self_first, "x"), sent(self_second, "y")
    if pieces:
        in_early = after(in_early, cross_parts[0]).reshape(ny, nx, share, early_grads + folds * width)
        in_early = scatter_along([in_early], "y")
    count = 2
    while count < nz:
        count *= 2
        earlier = (*self_parts, *in_early) if pieces else self_parts
        cross_parts = halve(place, [[after(part, *earlier) for part in cross_parts]], count, False)
    self_first = [after(self_first[0], cross_parts[0])] + self_first[1:]
    self_sums = add_last(place, (self_first, self_second))
    self_parts = sent(self_sums, "z")
    if pieces:
        in_early = [after(part, cross_parts[0]) for part in in_early]
        there = total_of([lax.dynamic_index_in_dim(part, 1 - here["x"], 0, keepdims=False) for part in in_early])
        in_early.append(shifted(there.astype(LOW), "x", 1))
        *cross_grads, in_grad, out_part = finish_first(
            place, cross_parts, in_early, order, early_grads, late, width, ff
        )
        self_parts = [after(self_parts[0], in_grad)] + self_parts[1:]
    else:
        cross_total = total_of([part[0] for part in cross_parts])
        at = 2 * width + side
        halves = [cross_total[:, n : n + cross_cols] for n in (0, cross_cols)]
        in_grad = jnp.concatenate([part[:, at : at + late].astype(LOW) for part in halves], axis=1)
        in_grad = reorder(in_grad, order, NT, F32)
        out_part = jnp.concatenate([part[:, at + late :].reshape(share, folds, side) for part in halves], axis=2)
        out_part = jnp.transpose(out_part, (1, 0, 2)).reshape(ff_share, width)
        cross_grads = [
            halves[0][:, :width],
            halves[1][:, :width],
            halves[1][:, width : 2 * width],
            halves[0][:, width : 2 * width],
            jnp.concatenate([part[:, 2 * width : at] for part in halves], axis=1),
        ]
    query_grad, key_grad, value_grad, last = finish_second(self_parts, width)
    table_grad = last[:, TABLE_LANE : TABLE_LANE + groups * heads].reshape(share, groups, heads)
    table_grad = jnp.transpose(table_grad, (1, 0, 2)).reshape(groups * share, heads)[:table_rows]
    return (
        layer_out,
        tokens_grad,
        memory_grad,
        query_grad,
        key_grad,
        value_grad,
        cross_grads[4],
        last[:, 0],
        table_grad,
        *cross_grads[:4],
        last[:, 1],
        in_grad,
        out_part,
        last[:, 2],
    )


def solution(mesh):
    rows = P(("wide", "narrow"), None)
    line = P(("wide", "narrow"))
    table = P("narrow", None)
    return jax.shard_map(
        local,
        mesh=mesh,
        in_specs=(
            (rows,) * 4 + (line,) + (rows,) * 4 + (line, table) + (rows,) * 4 + (line,) + (rows,) * 2 + (line, rows)
        ),
        out_specs=(rows,) * 7 + (line, table) + (rows,) * 4 + (line,) + (rows,) * 2 + (line,),
        check_vma=False,
    )
```

```python
import math

import jax
import jax.numpy as jnp
import numpy as np
from jax import lax
from jax.experimental import pallas as pl
from jax.experimental.pallas import tpu as pltpu
from jax.sharding import PartitionSpec as P

BUCKETS = 32
REACH = 128
LOW = jnp.bfloat16
F32 = jnp.float32
NN = (((1,), (0,)), ((), ()))
NT = (((1,), (1,)), ((), ()))
TN = (((0,), (0,)), ((), ()))
PAIRS = 6
LANES = 128
TABLE_LANE = 16
CHUNK = 384
MiB = 1024 * 1024
FIRST_AT = 4
ORDER_AT = 12
EARLY = 0.5
EARLY_GRAD = 0.25


def bucket_edges(bucket_count, far_reach):
    exact_span = bucket_count // 2
    edge_list = list(range(1, exact_span + 1))
    for target in range(exact_span + 1, bucket_count):
        distance = exact_span
        while (
            exact_span
            + int(
                math.log(distance / exact_span)
                / math.log(far_reach / exact_span)
                * (bucket_count - exact_span)
            )
            < target
        ):
            distance += 1
        edge_list.append(distance)
    return edge_list


def distance_one_hot(rows):
    edges = np.array(bucket_edges(BUCKETS, REACH))
    buckets = (np.arange(rows)[:, None] >= edges[None, :]).sum(axis=1)
    return (np.arange(BUCKETS)[:, None] == buckets[None, :]).astype(np.float32)


def table_hot(rows, blocks, share, table_rows):
    one_hot = distance_one_hot(rows)
    groups = -(-table_rows // share)
    hot = np.zeros((groups, blocks * share, rows), np.float32)
    for block in range(blocks):
        for row in range(table_rows):
            hot[row // share, block * share + row % share] = one_hot[block * table_rows + row]
    return hot


def grid_sizes():
    wide = lax.axis_size("wide")
    inner = wide // 2
    across = 1
    while across * across < inner:
        across *= 2
    return {"y": inner // across, "x": across, "c": 2, "z": lax.axis_size("narrow")}


def grid_place():
    sizes = grid_sizes()
    wide = lax.axis_index("wide")
    return {
        "y": wide // (2 * sizes["x"]),
        "x": (wide // 2) % sizes["x"],
        "c": wide % 2,
        "z": lax.axis_index("narrow"),
    }


def shifted(array, dim, step):
    sizes = grid_sizes()
    count = sizes[dim]
    if dim == "z":
        return lax.ppermute(array, "narrow", [(i, (i + step) % count) for i in range(count)])
    stride = {"y": 2 * sizes["x"], "x": 2, "c": 1}[dim]
    pairs = []
    for source in range(lax.axis_size("wide")):
        place = (source // stride) % count
        pairs.append((source, source + ((place + step) % count - place) * stride))
    return lax.ppermute(array, "wide", pairs)


def after(value, *earlier):
    return lax.optimization_barrier((value, *earlier))[0]


def received(block, dim):
    count = grid_sizes()[dim]
    return [shifted(block, dim, count - step) for step in range(1, count)]


def swapped(array):
    return shifted(array, "c", 1)


def in_order(block, others, dim, axis):
    here = grid_place()[dim]
    cyclic = [block] + others
    count = len(cyclic)
    ordered = []
    for place in range(count):
        picked = cyclic[0]
        for step in range(1, count):
            picked = jnp.where((here + step) % count == place, cyclic[step], picked)
        ordered.append(picked)
    return jnp.stack(ordered, axis)


class Weights:
    def __init__(self, arrays, spots):
        self.arrays = arrays
        self.spots = spots

    def load(self, place, refs, matrices, sems, ranges=None, lazy=False):
        waits = []
        count = 0
        for low, high in ranges or [(0, None)]:
            copies = []
            for source, first, column, at, block, row, rows, matrix, there, cols in self.spots:
                start = row if at is None else pl.multiple_of(place[at] * block, block) + row
                from_column, to_column, size = column + low, there + low, (high or cols) - low
                copies.append(
                    pltpu.make_async_copy(
                        refs[source].at[pl.ds(first, rows), pl.ds(from_column, size)],
                        matrices[matrix].at[pl.ds(start, rows), pl.ds(to_column, size)],
                        sems.at[count],
                    )
                )
                count += 1
            waits.append((copies, lambda copies=copies: [copy.wait() for copy in copies]))
            if not lazy:
                for copy in copies:
                    copy.start()
        if lazy:
            return waits
        return [wait for _, wait in waits]

    def sems(self, ranges=1):
        return [pltpu.SemaphoreType.DMA((max(len(self.spots) * ranges, 1),))]


def fetch(sources, targets, sems):
    copies = [pltpu.make_async_copy(a, b, sems.at[n]) for n, (a, b) in enumerate(zip(sources, targets))]
    for copy in copies:
        copy.start()
    return [copy.wait for copy in copies]


def in_pieces(block):
    sizes = grid_sizes()
    return sizes["y"] == 2 and sizes["x"] == 2 and block % 32 == 0


def from_neighbours(block):
    return [block, shifted(block, "x", 1), shifted(block, "y", 1)]


def from_corner(upper, lower):
    return [shifted(upper, "y", 1), shifted(lower, "x", 1)]


def gather_pieces(block, *earlier, near=None):
    near = near or from_neighbours(block)
    half = block.shape[0] // 2
    twins = [swapped(near[0])]
    near_x, near_y = (after(array, twins[0], *earlier) for array in near[1:])
    corner = [shifted(near_x[:half], "y", 1), shifted(near_y[half:], "x", 1)]
    twins += [swapped(near_x), swapped(near_y)]
    return near, twins, corner


def pairs(near, twins):
    return [array for pair in zip(near, twins) for array in pair]


def gather_whole(block):
    block = in_order(block, received(block, "x"), "x", 0)
    block = in_order(block, received(block, "y"), "y", 0)
    block = in_order(block, received(block, "c"), "c", 2)
    return block.reshape(-1, block.shape[-1])


def near_spots(sources, block, column, matrix, there, cols):
    return [
        (source, 0, column, FIRST_AT + n, block, 0, block, matrix, there, cols) for n, source in enumerate(sources)
    ]


def half_spots(sources, block, column, matrix, there, cols):
    half = block // 2
    return [
        (source, 0, column, FIRST_AT + 6 + n % 2, block, (n // 2) * half, half, matrix, there, cols)
        for n, source in enumerate(sources)
    ]


def folded_spots(spots, block, column, groups, width, matrix):
    return [
        (source, first, column + g * width, at, groups * block, g * block + row, rows, matrix, 0, width)
        for source, first, _, at, _, row, rows, *_ in spots
        for g in range(groups)
    ]


def with_twins(arrays):
    return [array for own in arrays for array in (own, swapped(own))]


def run(name, kernel, inputs, outputs, scratch=(), flops=0, weights=(), aliases=()):
    inputs = list(inputs)
    for group in weights:
        inputs += [(array, pltpu.HBM) for array in group.arrays]
    size = sum(math.prod(array.shape) * array.dtype.itemsize for array, _ in inputs)
    arrays = [
        array if space == pltpu.SMEM else pltpu.with_memory_space_constraint(array, space)
        for array, space in inputs
    ]
    shapes = [
        jax.ShapeDtypeStruct(*output[:2]) if len(output) > 2 else pltpu.VMEM(*output) for output in outputs
    ]
    return pl.pallas_call(
        kernel,
        name=name,
        in_specs=[pl.BlockSpec(memory_space=space) for _, space in inputs],
        out_specs=[
            pl.BlockSpec(memory_space=pltpu.HBM if output[2:] == (pltpu.HBM,) else pltpu.VMEM) for output in outputs
        ],
        out_shape=shapes,
        scratch_shapes=list(scratch),
        input_output_aliases=dict(aliases),
        compiler_params=pltpu.CompilerParams(vmem_limit_bytes=24 * MiB),
        cost_estimate=pl.CostEstimate(flops=flops, bytes_accessed=size // 2, transcendentals=0),
    )(*arrays)


def vmem(*arrays):
    return [(array, pltpu.VMEM) for array in arrays]


def dot(left, right, dims=NN):
    return lax.dot_general(left, right, dims, preferred_element_type=F32)


def scale_of(values):
    return lax.rsqrt(jnp.mean(values * values, axis=-1, keepdims=True) + 1e-06)


def norm_back(values, gain, grad):
    scale = scale_of(values)
    weighted = grad * gain
    middle = jnp.mean(values * weighted, axis=-1, keepdims=True)
    return (
        scale * weighted - values * (scale * scale * scale * middle),
        jnp.sum(grad * values * scale, axis=0, keepdims=True),
    )


def split_rows(matrix, core, keep, send):
    count, rows, _ = keep.shape
    if rows % 16:
        matrix = matrix.astype(F32)
    pieces = [matrix[n * rows : (n + 1) * rows].astype(keep.dtype) for n in range(2 * count)]

    @pl.when(core == 0)
    def _():
        for n in range(count):
            keep[n] = pieces[2 * n]
            send[n] = pieces[2 * n + 1]

    @pl.when(core == 1)
    def _():
        for n in range(count):
            keep[n] = pieces[2 * n + 1]
            send[n] = pieces[2 * n]


def lanes_of(pair, column=0):
    return pl.ds(pl.multiple_of(column + pair * LANES, LANES), LANES)


def head_mask(rows, head):
    lanes = lax.broadcasted_iota(jnp.int32, (rows, LANES), 1)
    return (lanes >= 64) if head else (lanes < 64)


def attend(q_ref, k_ref, v_ref, columns, allowed, bias, prob_ref, out_ref):
    rows = q_ref.shape[0]
    cols = k_ref.shape[0]

    def step(pair, carry):
        q = q_ref[:, lanes_of(pair, columns[0])]
        k = k_ref[:, lanes_of(pair, columns[1])]
        v_turned = v_ref[:, lanes_of(pair, columns[2])].T
        for head in range(2):
            mine = head_mask(rows, head)
            scores = dot(k, jnp.where(mine, q, jnp.zeros_like(q)), NT)
            if bias is not None:
                row = jnp.broadcast_to(bias[pl.ds(2 * pair + head, 1), :], (cols, rows))
                scores = scores + pltpu.roll(row, 0, 1, stride=1, stride_axis=0)
            scores = jnp.where(allowed[...] > 0, scores, -1e9)
            weights = jnp.exp(scores - jnp.max(scores, axis=0, keepdims=True))
            probs = (weights * (1.0 / jnp.sum(weights, axis=0, keepdims=True))).astype(LOW)
            prob_ref[2 * pair + head] = probs
            part = dot(v_turned[head * 64 : head * 64 + 64], probs)
            first = pl.multiple_of(pair * LANES + head * 64, 64)
            out_ref[pl.ds(first, 64), :] = part.astype(LOW)
        return carry

    lax.fori_loop(0, PAIRS, step, 0)


def attend_back(q_ref, k_ref, v_ref, columns, g_ref, prob_ref, outs, dist_ref):
    rows = q_ref.shape[0]
    cols = k_ref.shape[0]

    def step(pair, carry):
        q = q_ref[:, lanes_of(pair, columns[0])]
        k = k_ref[:, lanes_of(pair, columns[1])]
        v = v_ref[:, lanes_of(pair, columns[2])]
        g = g_ref[:, lanes_of(pair)]
        k_turned = k.T
        if dist_ref is not None:
            i = lax.broadcasted_iota(jnp.int32, (cols, cols), 0)
            j = lax.broadcasted_iota(jnp.int32, (cols, cols), 1)
            flip = (i + j == cols - 1).astype(LOW)
        grads = None
        query_parts = []
        for head in range(2):
            mine = head_mask(cols, head)
            low_probs = prob_ref[2 * pair + head]
            probs = low_probs.astype(F32)
            moved = probs * dot(v, jnp.where(head_mask(rows, head), g, jnp.zeros_like(g)), NT)
            low_scores = (moved - probs * jnp.sum(moved, axis=0, keepdims=True)).astype(LOW)
            if dist_ref is not None:
                lined = pltpu.roll(dot(flip, low_scores), 1, 1, stride=1, stride_axis=0)
                dist_ref[pl.ds(2 * pair + head, 1), :] = jnp.sum(lined, axis=0, keepdims=True)
            query_parts.append(dot(k_turned[head * 64 : head * 64 + 64], low_scores))
            new = (dot(low_scores, q), dot(low_probs, g))
            grads = new if head == 0 else tuple(jnp.where(mine, b, a) for a, b in zip(grads, new))
        query_grad = jnp.concatenate(query_parts, axis=0).T
        for (ref, column), grad in zip(outs, (query_grad, *grads)):
            ref[:, lanes_of(pair, column)] = grad.astype(LOW)
        return carry

    lax.fori_loop(0, PAIRS, step, 0)


def head_lanes(group, heads):
    head = lax.broadcasted_iota(jnp.int32, (16, LANES), 0)
    lane = lax.broadcasted_iota(jnp.int32, (16, LANES), 1)
    return ((head < heads) & (lane == TABLE_LANE + group * heads + head)).astype(F32)


def self_forward(place, tokens, row_ids, col_ids, pad, hot, weights, cut, block):
    rows, width = tokens.shape
    count = len(weights.arrays)
    heads = 2 * PAIRS
    groups = hot.shape[0]
    blocks = (width // block) // 2

    def kernel(place, tok, row_ids, col_ids, pad, hot, *refs):
        pieces, refs = refs[:count], refs[count:]
        qk, v, probs, out, keep, send, gains, matrix, allowed, bias, att, sems = refs
        wait, wait_late = weights.load(place, pieces, [matrix], sems, [(0, cut), (cut, cut + 2 * width)])
        i = lax.broadcasted_iota(jnp.int32, (rows, rows), 0)
        j = lax.broadcasted_iota(jnp.int32, (rows, rows), 1)
        same = (row_ids[...] == col_ids[...]) & (i <= j) & ((pad[...] == 1) | (i == j))
        allowed[...] = same.astype(F32)
        residual = tok[...].astype(F32)
        scaled = residual * scale_of(residual)
        wait()
        extra = matrix[:, 2 * width : cut].astype(F32)
        gains[...] = extra.T[:8]
        normed = (scaled * gains[0:1, :]).astype(LOW)
        total = None
        for group in range(groups):
            table = dot(extra[: hot.shape[1]], head_lanes(group, heads), NT)
            part = dot(table.astype(LOW), hot[group], TN)
            total = part if total is None else total + part
        bias[...] = total
        split_rows(normed.T, place[2], keep.at[0], send.at[0])
        qk[...] = dot(normed, matrix[:, : 2 * width]).astype(LOW)
        wait_late()
        v[...] = dot(normed, matrix[:, cut : cut + width]).astype(LOW)
        attend(qk, qk, v, (0, width, 0), allowed, bias, probs, att)
        attended = att[...]
        split_rows(attended, place[2], keep.at[1], send.at[1])
        out[...] = residual + dot(attended, matrix[:, cut + width :], TN)

    halves = ((2, blocks, block, rows), LOW)
    return run(
        "self_forward",
        kernel,
        [(place, pltpu.SMEM)] + vmem(tokens, row_ids, col_ids, pad, hot),
        [
            ((rows, 2 * width), LOW, None),
            ((rows, width), LOW, None),
            ((heads, rows, rows), LOW, None),
            ((rows, width), F32, None),
            halves,
            halves,
            ((8, width), F32),
        ],
        [
            pltpu.VMEM((width, cut + 2 * width), LOW),
            pltpu.VMEM((rows, rows), F32),
            pltpu.VMEM((16, rows), F32),
            pltpu.VMEM((width, rows), LOW),
        ]
        + weights.sems(2),
        flops=8 * rows * width * width,
        weights=[weights],
    )


def cross_forward(place, after_self, memory, gains, row_ids, col_ids, weights, block):
    rows, width = after_self.shape
    mem_rows = memory.shape[0]
    count = len(weights.arrays)
    blocks = (width // block) // 2

    def kernel(place, x, mem, gains, row_ids, col_ids, *refs):
        pieces, refs = refs[:count], refs[count:]
        q_far, kv_far, probs_far, out, keep, send, q, kv, probs, matrix, allowed, att, out_sems, sems = refs
        wait, wait_late = weights.load(place, pieces, [matrix], sems, [(2 * width, 4 * width), (0, 2 * width)])
        allowed[...] = (row_ids[...] == col_ids[...]).astype(F32)
        residual = x[...]
        normed = (residual * scale_of(residual) * gains[1:2, :]).astype(LOW)
        split_rows(normed.T, place[2], keep.at[0], send.at[0])
        split_rows(mem[...].T, place[2], keep.at[2], send.at[2])
        wait()
        kv[...] = dot(mem[...], matrix[:, 2 * width :]).astype(LOW)
        wait_late()
        q[...] = dot(normed, matrix[:, :width]).astype(LOW)
        waits = fetch((q, kv), (q_far, kv_far), out_sems)
        attend(q, kv, kv, (0, 0, width), allowed, None, probs, att)
        waits += fetch((probs,), (probs_far,), out_sems.at[pl.ds(2, 1)])
        attended = att[...]
        split_rows(attended, place[2], keep.at[1], send.at[1])
        out[...] = residual + dot(attended, matrix[:, width : 2 * width], TN)
        for copied in waits:
            copied()

    halves = ((3, blocks, block, rows), LOW)
    return run(
        "cross_forward",
        kernel,
        [(place, pltpu.SMEM)] + vmem(after_self, memory, gains, row_ids, col_ids),
        [
            ((rows, width), LOW, pltpu.HBM),
            ((mem_rows, 2 * width), LOW, pltpu.HBM),
            ((2 * PAIRS, mem_rows, rows), LOW, pltpu.HBM),
            ((rows, width), F32),
            halves,
            halves,
        ],
        [
            pltpu.VMEM((rows, width), LOW),
            pltpu.VMEM((mem_rows, 2 * width), LOW),
            pltpu.VMEM((2 * PAIRS, mem_rows, rows), LOW),
            pltpu.VMEM((width, 4 * width), LOW),
            pltpu.VMEM((mem_rows, rows), F32),
            pltpu.VMEM((width, rows), LOW),
            pltpu.SemaphoreType.DMA((3,)),
        ]
        + weights.sems(2),
        flops=8 * rows * width * width,
        weights=[weights],
    )


def hidden_order(nz, share, groups):
    units = np.arange(CHUNK).reshape(-1, nz, groups, share)
    order = np.transpose(units, (0, 2, 1, 3)).reshape(-1)
    matrix = np.zeros((CHUNK, CHUNK), np.float32)
    matrix[order, np.arange(CHUNK)] = 1.0
    return jnp.asarray(matrix).astype(LOW)


def reorder(array, order, dims, kind):
    def kernel(array, order, out):
        for start in range(0, array.shape[1], CHUNK):
            out[:, start : start + CHUNK] = dot(array[:, start : start + CHUNK], order[...], dims).astype(kind)

    return run("reorder", kernel, vmem(array, order), [(array.shape, kind, None)])[0]


def hidden_early(place, weights, width, ff):
    count = len(weights.arrays)

    def kernel(place, *refs):
        weights.load(place, refs[:count], refs[count : count + 2], refs[count + 2])[0]()

    return run(
        "hidden_early",
        kernel,
        [(place, pltpu.SMEM)],
        [((width, ff), LOW), ((ff, width), LOW)],
        weights.sems(),
        weights=[weights],
    )


def fetching(kernel, arrays):
    count = len(arrays)

    def fetched(*refs):
        sources, outs, refs = refs[:count], refs[count : -count - 1], refs[-count - 1 :]
        for wait in fetch(sources, refs[:-1], refs[-1]):
            wait()
        kernel(*refs[:-1], *outs)

    scratch = [pltpu.VMEM(array.shape, array.dtype) for array in arrays]
    return fetched, scratch + [pltpu.SemaphoreType.DMA((count,))]


def pack_first(squares, gains, table, cut):
    share, width = squares[0].shape
    table_rows, heads = table.shape

    def kernel(query, key, value, output, *refs):
        gains, (table, out, lanes) = refs[:3], refs[3:]
        lanes[...] = jnp.zeros_like(lanes)
        rows = jnp.concatenate([gain[...].astype(F32) for gain in gains] + [jnp.zeros((5, share), F32)], axis=0)
        lanes[:, :8] = rows.T
        for group in range(-(-table_rows // share)):
            part = table[...].astype(F32)[group * share : (group + 1) * share]
            at = TABLE_LANE + group * heads
            lanes[: part.shape[0], at : at + heads] = part
        out[:, :width] = query[...]
        out[:, width : 2 * width] = key[...]
        out[:, 2 * width : cut] = lanes[...].astype(LOW)
        out[:, cut : cut + width] = value[...]
        out[:, cut + width :] = output[...]

    arrays = [*squares, *[gain.reshape(1, share) for gain in gains], table]
    fetched, scratch = fetching(kernel, arrays)
    return run(
        "pack_first",
        fetched,
        [(array, pltpu.HBM) for array in arrays],
        [((share, cut + 2 * width), LOW)],
        [pltpu.VMEM((share, LANES), F32), *scratch],
    )[0]


def pack_rest(squares, hidden_in, hidden_out, order, early_cols):
    share, width = squares[0].shape
    ff = hidden_in.shape[1]
    folds = ff // width
    late = ff - early_cols

    def kernel(*refs):
        squares, (h_in, h_out, order, rest, early) = refs[:4], refs[4:]
        for start in range(0, ff, CHUNK):
            part = dot(h_in[:, start : start + CHUNK], order[...]).astype(LOW)
            if start < early_cols:
                early[:, start : start + CHUNK] = part
            else:
                at = 4 * width + start - early_cols
                rest[:, at : at + CHUNK] = part
        for n, square in enumerate(squares):
            rest[:, n * width : (n + 1) * width] = square[...]
        rows = h_out[...].astype(F32)
        for n in range(folds):
            at = 4 * width + late + n * width
            rest[:, at : at + width] = rows[n * share : (n + 1) * share].astype(LOW)

    arrays = [*squares, hidden_in, hidden_out, order]
    fetched, scratch = fetching(kernel, arrays)
    return run(
        "pack_rest",
        fetched,
        [(array, pltpu.HBM) for array in arrays],
        [((share, 4 * width + late + ff), LOW, None), ((share, early_cols), LOW, None)],
        scratch,
    )


def cut_halves(upper, lower, half, column):
    cols = upper.shape[1]

    def kernel(upper, lower, *refs):
        outs, sems = refs[:4], refs[4]
        top, bottom = upper.at[pl.ds(0, half)], lower.at[pl.ds(half, half)]
        sources = [
            ref.at[:, pl.ds(first, size)]
            for first, size in ((0, column), (column, cols - column))
            for ref in (top, bottom)
        ]
        for wait in fetch(sources, outs, sems):
            wait()

    return run(
        "cut_halves",
        kernel,
        [(upper, pltpu.HBM), (lower, pltpu.HBM)],
        [((half, column), LOW)] * 2 + [((half, cols - column), LOW)] * 2,
        [pltpu.SemaphoreType.DMA((4,))],
    )


def hidden_first(place, after_cross, out_grad, gains, m_in, m_out, weights, block):
    rows, width = after_cross.shape
    ff = m_in.shape[1]
    count = len(weights.arrays)
    blocks = (width // block) // 2
    ff_block = ff // (2 * blocks)
    factor = math.sqrt(2.0 / math.pi)

    def kernel(place, x, og, gains, m_in_before, m_out_before, *refs):
        pieces, refs = refs[:count], refs[count:]
        act, gu, keep, send, m_in, m_out, sems = refs
        (wait,) = weights.load(place, pieces, [m_in, m_out], sems)
        residual = x[...]
        normed = (residual * scale_of(residual) * gains[2:3, :]).astype(LOW)
        split_rows(normed.T, place[2], keep.at[:, :block], send.at[:, :block])
        grad = og[...]
        wait()
        for start in range(0, ff, CHUNK):
            stop = start + CHUNK
            u = dot(normed, m_in[:, start:stop])
            ga = dot(grad, m_out[start:stop, :], NT)
            square = u * u
            t = jnp.tanh(factor * u * (1.0 + 0.044715 * square))
            half = 0.5 * (1.0 + t)
            a = (u * half).astype(LOW)
            slope = half + (0.5 * factor) * u * (1.0 - t * t) * (1.0 + 3 * 0.044715 * square)
            gu[:, start:stop] = (slope * ga).astype(LOW)
            act[:, start:stop] = a
            turned = a.T
            for first in range(start, stop, ff_block):
                n = first // ff_block
                piece = turned[first - start : first - start + ff_block]

                @pl.when(place[2] == n % 2)
                def _(n=n, piece=piece):
                    keep[n // 2, block:] = piece

                @pl.when(place[2] != n % 2)
                def _(n=n, piece=piece):
                    send[n // 2, block:] = piece

    halves = ((blocks, block + ff_block, rows), LOW)
    return run(
        "hidden_first",
        kernel,
        [(place, pltpu.SMEM)] + vmem(after_cross, out_grad, gains, m_in, m_out),
        [
            ((rows, ff), LOW),
            ((rows, ff), LOW),
            halves,
            halves,
            (m_in.shape, LOW),
            (m_out.shape, LOW),
        ],
        weights.sems(),
        flops=4 * rows * width * ff,
        weights=[weights],
        aliases={4: 4, 5: 5},
    )


def hidden_second(after_cross, out_grad, gains, act, gu, m_in, m_out):
    rows, width = after_cross.shape
    ff = m_in.shape[1]

    def kernel(x, og, gains, act, gu, m_in, m_out, out, back_out, branch, gain_out):
        residual = x[...]
        back, gain = norm_back(residual, gains[2:3, :], dot(gu[...], m_in[...], NT))
        grad = og[...].astype(F32) + back
        back_out[...] = grad
        branch[...] = grad.astype(LOW)
        gain_out[...] = gain
        out[...] = (residual + dot(act[...], m_out[...])).astype(LOW)

    return run(
        "hidden_second",
        kernel,
        vmem(after_cross, out_grad, gains, act, gu, m_in, m_out),
        [((rows, width), LOW, None), ((rows, width), F32, None), ((rows, width), LOW, None), ((1, width), F32)],
        flops=4 * rows * width * ff,
    )


def cross_backward(place, grad, branch, after_self, gains, q, kv, probs, weights):
    rows, width = after_self.shape
    mem_rows = kv.shape[0]

    count = len(weights.arrays)

    def kernel(place, gains, *refs):
        far, refs = refs[:6], refs[6:]
        pieces, refs = refs[:count], refs[count:]
        out, back_out, gain_out, branch, grad, x, q, kv, probs, matrix, att, own_sems, sems = refs
        ranges = [(width, 2 * width), (0, width)]
        branch_wait = fetch(far[:1], (branch,), own_sems)
        loaded = weights.load(place, pieces, [matrix], sems, ranges, True)
        for copy in loaded[0][0]:
            copy.start()
        waits = fetch(far[1:4], (kv, probs, q), own_sems.at[pl.ds(1, 3)])
        for copy in loaded[1][0]:
            copy.start()
        late_waits = fetch(far[4:], (x, grad), own_sems.at[pl.ds(4, 2)])
        branch_wait[0]()
        loaded[0][1]()
        att[...] = dot(branch[...], matrix[:, width : 2 * width], NT).astype(LOW)
        outs = ((out, 0), (out, width), (out, 2 * width))
        for wait in waits:
            wait()
        attend_back(q, kv, kv, (0, 0, width), att, probs, outs, None)
        loaded[1][1]()
        for wait in late_waits:
            wait()
        back, gain = norm_back(x[...], gains[1:2, :], dot(out[:, :width], matrix[:, :width], NT))
        total = grad[...] + back
        back_out[...] = total
        out[:, 3 * width :] = total.astype(LOW)
        gain_out[...] = gain

    return run(
        "cross_backward",
        kernel,
        [(place, pltpu.SMEM)]
        + vmem(gains)
        + [(array, pltpu.HBM) for array in (branch, kv, probs, q, after_self, grad)],
        [
            ((rows, 4 * width), LOW),
            ((rows, width), F32),
            ((1, width), F32),
        ],
        [
            pltpu.VMEM((rows, width), LOW),
            pltpu.VMEM((rows, width), F32),
            pltpu.VMEM((rows, width), F32),
            pltpu.VMEM((rows, width), LOW),
            pltpu.VMEM((mem_rows, 2 * width), LOW),
            pltpu.VMEM((2 * PAIRS, mem_rows, rows), LOW),
            pltpu.VMEM((width, 2 * width), LOW),
            pltpu.VMEM((rows, width), LOW),
            pltpu.SemaphoreType.DMA((6,)),
        ]
        + weights.sems(2),
        flops=8 * rows * width * width,
        weights=[weights],
    )


def memory_gradient(place, grads, weights):
    rows = grads.shape[0]
    width = grads.shape[1] // 4
    count = len(weights.arrays)

    def kernel(place, grads, *refs):
        pieces, (out, matrix, sems) = refs[:count], refs[count:]
        (wait,) = weights.load(place, pieces, [matrix], sems, [(2 * width, 4 * width)])
        wait()
        out[...] = dot(grads[:, width : 3 * width], matrix[:, 2 * width :], NT)

    return run(
        "memory_gradient",
        kernel,
        [(place, pltpu.SMEM)] + vmem(grads),
        [((rows, width), F32, None)],
        [pltpu.VMEM((width, 4 * width), LOW)] + weights.sems(),
        flops=4 * rows * width * width,
        weights=[weights],
    )[0]


def self_backward(place, grad, cross_grads, tokens, gains, cross_gain, hidden_gain, qk, v, probs, hot, weights, cut, block):
    rows, width = tokens.shape
    count = len(weights.arrays)
    heads = 2 * PAIRS
    groups = hot.shape[0]
    blocks = (width // block) // 2
    under = width // 2 * LANES // width

    def kernel(place, grad, before, tok, gains, cross_gain, hidden_gain, hot, qk_far, v_far, probs_far, *refs):
        pieces, refs = refs[:count], refs[count:]
        out_q, out_k, out_v, tok_grad, extra_keep, extra_send, qk, v, probs, matrix, att, dist, parts, own_sems, sems = refs
        ranges = [(cut + width, cut + 2 * width), (0, cut + width)]
        loaded = weights.load(place, pieces, [matrix], sems, ranges, True)
        for copy in loaded[0][0]:
            copy.start()
        waits = fetch((v_far, probs_far, qk_far), (v, probs, qk), own_sems)
        for copy in loaded[1][0]:
            copy.start()
        loaded[0][1]()
        att[...] = dot(before[:, 3 * width :], matrix[:, cut + width :], NT).astype(LOW)
        outs = ((out_q, 0), (out_k, 0), (out_v.at[:rows], 0))
        dist[...] = jnp.zeros_like(dist)
        for wait in waits:
            wait()
        attend_back(qk, qk, v, (0, width, 0), att, probs, outs, dist)
        loaded[1][1]()
        normed_grad = dot(out_q[...], matrix[:, :width], NT) + dot(out_k[...], matrix[:, width : 2 * width], NT)
        normed_grad = normed_grad + dot(out_v[:rows, :], matrix[:, cut : cut + width], NT)
        back, gain = norm_back(tok[...].astype(F32), gains[0:1, :], normed_grad)
        tok_grad[...] = grad[...] + back
        parts[...] = jnp.zeros_like(parts)
        parts[0:1, :] = gain
        parts[1:2, :] = cross_gain[...]
        parts[2:3, :] = hidden_gain[...]
        columns = parts[...].T
        table = None
        for group in range(groups):
            sums = lax.dot_general(
                hot[group].astype(F32), dist[...], NT, precision=lax.Precision.HIGHEST, preferred_element_type=F32
            )
            part = lax.dot_general(
                sums, head_lanes(group, heads), NN, precision=lax.Precision.HIGHEST, preferred_element_type=F32
            )
            table = part if table is None else table + part
        columns = columns + jnp.concatenate([table] * (2 * blocks), axis=0)
        split_rows(columns, place[2], extra_keep, extra_send)
        sending = extra_send[...].astype(F32).reshape(width // 2, LANES)
        for n in range(width // LANES):
            out_v[rows:, n * LANES : (n + 1) * LANES] = sending[n * under : (n + 1) * under].astype(LOW)

    halves = ((blocks, block, LANES), LOW)
    return run(
        "self_backward",
        kernel,
        [(place, pltpu.SMEM)]
        + vmem(grad, cross_grads, tokens, gains, cross_gain, hidden_gain, hot)
        + [(array, pltpu.HBM) for array in (qk, v, probs)],
        [((rows, width), LOW)] * 2 + [((rows + under, width), LOW), ((rows, width), F32, None), halves],
        [
            pltpu.VMEM(halves[0], LOW),
            pltpu.VMEM((rows, 2 * width), LOW),
            pltpu.VMEM((rows, width), LOW),
            pltpu.VMEM((heads, rows, rows), LOW),
            pltpu.VMEM((width, cut + 2 * width), LOW),
            pltpu.VMEM((rows, width), LOW),
            pltpu.VMEM((16, rows), F32),
            pltpu.VMEM((LANES, width), F32),
            pltpu.SemaphoreType.DMA((3,)),
        ]
        + weights.sems(2),
        flops=8 * rows * width * width,
        weights=[weights],
    )


def weight_grads(place, lefts, rights, sections, cols, extras=(), straight=()):
    sizes = grid_sizes()
    counts = (sizes["y"], sizes["x"])
    blocks = counts[0] * counts[1]
    nz = sizes["z"]
    left_count, right_count = len(lefts), len(rights)
    block = min(section[0][3] for section in (*sections, *straight))
    across_z = sum(section[3] * (section[0][3] // block) for section in straight)
    tokens = rights[0][0].shape[0]
    most = max(section[0][3] for section in (*sections, *straight))

    def kernel(place, *refs):
        refs = list(refs)
        left = [(refs.pop(0), refs.pop(0)) for _ in range(left_count)]
        right = [(refs.pop(0), refs.pop(0)) for _ in range(right_count)]
        extra = [refs.pop(0) for _ in extras]
        far_extra, gathered = refs.pop(), refs.pop()
        outs = (refs[: counts[0]], refs[counts[0] : counts[0] + counts[1]])
        out_z = refs[-1]

        def place_of(half, n):
            step, other = n // counts[1 - half], n % counts[1 - half]
            there = (place[half] + step) % counts[half]
            return there * counts[1] + other if half == 0 else other * counts[1] + there

        def products(section, order):
            (l, n, row, rows), r, column, width = section[:4]
            joined = rows % 16 == 0 and row % 16 == 0
            if joined:
                for k in range(blocks):
                    for side in range(2):
                        gathered[k * rows : (k + 1) * rows, side * tokens : (side + 1) * tokens] = left[l][side][
                            n, order(k), row : row + rows, :
                        ]
            for first in range(0, width, 768):
                size = min(768, width - first)
                own, far = (ref[:tokens, column + first : column + first + size] for ref in right[r])
                if joined:
                    total = dot(gathered[: blocks * rows, :tokens], own)
                    total = total + dot(gathered[: blocks * rows, tokens:], far)
                for k in range(blocks):
                    if joined:
                        yield first, size, k, total[k * rows : (k + 1) * rows]
                        continue
                    own_rows, far_rows = (ref[n, order(k), row : row + rows, :] for ref in left[l])
                    yield first, size, k, dot(own_rows, own) + dot(far_rows, far)

        for section in straight:
            for first, size, index, total in products(section, lambda k: k):
                for g in range(section[0][3] // block):
                    at = section[5] + g * section[3] + first
                    for z in range(nz):
                        row = g * block + z * block // nz
                        part = total[row : row + block // nz]
                        out_z[z, index, :, at : at + size] = part.astype(LOW)
        for section in sections:
            groups = section[0][3] // block
            half = section[4]
            for first, size, k, total in products(section, lambda k: place_of(half, k)):
                for g in range(groups):
                    at = section[5] + g * section[3] + first
                    part = total[g * block : (g + 1) * block].astype(LOW)
                    outs[half][k // counts[1 - half]][k % counts[1 - half], :, at : at + size] = part
        if extras:
            sent_ref = right[-1][1]
            under = sent_ref.shape[0] - tokens
            for n in range(blocks * block // under):
                far_extra[n * under : (n + 1) * under, :] = sent_ref[tokens:, n * LANES : (n + 1) * LANES].astype(F32)
        for k in range(blocks if extras else 0):
            index = place_of(0, k)
            start = pl.multiple_of(index * block, 8)
            both = extra[0][index].astype(F32) + far_extra[pl.ds(start, block), :]
            outs[0][k // counts[1]][k % counts[1], :, cols[0] - LANES :] = both.astype(LOW)

    arrays = [array for pair in lefts for array in pair] + [array for pair in rights for array in pair]
    outputs = []
    if sections:
        for half in range(2):
            shape = (counts[1 - half], block, cols[half])
            outputs += [(shape, LOW, None)] + [(shape, LOW)] * (counts[half] - 1)
    if straight:
        outputs.append(((nz, blocks, block // nz, across_z), LOW, None))
    return run(
        "weight_grads",
        kernel,
        [(place, pltpu.SMEM)] + vmem(*arrays, *extras),
        outputs,
        [pltpu.VMEM((blocks * most, 2 * tokens), LOW), pltpu.VMEM((blocks * block, LANES), F32)],
        flops=sum(4 * s[0][3] * blocks * rights[0][0].shape[0] * s[3] for s in (*sections, *straight)),
    )


def add_stage(place, firsts, seconds):
    sizes = grid_sizes()
    counts = (sizes["x"], sizes["y"])

    def kernel(place, *refs):
        refs = list(refs)
        halves = [[[refs.pop(0) for _ in parts] for parts in groups] for groups in (firsts, seconds)]
        outs = (refs[: counts[0]], refs[counts[0] :])
        for half in range(2):
            here = place[1 - half]
            for step in range(counts[half]):
                index = (here + step) % counts[half]
                at = 0
                for parts in halves[half]:
                    total = parts[0][index].astype(F32)
                    for part in parts[1:]:
                        total = total + part[index].astype(F32)
                    outs[half][step][:, at : at + total.shape[1]] = total.astype(LOW)
                    at += total.shape[1]

    outputs = []
    for groups, count in zip((firsts, seconds), counts):
        outputs += [((groups[0][0].shape[1], sum(parts[0].shape[2] for parts in groups)), LOW)] * count
    arrays = [part for groups in (firsts, seconds) for parts in groups for part in parts]
    return run("add_stage", kernel, [(place, pltpu.SMEM)] + vmem(*arrays), outputs)


def add_last(place, halves):
    count = grid_sizes()["z"]
    share = halves[0][0].shape[0] // count
    halves = [[part.reshape(count, share, part.shape[-1]) for part in parts] for parts in halves]
    cols = [parts[0].shape[-1] for parts in halves]

    def kernel(place, *refs):
        refs = list(refs)
        first = 0
        inputs = [[refs.pop(0) for _ in parts] for parts in halves]
        for parts, size in zip(inputs, cols):
            for step in range(count):
                index = (place[3] + step) % count
                total = parts[0][index].astype(F32)
                for part in parts[1:]:
                    total = total + part[index].astype(F32)
                refs[step][:, first : first + size] = total.astype(LOW)
            first += size

    return run(
        "add_last",
        kernel,
        [(place, pltpu.SMEM)] + vmem(*[part for parts in halves for part in parts]),
        [((share, sum(cols)), LOW)] * count,
    )


def mirrored(place, count):
    return place - place % count + count - 1 - place % count


def halving_order(place, count):
    order = [place]
    while len(order) < count:
        size = count // len(order)
        order += [mirrored(block, size) for block in order]
    return order


def halve(place, sides, count, first):
    have = sides[0][0].shape[0]
    half = have // 2
    cols = [parts[0].shape[2] for parts in sides]
    shape = (half, sides[0][0].shape[1], sum(cols))

    def kernel(place, *refs):
        refs = list(refs)
        inputs = [[refs.pop(0) for _ in parts] for parts in sides]
        order = halving_order(place[3], have) if first else range(have)
        for n in range(have):
            at = 0
            for parts, size in zip(inputs, cols):
                total = parts[0][order[n]].astype(F32)
                for part in parts[1:]:
                    total = total + part[order[n]].astype(F32)
                refs[n // half][n % half, :, at : at + size] = total.astype(LOW)
                at += size

    arrays = [part for parts in sides for part in parts]
    keep, send = run("halve", kernel, [(place, pltpu.SMEM)] + vmem(*arrays), [(shape, LOW, None), (shape, LOW)])
    pairs = [(i, mirrored(i, count)) for i in range(grid_sizes()["z"])]
    return keep, lax.ppermute(send, "narrow", pairs)


def by_blocks(parts):
    count = grid_sizes()["z"]
    return [part.reshape(count, part.shape[0] // count, part.shape[1]) for part in parts]


def finish_first(place, cross, early, order, early_cols, late, width, ff):
    share, cols = cross[0].shape[1:]
    cols = cols // 2
    side = width // 2
    folds = ff // width

    def kernel(place, near, far, kept, kept_far, other, order, c_query, c_key, c_value, c_output, s_output, h_in, h_out):
        total = near[0].astype(F32) + far[0].astype(F32)
        c_query[...] = total[:, :width]
        c_output[...] = total[:, width : 2 * width]
        s_output[:, :side] = total[:, 2 * width : 2 * width + side]
        c_key[...] = total[:, cols : cols + width]
        c_value[...] = total[:, cols + width : cols + 2 * width]
        s_output[:, side:] = total[:, cols + 2 * width : cols + 2 * width + side]
        x = place[1]
        first = kept[x].astype(F32) + kept_far[x].astype(F32) + other[...].astype(F32)
        for n in range(folds):
            h_out[n * share : (n + 1) * share, :] = first[:, early_cols + n * width : early_cols + (n + 1) * width]
        at = 2 * width + side
        pieces = [(first, 0, early_cols), (total, at, late), (total, cols + at, late)]
        start = 0
        for source, column, count in pieces:
            for n in range(0, count, CHUNK):
                part = source[:, column + n : column + n + CHUNK].astype(LOW)
                h_in[:, start : start + CHUNK] = dot(part, order[...], NT)
                start += CHUNK

    square = ((share, width), F32, None)
    return run(
        "finish_first",
        kernel,
        [(place, pltpu.SMEM)] + vmem(*cross, *early, order),
        [square] * 5 + [((share, ff), F32, None), ((share * folds, width), F32, None)],
    )


def finish_second(parts, width):
    share = parts[0].shape[0]
    side = width // 2
    cut = width + side + LANES

    def kernel(*refs):
        parts, (query, key, value, small) = refs[:-4], refs[-4:]
        total = parts[0][...].astype(F32)
        for part in parts[1:]:
            total = total + part[...].astype(F32)
        query[...] = total[:, :width]
        key[:, :side] = total[:, width : width + side]
        key[:, side:] = total[:, cut : cut + side]
        value[...] = total[:, cut + side :]
        small[...] = total[:, width + side : cut]

    square = ((share, width), F32, None)
    return run("finish_second", kernel, vmem(*parts), [square] * 3 + [((share, LANES), F32, None)])


def total_of(parts):
    return sum(part.astype(F32) for part in parts)


def scatter_along(parts, dim):
    count, here = grid_sizes()[dim], grid_place()[dim]
    kept = [lax.dynamic_index_in_dim(part, here, 0, keepdims=False) for part in parts]
    for step in range(1, count):
        there = (here + step) % count
        part = total_of([lax.dynamic_index_in_dim(part, there, 0, keepdims=False) for part in parts])
        kept.append(shifted(part.astype(LOW), dim, step))
    return kept


def sent(parts, dim):
    return [parts[0]] + [shifted(part, dim, step) for step, part in enumerate(parts) if step]


def segment_ids(length_row, slot_count):
    ends = jnp.cumsum(length_row).astype(jnp.int32)
    places = jnp.arange(slot_count, dtype=jnp.int32)
    return jnp.sum((places[:, None] >= ends[None, :]).astype(jnp.int32), axis=1).astype(jnp.int32)


def local(
    tokens, memory, doc_lengths, mem_lengths, pad_mask,
    self_query, self_key, self_value, self_output, self_gain, bias_table,
    cross_query, cross_key, cross_value, cross_output, cross_gain,
    hidden_in, hidden_out, hidden_gain, out_grad,
):
    sizes = grid_sizes()
    here = grid_place()
    ny, nx, nz = sizes["y"], sizes["x"], sizes["z"]
    rows, width = tokens.shape
    mem_rows = memory.shape[0]
    ff = hidden_in.shape[1]
    share = self_query.shape[0]
    ff_share = hidden_out.shape[0]
    table_rows, heads = bias_table.shape
    block = nz * share
    ff_block = nz * ff_share
    cut = 2 * width + LANES

    spots = []
    for step in range(4):
        y = (here["y"] + step // 2) % ny
        x = (here["x"] + step % 2) % nx
        for core in range(2):
            spots.append((y * nx + x) * 2 + (here["c"] + core) % 2)
    for n in range(4):
        spots += [2 * n + here["c"], 2 * n + 1 - here["c"]]
    place = jnp.stack([here["y"], here["x"], here["c"], here["z"]] + spots).astype(jnp.int32)
    pieces = in_pieces(block)
    half = block // 2

    hot = jnp.asarray(table_hot(rows, nz, share, table_rows)).astype(LOW)
    groups = hot.shape[0]
    folds = ff // width
    order = hidden_order(nz, share, folds)
    early_cols = int(ff * EARLY) // LANES * LANES if pieces else 0
    cross_squares = (cross_query, cross_output, cross_key, cross_value)
    if pieces:
        self_own = pack_first(
            (self_query, self_key, self_value, self_output), (self_gain, cross_gain, hidden_gain), bias_table, cut
        )
        rest, in_own = pack_rest(cross_squares, hidden_in, hidden_out, order, early_cols)
    else:
        table = jnp.pad(bias_table, ((0, groups * share - table_rows), (0, 0)))
        table = jnp.transpose(table.reshape(groups, share, heads), (1, 0, 2)).reshape(share, groups * heads)
        extra = jnp.concatenate(
            [
                self_gain[:, None],
                cross_gain[:, None],
                hidden_gain[:, None],
                jnp.zeros((share, TABLE_LANE - 3), LOW),
                table,
                jnp.zeros((share, LANES - TABLE_LANE - groups * heads), LOW),
            ],
            axis=1,
        )
        self_own = jnp.concatenate([self_query, self_key, extra, self_value, self_output], axis=1)
        wide_out = jnp.transpose(hidden_out.reshape(folds, share, width), (1, 0, 2)).reshape(share, ff)
        rest = jnp.concatenate([*cross_squares, reorder(hidden_in, order, NN, LOW), wide_out], axis=1)
    self_others = received(self_own, "z")
    self_z = in_order(self_own, self_others, "z", 0).reshape(block, -1)
    rest = after(rest, self_others[0])
    rest = lax.all_gather(rest, "narrow", axis=0, tiled=True)

    seg_ids = segment_ids(doc_lengths[0], rows)
    mem_ids = segment_ids(mem_lengths[0], mem_rows)
    if pieces:
        in_x, in_y = shifted(in_own, "x", 1), shifted(in_own, "y", 1)
        in_xy = shifted(in_x, "y", 1)
        in_all = in_order(
            in_order(in_own, [in_x], "x", 0), [in_order(in_y, [in_xy], "x", 0)], "y", 0
        ).reshape(4, share, early_cols)
        near, twins, corner = gather_pieces(after(self_z, in_xy))
        in_all = lax.all_gather(after(in_all, rest, *corner), "narrow", axis=0, tiled=False)
        w_self = Weights(
            pairs(near, twins) + with_twins(corner),
            near_spots(range(6), block, 0, 0, 0, cut + 2 * width)
            + half_spots(range(6, 10), block, 0, 0, 0, cut + 2 * width),
        )
        rest_near = from_neighbours(after(rest, *twins, *corner))
    else:
        w_self = Weights([gather_whole(self_z)], [(0, 0, 0, None, 0, 0, width, 0, 0, cut + 2 * width)])

    og_far = swapped(out_grad)
    qk, v, self_probs, after_self, s_keep, s_send, gains = self_forward(
        place, after(tokens, og_far), seg_ids[:, None], seg_ids[None], pad_mask[:, None], hot, w_self, cut, block
    )
    s_far = swapped(s_send)
    if pieces:
        twin = swapped(rest_near[0])
        rest_x, rest_y = (after(array, after_self, s_far, twin) for array in rest_near[1:])
        top, bottom, upper, lower = cut_halves(rest_x, rest_y, half, ff)
        corner = from_corner(top, bottom)
        in_all = jnp.transpose(after(in_all, twin), (1, 0, 2, 3)).reshape(4 * block, early_cols)
        corner = [after(array, upper, lower, in_all) for array in corner]
        rest_arrays = [rest_near[0], twin] + with_twins([rest_x, rest_y])
        w_cross = Weights(
            rest_arrays + with_twins(corner),
            near_spots(range(6), block, 0, 0, 0, ff) + half_spots(range(6, 10), block, 0, 0, 0, ff),
        )
        last = from_corner(upper, lower)
        cross_in = after(after_self, s_far, upper, lower)
    else:
        rest = gather_whole(rest)
        w_cross = Weights([rest], [(0, 0, 0, None, 0, 0, width, 0, 0, ff)])
        m_in = rest[:, ff : 2 * ff]
        m_out = jnp.transpose(rest[:, 2 * ff :].reshape(-1, block, folds, width), (0, 2, 1, 3)).reshape(ff, width)
        cross_in = after_self
    q, kv, cross_probs, after_cross, c_keep, c_send = cross_forward(
        place, cross_in, memory, gains, mem_ids[:, None], seg_ids[None], w_cross, block
    )
    c_far = swapped(c_send)
    if pieces:
        late_cols = ff - early_cols
        spots = folded_spots(near_spots(range(6), block, 0, 1, 0, 0), block, ff + late_cols, folds, width, 1)
        if late_cols:
            spots += near_spots(range(6), block, ff, 0, early_cols, late_cols)
        early = list(rest_arrays)
        for twin, array in enumerate((in_all, swapped(in_all))):
            spots += [
                (6 + twin, n * block, 0, ORDER_AT + 2 * n + twin, block, 0, block, 0, 0, early_cols) for n in range(4)
            ]
            early.append(array)
        m_in, m_out = hidden_early(after(place, after_cross), Weights(early, spots), width, ff)
        last = with_twins([after(array, after_cross) for array in last])
        spots = folded_spots(half_spots(range(4), block, 0, 1, 0, 0), block, late_cols, folds, width, 1)
        if late_cols:
            spots += half_spots(range(4), block, 0, 0, early_cols, late_cols)
        w_last = Weights(last, spots)
    else:
        w_last = Weights([], [])

    act, gu, h_keep, h_send, m_in, m_out = hidden_first(
        place, after(after_cross, c_far), out_grad, gains, m_in, m_out, w_last, block
    )
    h_far, gu_far = swapped(h_send), swapped(gu)
    layer_out, grad, branch, hidden_gain_part = hidden_second(after_cross, out_grad, gains, act, gu, m_in, m_out)
    h_keep = after(h_keep, grad)
    side = width // 2
    early_grads = int(ff * EARLY_GRAD) // LANES * LANES if pieces else 0
    late = (ff - early_grads) // 2
    ff_cols = late + (0 if pieces else folds * side)
    ff_sections = [((0, 0, 0, block), 0, early_grads + n * late, late, n, 0) for n in range(2)]
    straight = []
    if pieces:
        straight = [
            ((0, 0, 0, block), 0, 0, early_grads, 2, 0),
            ((0, 0, block, ff_block), 1, 0, width, 2, early_grads),
        ]
    else:
        ff_sections += [((0, 0, block, ff_block), 1, n * side, side, n, late) for n in range(2)]
    ff_parts = weight_grads(
        place,
        [(h_keep[None], h_far[None])],
        [(gu, gu_far), (out_grad, og_far)],
        ff_sections,
        (ff_cols, ff_cols),
        straight=straight,
    )
    if pieces:
        *ff_parts, in_early = ff_parts
        in_early = lax.psum_scatter(in_early, "narrow", scatter_dimension=0, tiled=True)
    grad = after(grad, *ff_parts)
    ff_first, ff_second = sent(ff_parts[:ny], "y"), sent(ff_parts[ny:], "x")
    cross_cols = 2 * width + side + ff_cols

    branch_far = swapped(branch)
    cross_grads, grad, cross_gain_part = cross_backward(
        place, grad, after(branch, branch_far), after_self, gains, q, kv, cross_probs, w_cross
    )
    cross_parts = weight_grads(
        place,
        [(c_keep, c_far), (s_keep, s_far)],
        [(cross_grads, swapped(after(cross_grads, *ff_first, *ff_second))), (branch, branch_far)],
        [
            ((0, 0, 0, block), 0, 0, width, 0, 0),
            ((0, 1, 0, block), 1, 0, width, 0, width),
            ((1, 1, 0, block), 0, 3 * width, side, 0, 2 * width),
            ((0, 2, 0, block), 0, width, 2 * width, 1, 0),
            ((1, 1, 0, block), 0, 3 * width + side, side, 1, 2 * width),
        ],
        (2 * width + side, 2 * width + side),
    )
    cross_first, cross_second = cross_parts[:ny], cross_parts[ny:]
    cross_first, cross_second = sent(cross_first, "y"), sent(cross_second, "x")

    grad = after(grad, *cross_parts)
    self_dq, self_dk, self_dv, tokens_grad, extra_keep = self_backward(
        place, grad, cross_grads, tokens, gains, cross_gain_part, hidden_gain_part, qk, v,
        self_probs, hot, w_self, cut, block,
    )
    self_parts = weight_grads(
        place,
        [(s_keep, s_far)],
        [(self_dq, swapped(self_dq)), (self_dk, swapped(self_dk)), (self_dv, swapped(self_dv))],
        [
            ((0, 0, 0, block), 0, 0, width, 0, 0),
            ((0, 0, 0, block), 1, 0, side, 0, width),
            ((0, 0, 0, block), 1, side, side, 1, 0),
            ((0, 0, 0, block), 2, 0, width, 1, side),
        ],
        (width + side + LANES, width + side),
        (extra_keep,),
    )
    self_first, self_second = self_parts[:ny], self_parts[ny:]
    self_first, self_second = sent(self_first, "y"), sent(self_second, "x")
    cross_first = [after(cross_first[0], *self_parts)] + cross_first[1:]
    cross_parts = add_stage(place, [cross_first, ff_first], [cross_second, ff_second])
    cross_first, cross_second = cross_parts[:nx], cross_parts[nx:]
    cross_first, cross_second = sent(cross_first, "x"), sent(cross_second, "y")
    cross_parts = halve(place, [by_blocks(cross_first), by_blocks(cross_second)], 2, True)
    memory_grad = memory_gradient(after(place, *self_parts), cross_grads, w_cross)
    self_first = [after(self_first[0], cross_parts[0], memory_grad)] + self_first[1:]
    self_parts = add_stage(place, [self_first], [self_second])
    self_first, self_second = self_parts[:nx], self_parts[nx:]
    self_first, self_second = sent(self_first, "x"), sent(self_second, "y")
    if pieces:
        in_early = after(in_early, cross_parts[0]).reshape(ny, nx, share, early_grads + folds * width)
        in_early = scatter_along([in_early], "y")
    count = 2
    while count < nz:
        count *= 2
        earlier = (*self_parts, *in_early) if pieces else self_parts
        cross_parts = halve(place, [[after(part, *earlier) for part in cross_parts]], count, False)
    self_first = [after(self_first[0], cross_parts[0])] + self_first[1:]
    self_sums = add_last(place, (self_first, self_second))
    self_parts = sent(self_sums, "z")
    if pieces:
        in_early = [after(part, cross_parts[0]) for part in in_early]
        there = total_of([lax.dynamic_index_in_dim(part, 1 - here["x"], 0, keepdims=False) for part in in_early])
        in_early.append(shifted(there.astype(LOW), "x", 1))
        *cross_grads, in_grad, out_part = finish_first(
            place, cross_parts, in_early, order, early_grads, late, width, ff
        )
        self_parts = [after(self_parts[0], in_grad)] + self_parts[1:]
    else:
        cross_total = total_of([part[0] for part in cross_parts])
        at = 2 * width + side
        halves = [cross_total[:, n : n + cross_cols] for n in (0, cross_cols)]
        in_grad = jnp.concatenate([part[:, at : at + late].astype(LOW) for part in halves], axis=1)
        in_grad = reorder(in_grad, order, NT, F32)
        out_part = jnp.concatenate([part[:, at + late :].reshape(share, folds, side) for part in halves], axis=2)
        out_part = jnp.transpose(out_part, (1, 0, 2)).reshape(ff_share, width)
        cross_grads = [
            halves[0][:, :width],
            halves[1][:, :width],
            halves[1][:, width : 2 * width],
            halves[0][:, width : 2 * width],
            jnp.concatenate([part[:, 2 * width : at] for part in halves], axis=1),
        ]
    query_grad, key_grad, value_grad, last = finish_second(self_parts, width)
    table_grad = last[:, TABLE_LANE : TABLE_LANE + groups * heads].reshape(share, groups, heads)
    table_grad = jnp.transpose(table_grad, (1, 0, 2)).reshape(groups * share, heads)[:table_rows]
    return (
        layer_out,
        tokens_grad,
        memory_grad,
        query_grad,
        key_grad,
        value_grad,
        cross_grads[4],
        last[:, 0],
        table_grad,
        *cross_grads[:4],
        last[:, 1],
        in_grad,
        out_part,
        last[:, 2],
    )


def solution(mesh):
    rows = P(("wide", "narrow"), None)
    line = P(("wide", "narrow"))
    table = P("narrow", None)
    return jax.shard_map(
        local,
        mesh=mesh,
        in_specs=(
            (rows,) * 4 + (line,) + (rows,) * 4 + (line, table) + (rows,) * 4 + (line,) + (rows,) * 2 + (line, rows)
        ),
        out_specs=(rows,) * 7 + (line, table) + (rows,) * 4 + (line,) + (rows,) * 2 + (line,),
        check_vma=False,
    )
```

```python
import math

import jax
import jax.numpy as jnp
import numpy as np
from jax import lax
from jax.experimental import pallas as pl
from jax.experimental.pallas import tpu as pltpu
from jax.sharding import PartitionSpec as P

BUCKETS = 32
REACH = 128
LOW = jnp.bfloat16
F32 = jnp.float32
NN = (((1,), (0,)), ((), ()))
NT = (((1,), (1,)), ((), ()))
TN = (((0,), (0,)), ((), ()))
PAIRS = 6
LANES = 128
TABLE_LANE = 16
CHUNK = 384
MiB = 1024 * 1024
FIRST_AT = 4
ORDER_AT = 12
EARLY = 0.5
EARLY_GRAD = 0.25


def bucket_edges(bucket_count, far_reach):
    exact_span = bucket_count // 2
    edge_list = list(range(1, exact_span + 1))
    for target in range(exact_span + 1, bucket_count):
        distance = exact_span
        while (
            exact_span
            + int(
                math.log(distance / exact_span)
                / math.log(far_reach / exact_span)
                * (bucket_count - exact_span)
            )
            < target
        ):
            distance += 1
        edge_list.append(distance)
    return edge_list


def distance_one_hot(rows):
    edges = np.array(bucket_edges(BUCKETS, REACH))
    buckets = (np.arange(rows)[:, None] >= edges[None, :]).sum(axis=1)
    return (np.arange(BUCKETS)[:, None] == buckets[None, :]).astype(np.float32)


def table_hot(rows, blocks, share, table_rows):
    one_hot = distance_one_hot(rows)
    groups = -(-table_rows // share)
    hot = np.zeros((groups, blocks * share, rows), np.float32)
    for block in range(blocks):
        for row in range(table_rows):
            hot[row // share, block * share + row % share] = one_hot[block * table_rows + row]
    return hot


def grid_sizes():
    wide = lax.axis_size("wide")
    inner = wide // 2
    across = 1
    while across * across < inner:
        across *= 2
    return {"y": inner // across, "x": across, "c": 2, "z": lax.axis_size("narrow")}


def grid_place():
    sizes = grid_sizes()
    wide = lax.axis_index("wide")
    return {
        "y": wide // (2 * sizes["x"]),
        "x": (wide // 2) % sizes["x"],
        "c": wide % 2,
        "z": lax.axis_index("narrow"),
    }


def shifted(array, dim, step):
    sizes = grid_sizes()
    count = sizes[dim]
    if dim == "z":
        return lax.ppermute(array, "narrow", [(i, (i + step) % count) for i in range(count)])
    stride = {"y": 2 * sizes["x"], "x": 2, "c": 1}[dim]
    pairs = []
    for source in range(lax.axis_size("wide")):
        place = (source // stride) % count
        pairs.append((source, source + ((place + step) % count - place) * stride))
    return lax.ppermute(array, "wide", pairs)


def after(value, *earlier):
    return lax.optimization_barrier((value, *earlier))[0]


def received(block, dim):
    count = grid_sizes()[dim]
    return [shifted(block, dim, count - step) for step in range(1, count)]


def swapped(array):
    return shifted(array, "c", 1)


def in_order(block, others, dim, axis):
    here = grid_place()[dim]
    cyclic = [block] + others
    count = len(cyclic)
    ordered = []
    for place in range(count):
        picked = cyclic[0]
        for step in range(1, count):
            picked = jnp.where((here + step) % count == place, cyclic[step], picked)
        ordered.append(picked)
    return jnp.stack(ordered, axis)


class Weights:
    def __init__(self, arrays, spots):
        self.arrays = arrays
        self.spots = spots

    def load(self, place, refs, matrices, sems, ranges=None, lazy=False):
        waits = []
        count = 0
        for low, high in ranges or [(0, None)]:
            copies = []
            for source, first, column, at, block, row, rows, matrix, there, cols in self.spots:
                start = row if at is None else pl.multiple_of(place[at] * block, block) + row
                from_column, to_column, size = column + low, there + low, (high or cols) - low
                copies.append(
                    pltpu.make_async_copy(
                        refs[source].at[pl.ds(first, rows), pl.ds(from_column, size)],
                        matrices[matrix].at[pl.ds(start, rows), pl.ds(to_column, size)],
                        sems.at[count],
                    )
                )
                count += 1
            waits.append((copies, lambda copies=copies: [copy.wait() for copy in copies]))
            if not lazy:
                for copy in copies:
                    copy.start()
        if lazy:
            return waits
        return [wait for _, wait in waits]

    def sems(self, ranges=1):
        return [pltpu.SemaphoreType.DMA((max(len(self.spots) * ranges, 1),))]


def fetch(sources, targets, sems):
    copies = [pltpu.make_async_copy(a, b, sems.at[n]) for n, (a, b) in enumerate(zip(sources, targets))]
    for copy in copies:
        copy.start()
    return [copy.wait for copy in copies]


def in_pieces(block):
    sizes = grid_sizes()
    return sizes["y"] == 2 and sizes["x"] == 2 and block % 32 == 0


def from_neighbours(block):
    return [block, shifted(block, "x", 1), shifted(block, "y", 1)]


def from_corner(upper, lower):
    return [shifted(upper, "y", 1), shifted(lower, "x", 1)]


def gather_pieces(block, *earlier, near=None):
    near = near or from_neighbours(block)
    half = block.shape[0] // 2
    twins = [swapped(near[0])]
    near_x, near_y = (after(array, twins[0], *earlier) for array in near[1:])
    corner = [shifted(near_x[:half], "y", 1), shifted(near_y[half:], "x", 1)]
    twins += [swapped(near_x), swapped(near_y)]
    return near, twins, corner


def pairs(near, twins):
    return [array for pair in zip(near, twins) for array in pair]


def gather_whole(block):
    block = in_order(block, received(block, "x"), "x", 0)
    block = in_order(block, received(block, "y"), "y", 0)
    block = in_order(block, received(block, "c"), "c", 2)
    return block.reshape(-1, block.shape[-1])


def near_spots(sources, block, column, matrix, there, cols):
    return [
        (source, 0, column, FIRST_AT + n, block, 0, block, matrix, there, cols) for n, source in enumerate(sources)
    ]


def half_spots(sources, block, column, matrix, there, cols):
    half = block // 2
    return [
        (source, 0, column, FIRST_AT + 6 + n % 2, block, (n // 2) * half, half, matrix, there, cols)
        for n, source in enumerate(sources)
    ]


def folded_spots(spots, block, column, groups, width, matrix):
    return [
        (source, first, column + g * width, at, groups * block, g * block + row, rows, matrix, 0, width)
        for source, first, _, at, _, row, rows, *_ in spots
        for g in range(groups)
    ]


def with_twins(arrays):
    return [array for own in arrays for array in (own, swapped(own))]


def run(name, kernel, inputs, outputs, scratch=(), flops=0, weights=(), aliases=()):
    inputs = list(inputs)
    for group in weights:
        inputs += [(array, pltpu.HBM) for array in group.arrays]
    size = sum(math.prod(array.shape) * array.dtype.itemsize for array, _ in inputs)
    arrays = [
        array if space == pltpu.SMEM else pltpu.with_memory_space_constraint(array, space)
        for array, space in inputs
    ]
    shapes = [
        jax.ShapeDtypeStruct(*output[:2]) if len(output) > 2 else pltpu.VMEM(*output) for output in outputs
    ]
    return pl.pallas_call(
        kernel,
        name=name,
        in_specs=[pl.BlockSpec(memory_space=space) for _, space in inputs],
        out_specs=[
            pl.BlockSpec(memory_space=pltpu.HBM if output[2:] == (pltpu.HBM,) else pltpu.VMEM) for output in outputs
        ],
        out_shape=shapes,
        scratch_shapes=list(scratch),
        input_output_aliases=dict(aliases),
        compiler_params=pltpu.CompilerParams(vmem_limit_bytes=24 * MiB),
        cost_estimate=pl.CostEstimate(flops=flops, bytes_accessed=size // 2, transcendentals=0),
    )(*arrays)


def vmem(*arrays):
    return [(array, pltpu.VMEM) for array in arrays]


def dot(left, right, dims=NN):
    return lax.dot_general(left, right, dims, preferred_element_type=F32)


def scale_of(values):
    return lax.rsqrt(jnp.mean(values * values, axis=-1, keepdims=True) + 1e-06)


def norm_back(values, gain, grad):
    scale = scale_of(values)
    weighted = grad * gain
    middle = jnp.mean(values * weighted, axis=-1, keepdims=True)
    return (
        scale * weighted - values * (scale * scale * scale * middle),
        jnp.sum(grad * values * scale, axis=0, keepdims=True),
    )


def split_rows(matrix, core, keep, send):
    count, rows, _ = keep.shape
    if rows % 16:
        matrix = matrix.astype(F32)
    pieces = [matrix[n * rows : (n + 1) * rows].astype(keep.dtype) for n in range(2 * count)]

    @pl.when(core == 0)
    def _():
        for n in range(count):
            keep[n] = pieces[2 * n]
            send[n] = pieces[2 * n + 1]

    @pl.when(core == 1)
    def _():
        for n in range(count):
            keep[n] = pieces[2 * n + 1]
            send[n] = pieces[2 * n]


def lanes_of(pair, column=0):
    return pl.ds(pl.multiple_of(column + pair * LANES, LANES), LANES)


def head_mask(rows, head):
    lanes = lax.broadcasted_iota(jnp.int32, (rows, LANES), 1)
    return (lanes >= 64) if head else (lanes < 64)


def attend(q_ref, k_ref, v_ref, columns, allowed, bias, prob_ref, out_ref):
    rows = q_ref.shape[0]
    cols = k_ref.shape[0]

    def step(pair, carry):
        q = q_ref[:, lanes_of(pair, columns[0])]
        k = k_ref[:, lanes_of(pair, columns[1])]
        v_turned = v_ref[:, lanes_of(pair, columns[2])].T
        for head in range(2):
            mine = head_mask(rows, head)
            scores = dot(k, jnp.where(mine, q, jnp.zeros_like(q)), NT)
            if bias is not None:
                row = jnp.broadcast_to(bias[pl.ds(2 * pair + head, 1), :], (cols, rows))
                scores = scores + pltpu.roll(row, 0, 1, stride=1, stride_axis=0)
            scores = jnp.where(allowed[...] > 0, scores, -1e9)
            weights = jnp.exp(scores - jnp.max(scores, axis=0, keepdims=True))
            probs = (weights * (1.0 / jnp.sum(weights, axis=0, keepdims=True))).astype(LOW)
            prob_ref[2 * pair + head] = probs
            part = dot(v_turned[head * 64 : head * 64 + 64], probs)
            first = pl.multiple_of(pair * LANES + head * 64, 64)
            out_ref[pl.ds(first, 64), :] = part.astype(LOW)
        return carry

    lax.fori_loop(0, PAIRS, step, 0)


def attend_back(q_ref, k_ref, v_ref, columns, g_ref, prob_ref, outs, dist_ref):
    rows = q_ref.shape[0]
    cols = k_ref.shape[0]

    def step(pair, carry):
        q = q_ref[:, lanes_of(pair, columns[0])]
        k = k_ref[:, lanes_of(pair, columns[1])]
        v = v_ref[:, lanes_of(pair, columns[2])]
        g = g_ref[:, lanes_of(pair)]
        k_turned = k.T
        if dist_ref is not None:
            i = lax.broadcasted_iota(jnp.int32, (cols, cols), 0)
            j = lax.broadcasted_iota(jnp.int32, (cols, cols), 1)
            flip = (i + j == cols - 1).astype(LOW)
        grads = None
        query_parts = []
        for head in range(2):
            mine = head_mask(cols, head)
            low_probs = prob_ref[2 * pair + head]
            probs = low_probs.astype(F32)
            moved = probs * dot(v, jnp.where(head_mask(rows, head), g, jnp.zeros_like(g)), NT)
            low_scores = (moved - probs * jnp.sum(moved, axis=0, keepdims=True)).astype(LOW)
            if dist_ref is not None:
                lined = pltpu.roll(dot(flip, low_scores), 1, 1, stride=1, stride_axis=0)
                dist_ref[pl.ds(2 * pair + head, 1), :] = jnp.sum(lined, axis=0, keepdims=True)
            query_parts.append(dot(k_turned[head * 64 : head * 64 + 64], low_scores))
            new = (dot(low_scores, q), dot(low_probs, g))
            grads = new if head == 0 else tuple(jnp.where(mine, b, a) for a, b in zip(grads, new))
        query_grad = jnp.concatenate(query_parts, axis=0).T
        for (ref, column), grad in zip(outs, (query_grad, *grads)):
            ref[:, lanes_of(pair, column)] = grad.astype(LOW)
        return carry

    lax.fori_loop(0, PAIRS, step, 0)


def head_lanes(group, heads):
    head = lax.broadcasted_iota(jnp.int32, (16, LANES), 0)
    lane = lax.broadcasted_iota(jnp.int32, (16, LANES), 1)
    return ((head < heads) & (lane == TABLE_LANE + group * heads + head)).astype(F32)


def self_forward(place, tokens, row_ids, col_ids, pad, hot, weights, cut, block):
    rows, width = tokens.shape
    count = len(weights.arrays)
    heads = 2 * PAIRS
    groups = hot.shape[0]
    blocks = (width // block) // 2

    def kernel(place, tok, row_ids, col_ids, pad, hot, *refs):
        pieces, refs = refs[:count], refs[count:]
        qk, v, probs, out, keep, send, gains, matrix, allowed, bias, att, sems = refs
        wait, wait_late = weights.load(place, pieces, [matrix], sems, [(0, cut), (cut, cut + 2 * width)])
        i = lax.broadcasted_iota(jnp.int32, (rows, rows), 0)
        j = lax.broadcasted_iota(jnp.int32, (rows, rows), 1)
        same = (row_ids[...] == col_ids[...]) & (i <= j) & ((pad[...] == 1) | (i == j))
        allowed[...] = same.astype(F32)
        residual = tok[...].astype(F32)
        scaled = residual * scale_of(residual)
        wait()
        extra = matrix[:, 2 * width : cut].astype(F32)
        gains[...] = extra.T[:8]
        normed = (scaled * gains[0:1, :]).astype(LOW)
        total = None
        for group in range(groups):
            table = dot(extra[: hot.shape[1]], head_lanes(group, heads), NT)
            part = dot(table.astype(LOW), hot[group], TN)
            total = part if total is None else total + part
        bias[...] = total
        split_rows(normed.T, place[2], keep.at[0], send.at[0])
        qk[...] = dot(normed, matrix[:, : 2 * width]).astype(LOW)
        wait_late()
        v[...] = dot(normed, matrix[:, cut : cut + width]).astype(LOW)
        attend(qk, qk, v, (0, width, 0), allowed, bias, probs, att)
        attended = att[...]
        split_rows(attended, place[2], keep.at[1], send.at[1])
        out[...] = residual + dot(attended, matrix[:, cut + width :], TN)

    halves = ((2, blocks, block, rows), LOW)
    return run(
        "self_forward",
        kernel,
        [(place, pltpu.SMEM)] + vmem(tokens, row_ids, col_ids, pad, hot),
        [
            ((rows, 2 * width), LOW, None),
            ((rows, width), LOW, None),
            ((heads, rows, rows), LOW, None),
            ((rows, width), F32, None),
            halves,
            halves,
            ((8, width), F32),
        ],
        [
            pltpu.VMEM((width, cut + 2 * width), LOW),
            pltpu.VMEM((rows, rows), F32),
            pltpu.VMEM((16, rows), F32),
            pltpu.VMEM((width, rows), LOW),
        ]
        + weights.sems(2),
        flops=8 * rows * width * width,
        weights=[weights],
    )


def cross_forward(place, after_self, memory, gains, row_ids, col_ids, weights, block):
    rows, width = after_self.shape
    mem_rows = memory.shape[0]
    count = len(weights.arrays)
    blocks = (width // block) // 2

    def kernel(place, x, mem, gains, row_ids, col_ids, *refs):
        pieces, refs = refs[:count], refs[count:]
        q_far, kv_far, probs_far, out, keep, send, q, kv, probs, matrix, allowed, att, out_sems, sems = refs
        wait, wait_late = weights.load(place, pieces, [matrix], sems, [(2 * width, 4 * width), (0, 2 * width)])
        allowed[...] = (row_ids[...] == col_ids[...]).astype(F32)
        residual = x[...]
        normed = (residual * scale_of(residual) * gains[1:2, :]).astype(LOW)
        split_rows(normed.T, place[2], keep.at[0], send.at[0])
        split_rows(mem[...].T, place[2], keep.at[2], send.at[2])
        wait()
        kv[...] = dot(mem[...], matrix[:, 2 * width :]).astype(LOW)
        wait_late()
        q[...] = dot(normed, matrix[:, :width]).astype(LOW)
        waits = fetch((q, kv), (q_far, kv_far), out_sems)
        attend(q, kv, kv, (0, 0, width), allowed, None, probs, att)
        waits += fetch((probs,), (probs_far,), out_sems.at[pl.ds(2, 1)])
        attended = att[...]
        split_rows(attended, place[2], keep.at[1], send.at[1])
        out[...] = residual + dot(attended, matrix[:, width : 2 * width], TN)
        for copied in waits:
            copied()

    halves = ((3, blocks, block, rows), LOW)
    return run(
        "cross_forward",
        kernel,
        [(place, pltpu.SMEM)] + vmem(after_self, memory, gains, row_ids, col_ids),
        [
            ((rows, width), LOW, pltpu.HBM),
            ((mem_rows, 2 * width), LOW, pltpu.HBM),
            ((2 * PAIRS, mem_rows, rows), LOW, pltpu.HBM),
            ((rows, width), F32),
            halves,
            halves,
        ],
        [
            pltpu.VMEM((rows, width), LOW),
            pltpu.VMEM((mem_rows, 2 * width), LOW),
            pltpu.VMEM((2 * PAIRS, mem_rows, rows), LOW),
            pltpu.VMEM((width, 4 * width), LOW),
            pltpu.VMEM((mem_rows, rows), F32),
            pltpu.VMEM((width, rows), LOW),
            pltpu.SemaphoreType.DMA((3,)),
        ]
        + weights.sems(2),
        flops=8 * rows * width * width,
        weights=[weights],
    )


def hidden_order(nz, share, groups):
    units = np.arange(CHUNK).reshape(-1, nz, groups, share)
    order = np.transpose(units, (0, 2, 1, 3)).reshape(-1)
    matrix = np.zeros((CHUNK, CHUNK), np.float32)
    matrix[order, np.arange(CHUNK)] = 1.0
    return jnp.asarray(matrix).astype(LOW)


def reorder(array, order, dims, kind):
    def kernel(array, order, out):
        for start in range(0, array.shape[1], CHUNK):
            out[:, start : start + CHUNK] = dot(array[:, start : start + CHUNK], order[...], dims).astype(kind)

    return run("reorder", kernel, vmem(array, order), [(array.shape, kind, None)])[0]


def hidden_early(place, weights, width, ff):
    count = len(weights.arrays)

    def kernel(place, *refs):
        weights.load(place, refs[:count], refs[count : count + 2], refs[count + 2])[0]()

    return run(
        "hidden_early",
        kernel,
        [(place, pltpu.SMEM)],
        [((width, ff), LOW), ((ff, width), LOW)],
        weights.sems(),
        weights=[weights],
    )


def fetching(kernel, arrays):
    count = len(arrays)

    def fetched(*refs):
        sources, outs, refs = refs[:count], refs[count : -count - 1], refs[-count - 1 :]
        for wait in fetch(sources, refs[:-1], refs[-1]):
            wait()
        kernel(*refs[:-1], *outs)

    scratch = [pltpu.VMEM(array.shape, array.dtype) for array in arrays]
    return fetched, scratch + [pltpu.SemaphoreType.DMA((count,))]


def pack_first(squares, gains, table, cut):
    share, width = squares[0].shape
    table_rows, heads = table.shape

    def kernel(query, key, value, output, *refs):
        gains, (table, out, lanes) = refs[:3], refs[3:]
        lanes[...] = jnp.zeros_like(lanes)
        rows = jnp.concatenate([gain[...].astype(F32) for gain in gains] + [jnp.zeros((5, share), F32)], axis=0)
        lanes[:, :8] = rows.T
        for group in range(-(-table_rows // share)):
            part = table[...].astype(F32)[group * share : (group + 1) * share]
            at = TABLE_LANE + group * heads
            lanes[: part.shape[0], at : at + heads] = part
        out[:, :width] = query[...]
        out[:, width : 2 * width] = key[...]
        out[:, 2 * width : cut] = lanes[...].astype(LOW)
        out[:, cut : cut + width] = value[...]
        out[:, cut + width :] = output[...]

    arrays = [*squares, *[gain.reshape(1, share) for gain in gains], table]
    fetched, scratch = fetching(kernel, arrays)
    return run(
        "pack_first",
        fetched,
        [(array, pltpu.HBM) for array in arrays],
        [((share, cut + 2 * width), LOW)],
        [pltpu.VMEM((share, LANES), F32), *scratch],
    )[0]


def pack_rest(squares, hidden_in, hidden_out, order, early_cols):
    share, width = squares[0].shape
    ff = hidden_in.shape[1]
    folds = ff // width
    late = ff - early_cols

    def kernel(*refs):
        squares, (h_in, h_out, order, rest, early) = refs[:4], refs[4:]
        for start in range(0, ff, CHUNK):
            part = dot(h_in[:, start : start + CHUNK], order[...]).astype(LOW)
            if start < early_cols:
                early[:, start : start + CHUNK] = part
            else:
                at = 4 * width + start - early_cols
                rest[:, at : at + CHUNK] = part
        for n, square in enumerate(squares):
            rest[:, n * width : (n + 1) * width] = square[...]
        rows = h_out[...].astype(F32)
        for n in range(folds):
            at = 4 * width + late + n * width
            rest[:, at : at + width] = rows[n * share : (n + 1) * share].astype(LOW)

    arrays = [*squares, hidden_in, hidden_out, order]
    fetched, scratch = fetching(kernel, arrays)
    return run(
        "pack_rest",
        fetched,
        [(array, pltpu.HBM) for array in arrays],
        [((share, 4 * width + late + ff), LOW, None), ((share, early_cols), LOW, None)],
        scratch,
    )


def cut_halves(upper, lower, half, column):
    cols = upper.shape[1]

    def kernel(upper, lower, *refs):
        outs, sems = refs[:4], refs[4]
        top, bottom = upper.at[pl.ds(0, half)], lower.at[pl.ds(half, half)]
        sources = [
            ref.at[:, pl.ds(first, size)]
            for first, size in ((0, column), (column, cols - column))
            for ref in (top, bottom)
        ]
        for wait in fetch(sources, outs, sems):
            wait()

    return run(
        "cut_halves",
        kernel,
        [(upper, pltpu.HBM), (lower, pltpu.HBM)],
        [((half, column), LOW)] * 2 + [((half, cols - column), LOW)] * 2,
        [pltpu.SemaphoreType.DMA((4,))],
    )


def hidden_first(place, after_cross, out_grad, gains, m_in, m_out, weights, block):
    rows, width = after_cross.shape
    ff = m_in.shape[1]
    count = len(weights.arrays)
    blocks = (width // block) // 2
    ff_block = ff // (2 * blocks)
    factor = math.sqrt(2.0 / math.pi)

    def kernel(place, x, og, gains, m_in_before, m_out_before, *refs):
        pieces, refs = refs[:count], refs[count:]
        act, gu, keep, send, m_in, m_out, sems = refs
        (wait,) = weights.load(place, pieces, [m_in, m_out], sems)
        residual = x[...]
        normed = (residual * scale_of(residual) * gains[2:3, :]).astype(LOW)
        split_rows(normed.T, place[2], keep.at[:, :block], send.at[:, :block])
        grad = og[...]
        wait()
        for start in range(0, ff, CHUNK):
            stop = start + CHUNK
            u = dot(normed, m_in[:, start:stop])
            ga = dot(grad, m_out[start:stop, :], NT)
            square = u * u
            t = jnp.tanh(factor * u * (1.0 + 0.044715 * square))
            half = 0.5 * (1.0 + t)
            a = (u * half).astype(LOW)
            slope = half + (0.5 * factor) * u * (1.0 - t * t) * (1.0 + 3 * 0.044715 * square)
            gu[:, start:stop] = (slope * ga).astype(LOW)
            act[:, start:stop] = a
            turned = a.T
            for first in range(start, stop, ff_block):
                n = first // ff_block
                piece = turned[first - start : first - start + ff_block]

                @pl.when(place[2] == n % 2)
                def _(n=n, piece=piece):
                    keep[n // 2, block:] = piece

                @pl.when(place[2] != n % 2)
                def _(n=n, piece=piece):
                    send[n // 2, block:] = piece

    halves = ((blocks, block + ff_block, rows), LOW)
    return run(
        "hidden_first",
        kernel,
        [(place, pltpu.SMEM)] + vmem(after_cross, out_grad, gains, m_in, m_out),
        [
            ((rows, ff), LOW),
            ((rows, ff), LOW),
            halves,
            halves,
            (m_in.shape, LOW),
            (m_out.shape, LOW),
        ],
        weights.sems(),
        flops=4 * rows * width * ff,
        weights=[weights],
        aliases={4: 4, 5: 5},
    )


def hidden_second(after_cross, out_grad, gains, act, gu, m_in, m_out):
    rows, width = after_cross.shape
    ff = m_in.shape[1]

    def kernel(x, og, gains, act, gu, m_in, m_out, out, back_out, branch, gain_out):
        residual = x[...]
        back, gain = norm_back(residual, gains[2:3, :], dot(gu[...], m_in[...], NT))
        grad = og[...].astype(F32) + back
        back_out[...] = grad
        branch[...] = grad.astype(LOW)
        gain_out[...] = gain
        out[...] = (residual + dot(act[...], m_out[...])).astype(LOW)

    return run(
        "hidden_second",
        kernel,
        vmem(after_cross, out_grad, gains, act, gu, m_in, m_out),
        [((rows, width), LOW, None), ((rows, width), F32, None), ((rows, width), LOW, None), ((1, width), F32)],
        flops=4 * rows * width * ff,
    )


def cross_backward(place, grad, branch, after_self, gains, q, kv, probs, weights):
    rows, width = after_self.shape
    mem_rows = kv.shape[0]

    count = len(weights.arrays)

    def kernel(place, gains, *refs):
        far, refs = refs[:6], refs[6:]
        pieces, refs = refs[:count], refs[count:]
        out, back_out, gain_out, branch, grad, x, q, kv, probs, matrix, att, own_sems, sems = refs
        ranges = [(width, 2 * width), (0, width)]
        branch_wait = fetch(far[:1], (branch,), own_sems)
        loaded = weights.load(place, pieces, [matrix], sems, ranges, True)
        for copy in loaded[0][0]:
            copy.start()
        waits = fetch(far[1:4], (kv, probs, q), own_sems.at[pl.ds(1, 3)])
        for copy in loaded[1][0]:
            copy.start()
        late_waits = fetch(far[4:], (x, grad), own_sems.at[pl.ds(4, 2)])
        branch_wait[0]()
        loaded[0][1]()
        att[...] = dot(branch[...], matrix[:, width : 2 * width], NT).astype(LOW)
        outs = ((out, 0), (out, width), (out, 2 * width))
        for wait in waits:
            wait()
        attend_back(q, kv, kv, (0, 0, width), att, probs, outs, None)
        loaded[1][1]()
        for wait in late_waits:
            wait()
        back, gain = norm_back(x[...], gains[1:2, :], dot(out[:, :width], matrix[:, :width], NT))
        total = grad[...] + back
        back_out[...] = total
        out[:, 3 * width :] = total.astype(LOW)
        gain_out[...] = gain

    return run(
        "cross_backward",
        kernel,
        [(place, pltpu.SMEM)]
        + vmem(gains)
        + [(array, pltpu.HBM) for array in (branch, kv, probs, q, after_self, grad)],
        [
            ((rows, 4 * width), LOW),
            ((rows, width), F32),
            ((1, width), F32),
        ],
        [
            pltpu.VMEM((rows, width), LOW),
            pltpu.VMEM((rows, width), F32),
            pltpu.VMEM((rows, width), F32),
            pltpu.VMEM((rows, width), LOW),
            pltpu.VMEM((mem_rows, 2 * width), LOW),
            pltpu.VMEM((2 * PAIRS, mem_rows, rows), LOW),
            pltpu.VMEM((width, 2 * width), LOW),
            pltpu.VMEM((rows, width), LOW),
            pltpu.SemaphoreType.DMA((6,)),
        ]
        + weights.sems(2),
        flops=8 * rows * width * width,
        weights=[weights],
    )


def memory_gradient(place, grads, weights):
    rows = grads.shape[0]
    width = grads.shape[1] // 4
    count = len(weights.arrays)

    def kernel(place, grads, *refs):
        pieces, (out, matrix, sems) = refs[:count], refs[count:]
        (wait,) = weights.load(place, pieces, [matrix], sems, [(2 * width, 4 * width)])
        wait()
        out[...] = dot(grads[:, width : 3 * width], matrix[:, 2 * width :], NT)

    return run(
        "memory_gradient",
        kernel,
        [(place, pltpu.SMEM)] + vmem(grads),
        [((rows, width), F32, None)],
        [pltpu.VMEM((width, 4 * width), LOW)] + weights.sems(),
        flops=4 * rows * width * width,
        weights=[weights],
    )[0]


def self_backward(place, grad, cross_grads, tokens, gains, cross_gain, hidden_gain, qk, v, probs, hot, weights, cut, block):
    rows, width = tokens.shape
    count = len(weights.arrays)
    heads = 2 * PAIRS
    groups = hot.shape[0]
    blocks = (width // block) // 2
    under = width // 2 * LANES // width

    def kernel(place, grad, before, tok, gains, cross_gain, hidden_gain, hot, qk_far, v_far, probs_far, *refs):
        pieces, refs = refs[:count], refs[count:]
        out_q, out_k, out_v, tok_grad, extra_keep, extra_send, qk, v, probs, matrix, att, dist, parts, own_sems, sems = refs
        ranges = [(cut + width, cut + 2 * width), (0, cut + width)]
        loaded = weights.load(place, pieces, [matrix], sems, ranges, True)
        for copy in loaded[0][0]:
            copy.start()
        waits = fetch((v_far, probs_far, qk_far), (v, probs, qk), own_sems)
        for copy in loaded[1][0]:
            copy.start()
        loaded[0][1]()
        att[...] = dot(before[:, 3 * width :], matrix[:, cut + width :], NT).astype(LOW)
        outs = ((out_q, 0), (out_k, 0), (out_v.at[:rows], 0))
        dist[...] = jnp.zeros_like(dist)
        for wait in waits:
            wait()
        attend_back(qk, qk, v, (0, width, 0), att, probs, outs, dist)
        loaded[1][1]()
        normed_grad = dot(out_q[...], matrix[:, :width], NT) + dot(out_k[...], matrix[:, width : 2 * width], NT)
        normed_grad = normed_grad + dot(out_v[:rows, :], matrix[:, cut : cut + width], NT)
        back, gain = norm_back(tok[...].astype(F32), gains[0:1, :], normed_grad)
        tok_grad[...] = grad[...] + back
        parts[...] = jnp.zeros_like(parts)
        parts[0:1, :] = gain
        parts[1:2, :] = cross_gain[...]
        parts[2:3, :] = hidden_gain[...]
        columns = parts[...].T
        table = None
        for group in range(groups):
            sums = lax.dot_general(
                hot[group].astype(F32), dist[...], NT, precision=lax.Precision.HIGHEST, preferred_element_type=F32
            )
            part = lax.dot_general(
                sums, head_lanes(group, heads), NN, precision=lax.Precision.HIGHEST, preferred_element_type=F32
            )
            table = part if table is None else table + part
        columns = columns + jnp.concatenate([table] * (2 * blocks), axis=0)
        split_rows(columns, place[2], extra_keep, extra_send)
        sending = extra_send[...].astype(F32).reshape(width // 2, LANES)
        for n in range(width // LANES):
            out_v[rows:, n * LANES : (n + 1) * LANES] = sending[n * under : (n + 1) * under].astype(LOW)

    halves = ((blocks, block, LANES), LOW)
    return run(
        "self_backward",
        kernel,
        [(place, pltpu.SMEM)]
        + vmem(grad, cross_grads, tokens, gains, cross_gain, hidden_gain, hot)
        + [(array, pltpu.HBM) for array in (qk, v, probs)],
        [((rows, width), LOW)] * 2 + [((rows + under, width), LOW), ((rows, width), F32, None), halves],
        [
            pltpu.VMEM(halves[0], LOW),
            pltpu.VMEM((rows, 2 * width), LOW),
            pltpu.VMEM((rows, width), LOW),
            pltpu.VMEM((heads, rows, rows), LOW),
            pltpu.VMEM((width, cut + 2 * width), LOW),
            pltpu.VMEM((rows, width), LOW),
            pltpu.VMEM((16, rows), F32),
            pltpu.VMEM((LANES, width), F32),
            pltpu.SemaphoreType.DMA((3,)),
        ]
        + weights.sems(2),
        flops=8 * rows * width * width,
        weights=[weights],
    )


def weight_grads(place, lefts, rights, sections, cols, extras=(), straight=()):
    sizes = grid_sizes()
    counts = (sizes["y"], sizes["x"])
    blocks = counts[0] * counts[1]
    nz = sizes["z"]
    left_count, right_count = len(lefts), len(rights)
    block = min(section[0][3] for section in (*sections, *straight))
    across_z = sum(section[3] * (section[0][3] // block) for section in straight)
    tokens = rights[0][0].shape[0]
    most = max(section[0][3] for section in (*sections, *straight))

    def kernel(place, *refs):
        refs = list(refs)
        left = [(refs.pop(0), refs.pop(0)) for _ in range(left_count)]
        right = [(refs.pop(0), refs.pop(0)) for _ in range(right_count)]
        extra = [refs.pop(0) for _ in extras]
        far_extra, gathered = refs.pop(), refs.pop()
        outs = (refs[: counts[0]], refs[counts[0] : counts[0] + counts[1]])
        out_z = refs[-1]

        def place_of(half, n):
            step, other = n // counts[1 - half], n % counts[1 - half]
            there = (place[half] + step) % counts[half]
            return there * counts[1] + other if half == 0 else other * counts[1] + there

        def products(section, order):
            (l, n, row, rows), r, column, width = section[:4]
            joined = rows % 16 == 0 and row % 16 == 0
            if joined:
                for k in range(blocks):
                    for side in range(2):
                        gathered[k * rows : (k + 1) * rows, side * tokens : (side + 1) * tokens] = left[l][side][
                            n, order(k), row : row + rows, :
                        ]
            for first in range(0, width, 768):
                size = min(768, width - first)
                own, far = (ref[:tokens, column + first : column + first + size] for ref in right[r])
                if joined:
                    total = dot(gathered[: blocks * rows, :tokens], own)
                    total = total + dot(gathered[: blocks * rows, tokens:], far)
                for k in range(blocks):
                    if joined:
                        yield first, size, k, total[k * rows : (k + 1) * rows]
                        continue
                    own_rows, far_rows = (ref[n, order(k), row : row + rows, :] for ref in left[l])
                    yield first, size, k, dot(own_rows, own) + dot(far_rows, far)

        for section in straight:
            for first, size, index, total in products(section, lambda k: k):
                for g in range(section[0][3] // block):
                    at = section[5] + g * section[3] + first
                    for z in range(nz):
                        row = g * block + z * block // nz
                        part = total[row : row + block // nz]
                        out_z[z, index, :, at : at + size] = part.astype(LOW)
        for section in sections:
            groups = section[0][3] // block
            half = section[4]
            for first, size, k, total in products(section, lambda k: place_of(half, k)):
                for g in range(groups):
                    at = section[5] + g * section[3] + first
                    part = total[g * block : (g + 1) * block].astype(LOW)
                    outs[half][k // counts[1 - half]][k % counts[1 - half], :, at : at + size] = part
        if extras:
            sent_ref = right[-1][1]
            under = sent_ref.shape[0] - tokens
            for n in range(blocks * block // under):
                far_extra[n * under : (n + 1) * under, :] = sent_ref[tokens:, n * LANES : (n + 1) * LANES].astype(F32)
        for k in range(blocks if extras else 0):
            index = place_of(0, k)
            start = pl.multiple_of(index * block, 8)
            both = extra[0][index].astype(F32) + far_extra[pl.ds(start, block), :]
            outs[0][k // counts[1]][k % counts[1], :, cols[0] - LANES :] = both.astype(LOW)

    arrays = [array for pair in lefts for array in pair] + [array for pair in rights for array in pair]
    outputs = []
    if sections:
        for half in range(2):
            shape = (counts[1 - half], block, cols[half])
            outputs += [(shape, LOW, None)] + [(shape, LOW)] * (counts[half] - 1)
    if straight:
        outputs.append(((nz, blocks, block // nz, across_z), LOW, None))
    return run(
        "weight_grads",
        kernel,
        [(place, pltpu.SMEM)] + vmem(*arrays, *extras),
        outputs,
        [pltpu.VMEM((blocks * most, 2 * tokens), LOW), pltpu.VMEM((blocks * block, LANES), F32)],
        flops=sum(4 * s[0][3] * blocks * rights[0][0].shape[0] * s[3] for s in (*sections, *straight)),
    )


def add_stage(place, firsts, seconds):
    sizes = grid_sizes()
    counts = (sizes["x"], sizes["y"])

    def kernel(place, *refs):
        refs = list(refs)
        halves = [[[refs.pop(0) for _ in parts] for parts in groups] for groups in (firsts, seconds)]
        outs = (refs[: counts[0]], refs[counts[0] :])
        for half in range(2):
            here = place[1 - half]
            for step in range(counts[half]):
                index = (here + step) % counts[half]
                at = 0
                for parts in halves[half]:
                    total = parts[0][index].astype(F32)
                    for part in parts[1:]:
                        total = total + part[index].astype(F32)
                    outs[half][step][:, at : at + total.shape[1]] = total.astype(LOW)
                    at += total.shape[1]

    outputs = []
    for groups, count in zip((firsts, seconds), counts):
        outputs += [((groups[0][0].shape[1], sum(parts[0].shape[2] for parts in groups)), LOW)] * count
    arrays = [part for groups in (firsts, seconds) for parts in groups for part in parts]
    return run("add_stage", kernel, [(place, pltpu.SMEM)] + vmem(*arrays), outputs)


def add_last(place, halves):
    count = grid_sizes()["z"]
    share = halves[0][0].shape[0] // count
    halves = [[part.reshape(count, share, part.shape[-1]) for part in parts] for parts in halves]
    cols = [parts[0].shape[-1] for parts in halves]

    def kernel(place, *refs):
        refs = list(refs)
        first = 0
        inputs = [[refs.pop(0) for _ in parts] for parts in halves]
        for parts, size in zip(inputs, cols):
            for step in range(count):
                index = (place[3] + step) % count
                total = parts[0][index].astype(F32)
                for part in parts[1:]:
                    total = total + part[index].astype(F32)
                refs[step][:, first : first + size] = total.astype(LOW)
            first += size

    return run(
        "add_last",
        kernel,
        [(place, pltpu.SMEM)] + vmem(*[part for parts in halves for part in parts]),
        [((share, sum(cols)), LOW)] * count,
    )


def mirrored(place, count):
    return place - place % count + count - 1 - place % count


def halving_order(place, count):
    order = [place]
    while len(order) < count:
        size = count // len(order)
        order += [mirrored(block, size) for block in order]
    return order


def halve(place, sides, count, first):
    have = sides[0][0].shape[0]
    half = have // 2
    cols = [parts[0].shape[2] for parts in sides]
    shape = (half, sides[0][0].shape[1], sum(cols))

    def kernel(place, *refs):
        refs = list(refs)
        inputs = [[refs.pop(0) for _ in parts] for parts in sides]
        order = halving_order(place[3], have) if first else range(have)
        for n in range(have):
            at = 0
            for parts, size in zip(inputs, cols):
                total = parts[0][order[n]].astype(F32)
                for part in parts[1:]:
                    total = total + part[order[n]].astype(F32)
                refs[n // half][n % half, :, at : at + size] = total.astype(LOW)
                at += size

    arrays = [part for parts in sides for part in parts]
    keep, send = run("halve", kernel, [(place, pltpu.SMEM)] + vmem(*arrays), [(shape, LOW, None), (shape, LOW)])
    pairs = [(i, mirrored(i, count)) for i in range(grid_sizes()["z"])]
    return keep, lax.ppermute(send, "narrow", pairs)


def by_blocks(parts):
    count = grid_sizes()["z"]
    return [part.reshape(count, part.shape[0] // count, part.shape[1]) for part in parts]


def finish_first(place, cross, early, order, early_cols, late, width, ff):
    share, cols = cross[0].shape[1:]
    cols = cols // 2
    side = width // 2
    folds = ff // width

    def kernel(place, near, far, kept, kept_far, other, order, c_query, c_key, c_value, c_output, s_output, h_in, h_out):
        total = near[0].astype(F32) + far[0].astype(F32)
        c_query[...] = total[:, :width]
        c_output[...] = total[:, width : 2 * width]
        s_output[:, :side] = total[:, 2 * width : 2 * width + side]
        c_key[...] = total[:, cols : cols + width]
        c_value[...] = total[:, cols + width : cols + 2 * width]
        s_output[:, side:] = total[:, cols + 2 * width : cols + 2 * width + side]
        x = place[1]
        first = kept[x].astype(F32) + kept_far[x].astype(F32) + other[...].astype(F32)
        for n in range(folds):
            h_out[n * share : (n + 1) * share, :] = first[:, early_cols + n * width : early_cols + (n + 1) * width]
        at = 2 * width + side
        pieces = [(first, 0, early_cols), (total, at, late), (total, cols + at, late)]
        start = 0
        for source, column, count in pieces:
            for n in range(0, count, CHUNK):
                part = source[:, column + n : column + n + CHUNK].astype(LOW)
                h_in[:, start : start + CHUNK] = dot(part, order[...], NT)
                start += CHUNK

    square = ((share, width), F32, None)
    return run(
        "finish_first",
        kernel,
        [(place, pltpu.SMEM)] + vmem(*cross, *early, order),
        [square] * 5 + [((share, ff), F32, None), ((share * folds, width), F32, None)],
    )


def finish_second(parts, width):
    share = parts[0].shape[0]
    side = width // 2
    cut = width + side + LANES

    def kernel(*refs):
        parts, (query, key, value, small) = refs[:-4], refs[-4:]
        total = parts[0][...].astype(F32)
        for part in parts[1:]:
            total = total + part[...].astype(F32)
        query[...] = total[:, :width]
        key[:, :side] = total[:, width : width + side]
        key[:, side:] = total[:, cut : cut + side]
        value[...] = total[:, cut + side :]
        small[...] = total[:, width + side : cut]

    square = ((share, width), F32, None)
    return run("finish_second", kernel, vmem(*parts), [square] * 3 + [((share, LANES), F32, None)])


def total_of(parts):
    return sum(part.astype(F32) for part in parts)


def scatter_along(parts, dim):
    count, here = grid_sizes()[dim], grid_place()[dim]
    kept = [lax.dynamic_index_in_dim(part, here, 0, keepdims=False) for part in parts]
    for step in range(1, count):
        there = (here + step) % count
        part = total_of([lax.dynamic_index_in_dim(part, there, 0, keepdims=False) for part in parts])
        kept.append(shifted(part.astype(LOW), dim, step))
    return kept


def sent(parts, dim):
    return [parts[0]] + [shifted(part, dim, step) for step, part in enumerate(parts) if step]


def segment_ids(length_row, slot_count):
    ends = jnp.cumsum(length_row).astype(jnp.int32)
    places = jnp.arange(slot_count, dtype=jnp.int32)
    return jnp.sum((places[:, None] >= ends[None, :]).astype(jnp.int32), axis=1).astype(jnp.int32)


def local(
    tokens, memory, doc_lengths, mem_lengths, pad_mask,
    self_query, self_key, self_value, self_output, self_gain, bias_table,
    cross_query, cross_key, cross_value, cross_output, cross_gain,
    hidden_in, hidden_out, hidden_gain, out_grad,
):
    sizes = grid_sizes()
    here = grid_place()
    ny, nx, nz = sizes["y"], sizes["x"], sizes["z"]
    rows, width = tokens.shape
    mem_rows = memory.shape[0]
    ff = hidden_in.shape[1]
    share = self_query.shape[0]
    ff_share = hidden_out.shape[0]
    table_rows, heads = bias_table.shape
    block = nz * share
    ff_block = nz * ff_share
    cut = 2 * width + LANES

    spots = []
    for step in range(4):
        y = (here["y"] + step // 2) % ny
        x = (here["x"] + step % 2) % nx
        for core in range(2):
            spots.append((y * nx + x) * 2 + (here["c"] + core) % 2)
    for n in range(4):
        spots += [2 * n + here["c"], 2 * n + 1 - here["c"]]
    place = jnp.stack([here["y"], here["x"], here["c"], here["z"]] + spots).astype(jnp.int32)
    pieces = in_pieces(block)
    half = block // 2

    hot = jnp.asarray(table_hot(rows, nz, share, table_rows)).astype(LOW)
    groups = hot.shape[0]
    folds = ff // width
    order = hidden_order(nz, share, folds)
    early_cols = int(ff * EARLY) // LANES * LANES if pieces else 0
    cross_squares = (cross_query, cross_output, cross_key, cross_value)
    if pieces:
        self_own = pack_first(
            (self_query, self_key, self_value, self_output), (self_gain, cross_gain, hidden_gain), bias_table, cut
        )
        rest, in_own = pack_rest(cross_squares, hidden_in, hidden_out, order, early_cols)
    else:
        table = jnp.pad(bias_table, ((0, groups * share - table_rows), (0, 0)))
        table = jnp.transpose(table.reshape(groups, share, heads), (1, 0, 2)).reshape(share, groups * heads)
        extra = jnp.concatenate(
            [
                self_gain[:, None],
                cross_gain[:, None],
                hidden_gain[:, None],
                jnp.zeros((share, TABLE_LANE - 3), LOW),
                table,
                jnp.zeros((share, LANES - TABLE_LANE - groups * heads), LOW),
            ],
            axis=1,
        )
        self_own = jnp.concatenate([self_query, self_key, extra, self_value, self_output], axis=1)
        wide_out = jnp.transpose(hidden_out.reshape(folds, share, width), (1, 0, 2)).reshape(share, ff)
        rest = jnp.concatenate([*cross_squares, reorder(hidden_in, order, NN, LOW), wide_out], axis=1)
    self_others = received(self_own, "z")
    self_z = in_order(self_own, self_others, "z", 0).reshape(block, -1)
    rest = after(rest, self_others[0])
    rest = lax.all_gather(rest, "narrow", axis=0, tiled=True)

    seg_ids = segment_ids(doc_lengths[0], rows)
    mem_ids = segment_ids(mem_lengths[0], mem_rows)
    if pieces:
        in_x, in_y = shifted(in_own, "x", 1), shifted(in_own, "y", 1)
        in_xy = shifted(in_x, "y", 1)
        in_all = in_order(
            in_order(in_own, [in_x], "x", 0), [in_order(in_y, [in_xy], "x", 0)], "y", 0
        ).reshape(4, share, early_cols)
        near, twins, corner = gather_pieces(after(self_z, in_xy))
        in_all = lax.all_gather(after(in_all, rest, *corner), "narrow", axis=0, tiled=False)
        w_self = Weights(
            pairs(near, twins) + with_twins(corner),
            near_spots(range(6), block, 0, 0, 0, cut + 2 * width)
            + half_spots(range(6, 10), block, 0, 0, 0, cut + 2 * width),
        )
        rest_near = from_neighbours(after(rest, *twins, *corner))
    else:
        w_self = Weights([gather_whole(self_z)], [(0, 0, 0, None, 0, 0, width, 0, 0, cut + 2 * width)])

    og_far = swapped(out_grad)
    qk, v, self_probs, after_self, s_keep, s_send, gains = self_forward(
        place, after(tokens, og_far), seg_ids[:, None], seg_ids[None], pad_mask[:, None], hot, w_self, cut, block
    )
    s_far = swapped(s_send)
    if pieces:
        twin = swapped(rest_near[0])
        rest_x, rest_y = (after(array, after_self, s_far, twin) for array in rest_near[1:])
        top, bottom, upper, lower = cut_halves(rest_x, rest_y, half, ff)
        corner = from_corner(top, bottom)
        in_all = jnp.transpose(after(in_all, twin), (1, 0, 2, 3)).reshape(4 * block, early_cols)
        corner = [after(array, upper, lower, in_all) for array in corner]
        rest_arrays = [rest_near[0], twin] + with_twins([rest_x, rest_y])
        w_cross = Weights(
            rest_arrays + with_twins(corner),
            near_spots(range(6), block, 0, 0, 0, ff) + half_spots(range(6, 10), block, 0, 0, 0, ff),
        )
        last = from_corner(upper, lower)
        cross_in = after(after_self, s_far, upper, lower)
    else:
        rest = gather_whole(rest)
        w_cross = Weights([rest], [(0, 0, 0, None, 0, 0, width, 0, 0, ff)])
        m_in = rest[:, ff : 2 * ff]
        m_out = jnp.transpose(rest[:, 2 * ff :].reshape(-1, block, folds, width), (0, 2, 1, 3)).reshape(ff, width)
        cross_in = after_self
    q, kv, cross_probs, after_cross, c_keep, c_send = cross_forward(
        place, cross_in, memory, gains, mem_ids[:, None], seg_ids[None], w_cross, block
    )
    c_far = swapped(c_send)
    if pieces:
        late_cols = ff - early_cols
        spots = folded_spots(near_spots(range(6), block, 0, 1, 0, 0), block, ff + late_cols, folds, width, 1)
        if late_cols:
            spots += near_spots(range(6), block, ff, 0, early_cols, late_cols)
        early = list(rest_arrays)
        for twin, array in enumerate((in_all, swapped(in_all))):
            spots += [
                (6 + twin, n * block, 0, ORDER_AT + 2 * n + twin, block, 0, block, 0, 0, early_cols) for n in range(4)
            ]
            early.append(array)
        m_in, m_out = hidden_early(after(place, after_cross), Weights(early, spots), width, ff)
        last = with_twins([after(array, after_cross) for array in last])
        spots = folded_spots(half_spots(range(4), block, 0, 1, 0, 0), block, late_cols, folds, width, 1)
        if late_cols:
            spots += half_spots(range(4), block, 0, 0, early_cols, late_cols)
        w_last = Weights(last, spots)
    else:
        w_last = Weights([], [])

    act, gu, h_keep, h_send, m_in, m_out = hidden_first(
        place, after(after_cross, c_far), out_grad, gains, m_in, m_out, w_last, block
    )
    h_far, gu_far = swapped(h_send), swapped(gu)
    layer_out, grad, branch, hidden_gain_part = hidden_second(after_cross, out_grad, gains, act, gu, m_in, m_out)
    h_keep = after(h_keep, grad)
    side = width // 2
    early_grads = int(ff * EARLY_GRAD) // LANES * LANES if pieces else 0
    late = (ff - early_grads) // 2
    ff_cols = late + (0 if pieces else folds * side)
    ff_sections = [((0, 0, 0, block), 0, early_grads + n * late, late, n, 0) for n in range(2)]
    straight = []
    if pieces:
        straight = [
            ((0, 0, 0, block), 0, 0, early_grads, 2, 0),
            ((0, 0, block, ff_block), 1, 0, width, 2, early_grads),
        ]
    else:
        ff_sections += [((0, 0, block, ff_block), 1, n * side, side, n, late) for n in range(2)]
    ff_parts = weight_grads(
        place,
        [(h_keep[None], h_far[None])],
        [(gu, gu_far), (out_grad, og_far)],
        ff_sections,
        (ff_cols, ff_cols),
        straight=straight,
    )
    if pieces:
        *ff_parts, in_early = ff_parts
        in_early = lax.psum_scatter(in_early, "narrow", scatter_dimension=0, tiled=True)
    grad = after(grad, *ff_parts)
    ff_first, ff_second = sent(ff_parts[:ny], "y"), sent(ff_parts[ny:], "x")
    cross_cols = 2 * width + side + ff_cols

    branch_far = swapped(branch)
    cross_grads, grad, cross_gain_part = cross_backward(
        place, grad, after(branch, branch_far), after_self, gains, q, kv, cross_probs, w_cross
    )
    cross_parts = weight_grads(
        place,
        [(c_keep, c_far), (s_keep, s_far)],
        [(cross_grads, swapped(after(cross_grads, *ff_first, *ff_second))), (branch, branch_far)],
        [
            ((0, 0, 0, block), 0, 0, width, 0, 0),
            ((0, 1, 0, block), 1, 0, width, 0, width),
            ((1, 1, 0, block), 0, 3 * width, side, 0, 2 * width),
            ((0, 2, 0, block), 0, width, 2 * width, 1, 0),
            ((1, 1, 0, block), 0, 3 * width + side, side, 1, 2 * width),
        ],
        (2 * width + side, 2 * width + side),
    )
    cross_first, cross_second = cross_parts[:ny], cross_parts[ny:]
    cross_first, cross_second = sent(cross_first, "y"), sent(cross_second, "x")

    grad = after(grad, *cross_parts)
    self_dq, self_dk, self_dv, tokens_grad, extra_keep = self_backward(
        place, grad, cross_grads, tokens, gains, cross_gain_part, hidden_gain_part, qk, v,
        self_probs, hot, w_self, cut, block,
    )
    self_parts = weight_grads(
        place,
        [(s_keep, s_far)],
        [(self_dq, swapped(self_dq)), (self_dk, swapped(self_dk)), (self_dv, swapped(self_dv))],
        [
            ((0, 0, 0, block), 0, 0, width, 0, 0),
            ((0, 0, 0, block), 1, 0, side, 0, width),
            ((0, 0, 0, block), 1, side, side, 1, 0),
            ((0, 0, 0, block), 2, 0, width, 1, side),
        ],
        (width + side + LANES, width + side),
        (extra_keep,),
    )
    self_first, self_second = self_parts[:ny], self_parts[ny:]
    self_first, self_second = sent(self_first, "y"), sent(self_second, "x")
    cross_first = [after(cross_first[0], *self_parts)] + cross_first[1:]
    cross_parts = add_stage(place, [cross_first, ff_first], [cross_second, ff_second])
    cross_first, cross_second = cross_parts[:nx], cross_parts[nx:]
    cross_first, cross_second = sent(cross_first, "x"), sent(cross_second, "y")
    memory_grad = memory_gradient(after(place, *cross_parts), cross_grads, w_cross)
    cross_first = [after(cross_first[0], memory_grad)] + cross_first[1:]
    cross_parts = halve(place, [by_blocks(cross_first), by_blocks(cross_second)], 2, True)
    self_first = [after(self_first[0], cross_parts[0])] + self_first[1:]
    self_parts = add_stage(place, [self_first], [self_second])
    self_first, self_second = self_parts[:nx], self_parts[nx:]
    self_first, self_second = sent(self_first, "x"), sent(self_second, "y")
    if pieces:
        in_early = after(in_early, cross_parts[0]).reshape(ny, nx, share, early_grads + folds * width)
        in_early = scatter_along([in_early], "y")
    count = 2
    while count < nz:
        count *= 2
        earlier = (*self_parts, *in_early) if pieces else self_parts
        cross_parts = halve(place, [[after(part, *earlier) for part in cross_parts]], count, False)
    self_sums = add_last(place, (self_first, self_second))
    self_parts = sent(self_sums, "z")
    if pieces:
        in_early = [after(part, cross_parts[0]) for part in in_early]
        there = total_of([lax.dynamic_index_in_dim(part, 1 - here["x"], 0, keepdims=False) for part in in_early])
        in_early.append(shifted(there.astype(LOW), "x", 1))
        *cross_grads, in_grad, out_part = finish_first(
            place, cross_parts, in_early, order, early_grads, late, width, ff
        )
        self_parts = [after(self_parts[0], in_grad)] + self_parts[1:]
    else:
        cross_total = total_of([part[0] for part in cross_parts])
        at = 2 * width + side
        halves = [cross_total[:, n : n + cross_cols] for n in (0, cross_cols)]
        in_grad = jnp.concatenate([part[:, at : at + late].astype(LOW) for part in halves], axis=1)
        in_grad = reorder(in_grad, order, NT, F32)
        out_part = jnp.concatenate([part[:, at + late :].reshape(share, folds, side) for part in halves], axis=2)
        out_part = jnp.transpose(out_part, (1, 0, 2)).reshape(ff_share, width)
        cross_grads = [
            halves[0][:, :width],
            halves[1][:, :width],
            halves[1][:, width : 2 * width],
            halves[0][:, width : 2 * width],
            jnp.concatenate([part[:, 2 * width : at] for part in halves], axis=1),
        ]
    query_grad, key_grad, value_grad, last = finish_second(self_parts, width)
    table_grad = last[:, TABLE_LANE : TABLE_LANE + groups * heads].reshape(share, groups, heads)
    table_grad = jnp.transpose(table_grad, (1, 0, 2)).reshape(groups * share, heads)[:table_rows]
    return (
        layer_out,
        tokens_grad,
        memory_grad,
        query_grad,
        key_grad,
        value_grad,
        cross_grads[4],
        last[:, 0],
        table_grad,
        *cross_grads[:4],
        last[:, 1],
        in_grad,
        out_part,
        last[:, 2],
    )


def solution(mesh):
    rows = P(("wide", "narrow"), None)
    line = P(("wide", "narrow"))
    table = P("narrow", None)
    return jax.shard_map(
        local,
        mesh=mesh,
        in_specs=(
            (rows,) * 4 + (line,) + (rows,) * 4 + (line, table) + (rows,) * 4 + (line,) + (rows,) * 2 + (line, rows)
        ),
        out_specs=(rows,) * 7 + (line, table) + (rows,) * 4 + (line,) + (rows,) * 2 + (line,),
        check_vma=False,
    )
```
